512 devices in a mesh: ctx: 64 (over y, x, core), head: 8 (over z).
Axes of the slice: x: 4, y: 8, z: 8, core: 2. Of those that a mesh axis runs over, the one named last changes fastest.
Arguments:
- inputs: bfloat16 [16384, 8192], P('ctx', 'head'), may hold values from -6 to 6
- b_proj: bfloat16 [1, 16384, 8, 128], P(None, 'ctx', 'head'), may hold values from -2 to 2
- c_proj: bfloat16 [1, 16384, 8, 128], P(None, 'ctx', 'head'), may hold values from -2 to 2
- step_sizes: float32 [1, 64, 16384], P(None, 'head', 'ctx'), may hold values from 0 to 0.18
- log_rate: float32 [1, 64], P(None, 'head'), may hold values from -7 to -2.1
- forget: float32 [1, 64, 16384], P(None, 'head', 'ctx'), may hold values from 0 to 1.6
- skip_gain: float32 [1, 64], P(None, 'head'), may hold values from 0.35 to 1.9
- norm_gain: float32 [1, 8192], P(None, 'head'), may hold values from 0.5 to 1.5
- target: bfloat16 [16384, 8192], P('ctx', 'head'), may hold values from -6 to 6
Outputs:
- grad_input: float32 [16384, 8192], P('ctx', 'head')
- grad_b: float32 [1, 16384, 8, 128], P(None, 'ctx', 'head')
- grad_c: float32 [1, 16384, 8, 128], P(None, 'ctx', 'head')
- grad_steps: float32 [1, 64, 16384], P(None, 'head', 'ctx')
The draws below stay inside these ranges and needn't reach their ends.
All inputs are finite; a program needn't handle non-finite values.
Results may differ from the reference program's by a relative error of at most 0.00035.
Values sent between devices are 32-bit elements; how exact they have to be, the bound alone decides.
A program may use at most 128 MiB of HBM per device.

```python
import jax
import jax.numpy as jnp
from jax import lax

H = 64
P_SIZE = 128
N = 128
G = 8
DEPTH_STACKED = 1
TOK_DEV = 256
DIN = 8192
SEQUENCE_LENGTH = 16384
N_CTX = 64


def head_windows(key, fast_pct):
    key = jax.random.fold_in(key, 11)
    key_fast, key_short, key_keep = jax.random.split(key, 3)
    is_fast = jax.random.randint(key_fast, (DEPTH_STACKED, H), 0, 100) < fast_pct
    short_window = jax.random.uniform(key_short, (DEPTH_STACKED, H), jnp.float32, 70.0, 85.0)
    kept_log = jax.random.uniform(key_keep, (DEPTH_STACKED, H), jnp.float32, 0.15, 0.6)
    long_window = SEQUENCE_LENGTH / kept_log
    return jnp.where(is_fast, short_window, long_window)


def draw_step_sizes(key, part):
    window = head_windows(key, 40)
    key = jax.random.fold_in(key, 1)
    rough = jax.random.uniform(key, (DEPTH_STACKED, H, SEQUENCE_LENGTH), jnp.float32, 0.5, 1.5)
    return rough * (window ** (-0.5))[:, :, None]


def draw_log_rate(key, part):
    window = head_windows(key, 40)
    return -0.5 * jnp.log(window)


def draw_forget(key, part):
    key = jax.random.fold_in(key, 3)
    anchor_offset, key_loss = jax.random.split(key)
    spike_offset = jax.random.randint(anchor_offset, (DEPTH_STACKED, 3), 0, SEQUENCE_LENGTH)
    loss = jax.random.uniform(key_loss, (DEPTH_STACKED, 3, H), jnp.float32, 0.22, 0.51)
    sequence_offsets = jnp.arange(SEQUENCE_LENGTH)
    agreeing_tally = (sequence_offsets[None, None, :] == spike_offset[:, :, None]).astype(jnp.float32)
    return jnp.einsum('lbh,lbt->lht', loss, agreeing_tally)


def draw_skip_gain(key, part):
    key = jax.random.fold_in(key, 4)
    spread = jax.random.uniform(key, (DEPTH_STACKED, H), jnp.float32, 0.8, 1.25)
    rising = 0.5 * 3.0 ** (jnp.arange(H).astype(jnp.float32) / (H - 1))
    return spread * rising[None, :]


def block_levels(stream_key, shape, cuts, smallest, largest):
    gain = 1.0
    for axis_at, parts in cuts:
        draws = jax.random.uniform(jax.random.fold_in(jax.random.fold_in(stream_key, 6), axis_at), (parts,), jnp.float32, smallest / len(cuts), largest / len(cuts))
        gain = gain * jnp.repeat(jnp.exp(draws), shape[axis_at] // parts).reshape((-1,) + (1,) * (len(shape) - 1 - axis_at))
    return gain


def normal_values(own_key, extent, scale, reach, shards=(), dtype=jnp.bfloat16):
    values = scale * jax.random.normal(own_key, extent, jnp.float32)
    if shards:
        values = values * block_levels(own_key, extent, shards, -0.22, 0.18)
    return jnp.clip(values, -reach, reach).astype(dtype)


def setup_inputs(seed: int = 0) -> dict:
    key_of = jax.random.split(jax.random.key(seed), 10)
    return {
        "inputs": normal_values(key_of[0], (SEQUENCE_LENGTH, DIN), 1.0, 6.0, ((0, 64), (1, 8))),
        "b_proj": normal_values(key_of[1], (DEPTH_STACKED, SEQUENCE_LENGTH, G, N), 0.3, 2.0, ((1, 64), (2, 8))),
        "c_proj": normal_values(key_of[2], (DEPTH_STACKED, SEQUENCE_LENGTH, G, N), 0.3, 2.0, ((1, 64), (2, 8))),
        "step_sizes": draw_step_sizes(jax.random.fold_in(key_of[9], 71), 0),
        "log_rate": draw_log_rate(jax.random.fold_in(key_of[9], 71), 0),
        "forget": draw_forget(jax.random.fold_in(key_of[9], 71), 0),
        "skip_gain": draw_skip_gain(jax.random.fold_in(key_of[9], 71), 0),
        "norm_gain": jnp.clip(1.0 + 0.1 * jax.random.normal(key_of[7], (DEPTH_STACKED, DIN), jnp.float32), 0.5, 1.5),
        "target": normal_values(key_of[8], (SEQUENCE_LENGTH, DIN), 1.0, 6.0, ((0, 64), (1, 8))),
    }


PRECISE = lax.Precision.HIGHEST
EPSILON = 1e-05

def summary(tok_heads, b_heads, step_size, logdec):
    cum_decay = jnp.cumsum(logdec, axis=1)
    end_weight = jnp.exp(cum_decay[:, -1:] - cum_decay) * step_size
    local_state = jnp.einsum('hs,shp,shn->hpn', end_weight, tok_heads, b_heads, precision=PRECISE)
    return (local_state, jnp.exp(cum_decay[:, -1]))

def mixer_out(tok_heads, b_heads, c_heads, step_size, logdec, skip_row, state_in):
    cum_decay = jnp.cumsum(logdec, axis=1)
    line_number = jnp.arange(tok_heads.shape[0])
    causal_mask = line_number[:, None] >= line_number[None, :]
    gap_decay = cum_decay[:, :, None] - cum_decay[:, None, :]
    decay_mat = jnp.where(causal_mask[None], jnp.exp(jnp.where(causal_mask[None], gap_decay, 0.0)), 0.0)
    scores = jnp.einsum('thn,shn->hts', c_heads, b_heads, precision=PRECISE)
    weights = scores * decay_mat * step_size[:, None, :]
    near_part = jnp.einsum('hts,shp->thp', weights, tok_heads, precision=PRECISE)
    far_part = jnp.einsum('thn,hpn->thp', c_heads, state_in, precision=PRECISE) * jnp.exp(cum_decay).T[:, :, None]
    return near_part + far_part + skip_row[None, :, None] * tok_heads

def layer_fwd(current, b_layer, c_layer, step_row, rate_row, forget_row, skip_row, gain_row):
    logdec = -step_row * jnp.exp(rate_row)[:, None] - forget_row
    tok_blocks = current.reshape(N_CTX, TOK_DEV, H, P_SIZE)
    b_blocks = b_layer.reshape(N_CTX, TOK_DEV, G, N)
    c_blocks = c_layer.reshape(N_CTX, TOK_DEV, G, N)
    step_blocks = step_row.reshape(H, N_CTX, TOK_DEV).transpose(1, 0, 2)
    dec_blocks = logdec.reshape(H, N_CTX, TOK_DEV).transpose(1, 0, 2)

    def span_step(state_in, pieces):
        tok_heads, b_grp, c_grp, step_size, block_dec = pieces
        b_heads = jnp.repeat(b_grp, H // G, axis=1)
        c_heads = jnp.repeat(c_grp, H // G, axis=1)
        mixed = mixer_out(tok_heads, b_heads, c_heads, step_size, block_dec, skip_row, state_in)
        local_state, span_total = summary(tok_heads, b_heads, step_size, block_dec)
        return (span_total[:, None, None] * state_in + local_state, mixed)
    start = jnp.zeros((H, P_SIZE, N), jnp.float32)
    _, mixed_all = lax.scan(jax.checkpoint(span_step), start, (tok_blocks, b_blocks, c_blocks, step_blocks, dec_blocks))
    mixed = mixed_all.reshape(N_CTX * TOK_DEV, H * P_SIZE)
    inv_scale = lax.rsqrt(lax.optimization_barrier(jnp.mean(mixed * mixed, axis=1)) + EPSILON)
    return current + gain_row * mixed * inv_scale[:, None]

def reference(inputs, b_proj, c_proj, step_sizes, log_rate, forget, skip_gain, norm_gain, target):

    def network(first, b_all, c_all, steps_all):
        current = first
        for layer_idx in range(DEPTH_STACKED):
            current = layer_fwd(current, b_all[layer_idx], c_all[layer_idx], steps_all[layer_idx], log_rate[layer_idx], forget[layer_idx], skip_gain[layer_idx], norm_gain[layer_idx])
        return current
    final, pullback = jax.vjp(network, inputs.astype(jnp.float32), b_proj.astype(jnp.float32), c_proj.astype(jnp.float32), step_sizes)
    grad_input, grad_b, grad_c, grad_steps = pullback(final - target.astype(jnp.float32))
    return (grad_input, grad_b, grad_c, grad_steps)
```

```python
import functools

import jax
import jax.numpy as jnp
from jax import lax
from jax.experimental import pallas as pl
from jax.experimental.pallas import tpu as pltpu
from jax.sharding import PartitionSpec as P

EPSILON = 1e-05
MESH = pl.DeviceIdType.MESH
F32 = jnp.float32
BF16 = jnp.bfloat16
NN = (((1,), (0,)), ((), ()))
NT = (((1,), (1,)), ((), ()))

CUM, EXPCUM, ENDW, ENDDEC, STEP = range(5)


def mm(left, right, dims=NN):
    return lax.dot_general(left, right, dims, preferred_element_type=F32)


def split2(value):
    high = value.astype(BF16)
    low = (value - high.astype(F32)).astype(BF16)
    return high, low


def split3(value):
    high = value.astype(BF16)
    rest = value - high.astype(F32)
    mid = rest.astype(BF16)
    low = (rest - mid.astype(F32)).astype(BF16)
    return high, mid, low


def mm3(left, right, dims=NN):
    (lh, ll), (rh, rl) = left, right
    return mm(lh, rh, dims) + (mm(lh, rl, dims) + mm(ll, rh, dims))


def kernel(
    chips,
    ranks,
    width,
    x_ref,
    target_ref,
    b_ref,
    c_ref,
    step_ref,
    forget_ref,
    rate_ref,
    skip_ref,
    gain_ref,
    gx_ref,
    gb_ref,
    gc_ref,
    gs_ref,
    rows_ref,
    cols_ref,
    scores_ref,
    mixed_ref,
    gm_ref,
    y_ref,
    rq_ref,
    ext_ref,
    sin_ref,
    gout_ref,
    btr_ref,
    ctr_ref,
    dst_ref,
    sum_ref,
    fl_own,
    fl_got,
    fm_out,
    fm_in,
    fp_out,
    fp_in,
    fs_out,
    fs_in,
    bl_own,
    bl_got,
    bm_out,
    bm_in,
    bp_out,
    bp_in,
    bs_out,
    bs_in,
    z_out,
    z_in,
    pair_send,
    pair_recv,
    ring_send,
    ring_recv,
    z_send,
    z_recv,
):
    tokens = x_ref.shape[0]
    heads = step_ref.shape[0]
    half = heads // 2
    chan = x_ref.shape[1] // heads
    piece = half * 128 // chips
    per_head = chips // half
    ctx = lax.axis_index("ctx")
    rank = lax.axis_index("head")
    chip, core = lax.div(ctx, 2), lax.rem(ctx, 2)
    sibling = (chip * 2 + 1 - core, rank)

    def partner(turn):
        if chips != 32:
            return lax.rem(chip + 1 + turn, chips)
        row, column = lax.div(chip, 4), lax.rem(chip, 4)
        q, r = lax.div(turn, 4), lax.rem(turn, 4)
        down = 4 + (1 - 2 * lax.rem(q, 2)) * lax.div(q + 1, 2)
        along = 2 + (1 - 2 * lax.rem(r, 2)) * lax.div(r + 1, 2)
        return lax.rem(row + down, 8) * 4 + lax.rem(column + along, 4)

    def device(at_chip):
        return (at_chip * 2 + core, rank)

    def loop(low, high, step):
        def turn(i, carry):
            step(i)
            return carry

        lax.fori_loop(low, high, turn, 0)

    barrier = pltpu.get_barrier_semaphore()

    def greet(turn):
        pl.semaphore_signal(barrier, inc=1, device_id=device(partner(turn)), device_id_type=MESH)

    def greet_rank(turn):
        other = lax.rem(rank + 1 + turn, ranks)
        pl.semaphore_signal(barrier, inc=1, device_id=(ctx, other), device_id_type=MESH)

    loop(0, chips - 1, greet)
    loop(0, ranks - 1, greet_rank)
    pl.semaphore_signal(barrier, inc=1, device_id=sibling, device_id_type=MESH)

    head_iota = lax.broadcasted_iota(jnp.int32, (heads, tokens), 0)
    rate = jnp.zeros((heads, tokens), F32)
    for h in range(heads):
        rate = jnp.where(head_iota == h, rate_ref[0, h], rate)
    rate = jnp.exp(rate)
    step = step_ref[...]
    logdec = -step * rate - forget_ref[...]
    down_iota = lax.broadcasted_iota(jnp.int32, (tokens, tokens), 0)
    along_iota = lax.broadcasted_iota(jnp.int32, (tokens, tokens), 1)
    upper = (down_iota <= along_iota).astype(F32).astype(BF16)
    parts = split3(logdec)
    cum = mm(parts[0], upper) + (mm(parts[1], upper) + mm(parts[2], upper))
    last = cum[:, tokens - 1 : tokens]
    expcum = jnp.exp(cum)
    enddec = jnp.exp(last - cum)
    rows = [cum, expcum, enddec * step, enddec, step]
    for i, row in enumerate(rows):
        rows_ref[i] = row
    table = jnp.concatenate(rows + [jnp.zeros((128 - heads * len(rows), tokens), F32)], axis=0)
    cols_ref[...] = table.T
    btr_ref[...] = b_ref[...].astype(F32).T.astype(BF16)
    ctr_ref[...] = c_ref[...].astype(F32).T.astype(BF16)

    def columns_of(h):
        rolled = pltpu.roll(cols_ref[...], lax.rem(128 - h, 128), 1)
        return [rolled[:, 8 * q : 8 * q + 1] for q in range(5)]

    def channels(h):
        return pl.ds(pl.multiple_of(h * chan, chan), chan)

    def row_of(q, h):
        return rows_ref[q, pl.ds(h, 1), :]

    def decay_of(h):
        return jnp.broadcast_to(row_of(EXPCUM, h)[:, tokens - 1 : tokens], (1, 128))

    def local_state(i, h):
        weighted = x_ref[:, channels(h)].astype(F32) * columns_of(h)[ENDW]
        high, low = split2(weighted)
        fl_own[h, 0:128, :] = mm(btr_ref[...], high) + mm(btr_ref[...], low)
        fl_own[h, 128:136, :] = jnp.broadcast_to(decay_of(h), (8, 128))

    def to_sibling(source, target, sem):
        return pltpu.make_async_remote_copy(
            src_ref=source,
            dst_ref=target,
            send_sem=pair_send.at[sem],
            recv_sem=pair_recv.at[sem],
            device_id=sibling,
            device_id_type=MESH,
        )

    mine, theirs = core * half, (1 - core) * half
    loop(0, half, lambda i: local_state(i, theirs + i))
    pl.semaphore_wait(barrier, (chips - 1) + (ranks - 1) + 1)
    swap = to_sibling(fl_own.at[pl.ds(theirs, half)], fl_got, 0)
    swap.start()
    loop(0, half, lambda i: local_state(i, mine + i))
    swap.wait_recv()

    def ring_copy(source, target, rows_sent, sem, to, slot):
        return pltpu.make_async_remote_copy(
            src_ref=source.at[to, 0:rows_sent],
            dst_ref=target.at[slot, 0:rows_sent],
            send_sem=ring_send.at[sem, to],
            recv_sem=ring_recv.at[sem, slot],
            device_id=device(to),
            device_id_type=MESH,
        )

    def ring_start(source, target, rows_sent, sem):
        def start(turn):
            ring_copy(source, target, rows_sent, sem, partner(turn), chip).start()

        loop(0, chips - 1, start)
        target[chip, 0:rows_sent, :] = source[chip, 0:rows_sent, :]

    def ring_arrived(source, target, rows_sent, sem):
        def arrived(turn):
            other = partner(turn)
            ring_copy(source, target, rows_sent, sem, other, other).wait_recv()

        loop(0, chips - 1, arrived)

    def ring_sent(source, target, rows_sent, sem):
        def sent(turn):
            other = partner(turn)
            ring_copy(source, target, rows_sent, sem, other, other).wait_send()

        loop(0, chips - 1, sent)

    def pair_of(own, got, i):
        own_rows, got_rows = own[mine + i, 0:128, :], got[i, 0:128, :]
        first = jnp.where(core == 0, own_rows, got_rows)
        second = jnp.where(core == 0, got_rows, own_rows)
        return first, second

    def decay_pair(i):
        own_decay, got_decay = fl_own[mine + i, 128:129, :], fl_got[i, 128:129, :]
        first = jnp.where(core == 0, own_decay, got_decay)
        second = jnp.where(core == 0, got_decay, own_decay)
        return first, second

    def join_forward(i):
        first, second = pair_of(fl_own, fl_got, i)
        decay0, decay1 = decay_pair(i)
        joined = decay1 * first + second
        decay = jnp.broadcast_to(decay0 * decay1, (8, 128))
        for j in range(per_head):
            fm_out[i * per_head + j, 0:piece, :] = joined[j * piece : (j + 1) * piece, :]
            fm_out[i * per_head + j, piece : piece + 8, :] = decay

    loop(0, half, join_forward)
    ring_start(fm_out, fm_in, piece + 1, 0)

    scores_ref[...] = mm(c_ref[...], b_ref[...], NT)

    def near(h):
        cols = columns_of(h)
        gap = jnp.where(down_iota >= along_iota, cols[CUM] - row_of(CUM, h), -1e30)
        weights = scores_ref[...] * jnp.exp(gap) * row_of(STEP, h)
        high, low = split2(weights)
        x_h = x_ref[:, channels(h)]
        mixed_ref[:, channels(h)] = mm(high, x_h) + mm(low, x_h)

    loop(0, heads, near)

    ring_arrived(fm_out, fm_in, piece + 1, 0)

    def scan_forward(t, state):
        fp_out[t] = state
        return fm_in[t, piece : piece + 1, :] * state + fm_in[t, 0:piece, :]

    lax.fori_loop(0, chips, scan_forward, jnp.zeros((piece, 128), F32))
    ring_start(fp_out, fp_in, piece, 1)
    ring_arrived(fp_out, fp_in, piece, 1)

    def enter(i):
        first, _ = pair_of(fl_own, fl_got, i)
        decay0, _ = decay_pair(i)
        for_first = jnp.concatenate([fp_in[i * per_head + j] for j in range(per_head)], axis=0)
        for_second = decay0 * for_first + first
        sin_ref[mine + i] = jnp.where(core == 0, for_first, for_second)
        fs_out[i] = jnp.where(core == 0, for_second, for_first)

    loop(0, half, enter)
    swap_in = to_sibling(fs_out, fs_in, 1)
    swap_in.start()

    sum_ref[...] = jnp.zeros_like(sum_ref)

    def far(h):
        cols = columns_of(h)
        high, low = split2(sin_ref[h])
        reached = mm(c_ref[...], high) + mm(c_ref[...], low)
        x_h = x_ref[:, channels(h)].astype(F32)
        mixed = mixed_ref[:, channels(h)] + cols[EXPCUM] * reached + skip_ref[0, h] * x_h
        mixed_ref[:, channels(h)] = mixed
        gained = gain_ref[:, channels(h)] * mixed
        sum_ref[0] += mixed * mixed
        sum_ref[1] += gained * (x_h - target_ref[:, channels(h)].astype(F32))
        sum_ref[2] += gained * gained

    loop(0, half, lambda i: far(mine + i))
    swap_in.wait_recv()

    def take(i):
        sin_ref[theirs + i] = fs_in[i]

    loop(0, half, take)
    loop(0, half, lambda i: far(theirs + i))

    lane = lax.broadcasted_iota(jnp.int32, (tokens, 128), 1)
    packed = jnp.zeros((tokens, 128), F32)
    for i in range(3):
        packed = jnp.where(lane == i, jnp.sum(sum_ref[i], axis=1, keepdims=True), packed)
    z_out[...] = packed.T[0:8, :]

    def z_copy(to, slot):
        return pltpu.make_async_remote_copy(
            src_ref=z_out,
            dst_ref=z_in.at[slot],
            send_sem=z_send.at[to],
            recv_sem=z_recv.at[slot],
            device_id=(ctx, to),
            device_id_type=MESH,
        )

    def z_start(turn):
        z_copy(lax.rem(rank + 1 + turn, ranks), rank).start()

    def z_arrived(turn):
        other = lax.rem(rank + 1 + turn, ranks)
        z_copy(other, other).wait_recv()

    def z_sent(turn):
        other = lax.rem(rank + 1 + turn, ranks)
        z_copy(other, other).wait_send()

    loop(0, ranks - 1, z_start)
    z_in[rank] = z_out[...]
    loop(0, ranks - 1, z_arrived)
    total = z_in[0]
    for i in range(1, ranks):
        total = total + z_in[i]
    inv_scale = lax.rsqrt(total[0:1, :] / width + EPSILON)
    inner = total[1:2, :] + inv_scale * total[2:3, :]
    coef = inner * inv_scale * inv_scale * inv_scale / width
    back = jnp.concatenate([inv_scale, coef, jnp.zeros((126, tokens), F32)], axis=0).T
    inv_col, coef_col = back[:, 0:1], back[:, 1:2]

    def norm_back(h):
        gain = gain_ref[:, channels(h)]
        mixed = mixed_ref[:, channels(h)]
        x_h = x_ref[:, channels(h)].astype(F32)
        grad_out = x_h + gain * mixed * inv_col - target_ref[:, channels(h)].astype(F32)
        grad_mixed = gain * grad_out * inv_col - mixed * coef_col
        gm_ref[:, channels(h)] = grad_mixed
        gx_ref[:, channels(h)] = grad_out + skip_ref[0, h] * grad_mixed
        high, low = split2(grad_mixed * columns_of(h)[EXPCUM])
        bl_own[h] = mm(ctr_ref[...], high) + mm(ctr_ref[...], low)

    loop(0, half, lambda i: norm_back(theirs + i))
    swap_back = to_sibling(bl_own.at[pl.ds(theirs, half)], bl_got, 2)
    swap_back.start()
    loop(0, half, lambda i: norm_back(mine + i))
    swap_back.wait_recv()

    def join_back(i):
        first, second = pair_of(bl_own, bl_got, i)
        decay0, _ = decay_pair(i)
        joined = decay0 * second + first
        for j in range(per_head):
            bm_out[i * per_head + j] = joined[j * piece : (j + 1) * piece, :]

    loop(0, half, join_back)
    ring_start(bm_out, bm_in, piece, 2)

    rq_ref[...] = jnp.zeros_like(rq_ref)
    gc_ref[...] = jnp.zeros_like(gc_ref)
    gb_ref[...] = jnp.zeros_like(gb_ref)
    dst_ref[...] = jnp.zeros_like(dst_ref)
    scores_ref[...] = mm(b_ref[...], c_ref[...], NT)

    def near_back(h):
        cols = columns_of(h)
        gap = jnp.where(along_iota >= down_iota, row_of(CUM, h) - cols[CUM], -1e30)
        decay = jnp.exp(gap)
        grad_mixed = gm_ref[:, channels(h)]
        gm_parts = split2(grad_mixed)
        x_h = x_ref[:, channels(h)]
        y_ref[:, channels(h)] = mm3(split2(scores_ref[...] * decay), gm_parts)
        grad_weights = mm(x_h, gm_parts[0], NT) + mm(x_h, gm_parts[1], NT)
        dst_ref[...] += grad_weights * decay * cols[STEP]
        own = grad_mixed * (mixed_ref[:, channels(h)] - skip_ref[0, h] * x_h.astype(F32))
        rq_ref[...] = jnp.where(lane == h, jnp.sum(own, axis=1, keepdims=True), rq_ref[...])
        gc_ref[...] += mm3(split2(grad_mixed * cols[EXPCUM]), split2(sin_ref[h]), NT)

    loop(0, heads, near_back)
    grad_scores = dst_ref[...]
    high, low = split2(grad_scores)
    gb_ref[...] += mm(high, c_ref[...]) + mm(low, c_ref[...])
    high, low = split2(grad_scores.T)
    gc_ref[...] += mm(high, b_ref[...]) + mm(low, b_ref[...])

    ring_arrived(bm_out, bm_in, piece, 2)

    def scan_back(turn, grad):
        t = chips - 1 - turn
        bp_out[t] = grad
        return fm_in[t, piece : piece + 1, :] * grad + bm_in[t]

    lax.fori_loop(0, chips, scan_back, jnp.zeros((piece, 128), F32))
    ring_start(bp_out, bp_in, piece, 3)
    ring_arrived(bp_out, bp_in, piece, 3)

    def leave(i):
        _, second = pair_of(bl_own, bl_got, i)
        _, decay1 = decay_pair(i)
        for_second = jnp.concatenate([bp_in[i * per_head + j] for j in range(per_head)], axis=0)
        for_first = decay1 * for_second + second
        gout_ref[mine + i] = jnp.where(core == 0, for_first, for_second)
        bs_out[i] = jnp.where(core == 0, for_second, for_first)

    loop(0, half, leave)
    swap_out = to_sibling(bs_out, bs_in, 3)
    swap_out.start()

    def far_back(h):
        cols = columns_of(h)
        grad_state = gout_ref[h]
        high, low = split2(grad_state)
        x_h = x_ref[:, channels(h)]
        reached = mm(b_ref[...], high) + mm(b_ref[...], low)
        value = y_ref[:, channels(h)] + cols[ENDDEC] * reached
        gx_ref[:, channels(h)] += cols[STEP] * value
        own = jnp.sum(x_h.astype(F32) * value, axis=1, keepdims=True)
        rq_ref[...] = jnp.where(lane == h + 8, own, rq_ref[...])
        gb_ref[...] += cols[ENDW] * (mm(x_h, high, NT) + mm(x_h, low, NT))
        leaving = decay_of(h) * sin_ref[h] + fl_own[h, 0:128, :]
        ext_ref[pl.ds(h, 1), :] = jnp.sum(grad_state * leaving, axis=0, keepdims=True)

    loop(0, half, lambda i: far_back(mine + i))
    swap_out.wait_recv()

    def take_back(i):
        gout_ref[theirs + i] = bs_in[i]

    loop(0, half, take_back)
    loop(0, half, lambda i: far_back(theirs + i))

    ends = rq_ref[...].T
    inner_x = ends[8 : 8 + heads, :]
    extra = jnp.sum(ext_ref[...], axis=1, keepdims=True)
    token_iota = lax.broadcasted_iota(jnp.int32, (heads, tokens), 1)
    grad_cum = ends[0:heads, :] - step * inner_x + jnp.where(token_iota == tokens - 1, extra, 0.0)
    lower = (down_iota >= along_iota).astype(F32).astype(BF16)
    parts = split3(grad_cum)
    grad_dec = mm(parts[0], lower) + (mm(parts[1], lower) + mm(parts[2], lower))
    gs_ref[...] = inner_x - rate * grad_dec

    swap.wait_send()
    swap_in.wait_send()
    swap_back.wait_send()
    swap_out.wait_send()
    ring_sent(fm_out, fm_in, piece + 1, 0)
    ring_sent(fp_out, fp_in, piece, 1)
    ring_sent(bm_out, bm_in, piece, 2)
    ring_sent(bp_out, bp_in, piece, 3)
    loop(0, ranks - 1, z_sent)


def body(chips, ranks, inputs, b_proj, c_proj, step_sizes, log_rate, forget, skip_gain, norm_gain, target):
    tokens, wide = inputs.shape
    heads = step_sizes.shape[1]
    half = heads // 2
    piece = half * 128 // chips
    vmem = pl.BlockSpec(memory_space=pltpu.VMEM)
    smem = pl.BlockSpec(memory_space=pltpu.SMEM)

    def buffer(*shape, dtype=F32):
        return pltpu.VMEM(shape, dtype)

    state = (heads, 128, 128)
    half_state = (half, 128, 128)
    grad_x, grad_b, grad_c, grad_steps = pl.pallas_call(
        functools.partial(kernel, chips, ranks, float(wide * ranks)),
        out_shape=(
            jax.ShapeDtypeStruct((tokens, wide), F32),
            jax.ShapeDtypeStruct((tokens, 128), F32),
            jax.ShapeDtypeStruct((tokens, 128), F32),
            jax.ShapeDtypeStruct((heads, tokens), F32),
        ),
        in_specs=[vmem] * 6 + [smem] * 2 + [vmem],
        out_specs=[vmem] * 4,
        scratch_shapes=[
            buffer(5, heads, tokens),
            buffer(tokens, 128),
            buffer(tokens, tokens),
            buffer(tokens, wide),
            buffer(tokens, wide),
            buffer(tokens, wide),
            buffer(tokens, 128),
            buffer(heads, 128),
            buffer(*state),
            buffer(*state),
            buffer(128, tokens, dtype=BF16),
            buffer(128, tokens, dtype=BF16),
            buffer(tokens, tokens),
            buffer(3, tokens, 128),
            buffer(heads, 136, 128),
            buffer(half, 136, 128),
            buffer(chips, piece + 8, 128),
            buffer(chips, piece + 8, 128),
            buffer(chips, piece, 128),
            buffer(chips, piece, 128),
            buffer(*half_state),
            buffer(*half_state),
            buffer(*state),
            buffer(*half_state),
            buffer(chips, piece, 128),
            buffer(chips, piece, 128),
            buffer(chips, piece, 128),
            buffer(chips, piece, 128),
            buffer(*half_state),
            buffer(*half_state),
            buffer(8, tokens),
            buffer(ranks, 8, tokens),
            pltpu.SemaphoreType.DMA((4,)),
            pltpu.SemaphoreType.DMA((4,)),
            pltpu.SemaphoreType.DMA((4, chips)),
            pltpu.SemaphoreType.DMA((4, chips)),
            pltpu.SemaphoreType.DMA((ranks,)),
            pltpu.SemaphoreType.DMA((ranks,)),
        ],
        compiler_params=pltpu.CompilerParams(
            collective_id=0, has_side_effects=True, vmem_limit_bytes=40 * 1024 * 1024
        ),
        name="layer",
    )(
        inputs,
        target,
        b_proj.reshape(tokens, 128),
        c_proj.reshape(tokens, 128),
        step_sizes[0],
        forget[0],
        log_rate,
        skip_gain,
        norm_gain,
    )
    return (
        grad_x,
        grad_b.reshape(1, tokens, 1, 128),
        grad_c.reshape(1, tokens, 1, 128),
        grad_steps[None],
    )


def solution(mesh):
    chips, ranks = mesh.shape["ctx"] // 2, mesh.shape["head"]
    in_specs = (
        P("ctx", "head"),
        P(None, "ctx", "head", None),
        P(None, "ctx", "head", None),
        P(None, "head", "ctx"),
        P(None, "head"),
        P(None, "head", "ctx"),
        P(None, "head"),
        P(None, "head"),
        P("ctx", "head"),
    )
    out_specs = (
        P("ctx", "head"),
        P(None, "ctx", "head", None),
        P(None, "ctx", "head", None),
        P(None, "head", "ctx"),
    )
    return jax.shard_map(
        functools.partial(body, chips, ranks),
        mesh=mesh,
        in_specs=in_specs,
        out_specs=out_specs,
        check_vma=False,
    )
```

```python
import functools

import jax
import jax.numpy as jnp
from jax import lax
from jax.experimental import pallas as pl
from jax.experimental.pallas import tpu as pltpu
from jax.sharding import PartitionSpec as P

EPSILON = 1e-05
MESH = pl.DeviceIdType.MESH
F32 = jnp.float32
BF16 = jnp.bfloat16
NN = (((1,), (0,)), ((), ()))
NT = (((1,), (1,)), ((), ()))

CUM, EXPCUM, ENDW, ENDDEC, STEP = range(5)


def mm(left, right, dims=NN):
    return lax.dot_general(left, right, dims, preferred_element_type=F32)


def split2(value):
    high = value.astype(BF16)
    low = (value - high.astype(F32)).astype(BF16)
    return high, low


def split3(value):
    high = value.astype(BF16)
    rest = value - high.astype(F32)
    mid = rest.astype(BF16)
    low = (rest - mid.astype(F32)).astype(BF16)
    return high, mid, low


def mm3(left, right, dims=NN):
    (lh, ll), (rh, rl) = left, right
    return mm(lh, rh, dims) + (mm(lh, rl, dims) + mm(ll, rh, dims))


def kernel(
    chips,
    ranks,
    width,
    x_hbm,
    target_hbm,
    b_hbm,
    c_hbm,
    step_hbm,
    forget_hbm,
    rate_hbm,
    skip_hbm,
    gain_hbm,
    gx_ref,
    gb_ref,
    gc_ref,
    gs_ref,
    x_ref,
    target_ref,
    b_ref,
    c_ref,
    step_ref,
    forget_ref,
    rate_ref,
    skip_ref,
    gain_ref,
    rows_ref,
    cols_ref,
    ends_ref,
    skips_ref,
    scores_ref,
    mixed_ref,
    gm_ref,
    y_ref,
    rq_ref,
    ext_ref,
    sin_ref,
    gout_ref,
    btr_ref,
    ctr_ref,
    dst_ref,
    sum_ref,
    fl_own,
    fl_got,
    fm_out,
    fm_in,
    fp_out,
    fp_in,
    fs_out,
    fs_in,
    bl_own,
    bl_got,
    bm_out,
    bm_in,
    bp_out,
    bp_in,
    bs_out,
    bs_in,
    z_out,
    z_in,
    load_sem,
    pair_send,
    pair_recv,
    ring_send,
    ring_recv,
    z_send,
    z_recv,
):
    tokens = x_ref.shape[0]
    heads = step_ref.shape[0]
    half = heads // 2
    chan = x_ref.shape[1] // heads
    parts, pair = 2, half // 2
    piece = pair * 128 // chips
    per_head = chips // pair
    ctx = lax.axis_index("ctx")
    rank = lax.axis_index("head")
    chip, core = lax.div(ctx, 2), lax.rem(ctx, 2)
    sibling = (chip * 2 + 1 - core, rank)
    lines = chips // 4
    line, place = lax.div(chip, 4), lax.rem(chip, 4)

    loads = [
        pltpu.make_async_copy(source, target, load_sem.at[i])
        for i, (source, target) in enumerate(
            (
                (step_hbm, step_ref),
                (forget_hbm, forget_ref),
                (rate_hbm, rate_ref),
                (b_hbm, b_ref),
                (x_hbm, x_ref),
                (c_hbm, c_ref),
                (skip_hbm, skip_ref),
                (gain_hbm, gain_ref),
                (target_hbm, target_ref),
            )
        )
    ]
    for load in loads:
        load.start()

    def loop(low, high, step):
        def turn(i, carry):
            step(i)
            return carry

        lax.fori_loop(low, high, turn, 0)

    def other_chips(act):
        columns = [lax.rem(place + along, 4) for along in (2, 1, 3, 0)]

        def on_line(q, count):
            down = lines // 2 + (1 - 2 * lax.rem(q, 2)) * lax.div(q + 1, 2)
            base = lax.rem(line + down, lines) * 4
            for column in columns[:count]:
                act(base + column)

        if lines > 1:
            loop(0, lines - 1, lambda q: on_line(q, 4))
        on_line(jnp.int32(lines - 1), 3)

    def other_ranks(act):
        for away in sorted(range(1, ranks), key=lambda k: -min(k, ranks - k)):
            act(lax.rem(rank + away, ranks))

    barrier = pltpu.get_barrier_semaphore()

    def greet(device):
        pl.semaphore_signal(barrier, inc=1, device_id=device, device_id_type=MESH)

    other_chips(lambda other: greet((other * 2 + core, rank)))
    other_ranks(lambda other: greet((ctx, other)))
    greet(sibling)

    down_iota = lax.broadcasted_iota(jnp.int32, (tokens, tokens), 0)
    along_iota = lax.broadcasted_iota(jnp.int32, (tokens, tokens), 1)
    diagonal = down_iota[0:heads, 0:heads] == along_iota[0:heads, 0:heads]

    def as_column(row):
        return jnp.sum(jnp.where(diagonal, row, 0.0), axis=1, keepdims=True)

    for load in loads[0:3]:
        load.wait()
    rate = jnp.exp(as_column(rate_ref[...]))
    step = step_ref[...]
    logdec = -step * rate - forget_ref[...]
    upper = (down_iota <= along_iota).astype(F32).astype(BF16)
    high, mid, low = split3(logdec)
    cum = mm(high, upper) + (mm(mid, upper) + mm(low, upper))
    last = cum[:, tokens - 1 : tokens]
    expcum = jnp.exp(cum)
    enddec = jnp.exp(last - cum)
    table = [cum, expcum, enddec * step, enddec, step]
    rows_ref[0] = cum
    rows_ref[1] = step
    ends_ref[...] = jnp.broadcast_to(jnp.exp(last), (heads, 128))
    table = jnp.concatenate(table + [jnp.zeros((128 - heads * len(table), tokens), F32)], axis=0)
    cols_ref[...] = table.T
    loads[3].wait()
    btr_ref[...] = b_ref[...].astype(F32).T.astype(BF16)
    loads[4].wait()

    def columns_of(h):
        rolled = pltpu.roll(cols_ref[...], lax.rem(128 - h, 128), 1)
        return [rolled[:, 8 * q : 8 * q + 1] for q in range(5)]

    def channels(h):
        return pl.ds(pl.multiple_of(h * chan, chan), chan)

    def cum_row(h):
        return rows_ref[0, pl.ds(h, 1), :]

    def step_row(h):
        return rows_ref[1, pl.ds(h, 1), :]

    def decay_of(h):
        return ends_ref[pl.ds(h, 1), :]

    def skip_of(h):
        return skips_ref[pl.ds(h, 1), :]

    def local_state(h):
        weighted = x_ref[:, channels(h)].astype(F32) * columns_of(h)[ENDW]
        high, low = split2(weighted)
        fl_own[h, 0:128, :] = mm(btr_ref[...], high) + mm(btr_ref[...], low)
        fl_own[h, 128:136, :] = jnp.broadcast_to(decay_of(h), (8, 128))

    def to_sibling(source, target, sem):
        return pltpu.make_async_remote_copy(
            src_ref=source,
            dst_ref=target,
            send_sem=pair_send.at[sem],
            recv_sem=pair_recv.at[sem],
            device_id=sibling,
            device_id_type=MESH,
        )

    mine, theirs = core * half, (1 - core) * half

    def swap_of(own, got, part, sem):
        return to_sibling(own.at[pl.ds(theirs + part * pair, pair)], got.at[pl.ds(part * pair, pair)], sem)

    def heads_of(base, part, act):
        loop(0, pair, lambda i: act(base + part * pair + i))

    def ring_start(source, target, part, rows_sent, sem):
        def start(other):
            pltpu.make_async_remote_copy(
                src_ref=source.at[part, other, 0:rows_sent],
                dst_ref=target.at[part, chip, 0:rows_sent],
                send_sem=ring_send.at[sem],
                recv_sem=ring_recv.at[sem],
                device_id=(other * 2 + core, rank),
                device_id_type=MESH,
            ).start()

        other_chips(start)
        target[part, chip, 0:rows_sent, :] = source[part, chip, 0:rows_sent, :]

    def ring_all(source, target, part, rows_sent, sem):
        return pltpu.make_async_remote_copy(
            src_ref=source.at[part, 0 : chips - 1, 0:rows_sent],
            dst_ref=target.at[part, 0 : chips - 1, 0:rows_sent],
            send_sem=ring_send.at[sem],
            recv_sem=ring_recv.at[sem],
            device_id=sibling,
            device_id_type=MESH,
        )

    def pair_of(own, got, i):
        own_rows, got_rows = own[mine + i, 0:128, :], got[i, 0:128, :]
        first = jnp.where(core == 0, own_rows, got_rows)
        second = jnp.where(core == 0, got_rows, own_rows)
        return first, second

    def decay_pair(i):
        own_decay, got_decay = fl_own[mine + i, 128:129, :], fl_got[i, 128:129, :]
        first = jnp.where(core == 0, own_decay, got_decay)
        second = jnp.where(core == 0, got_decay, own_decay)
        return first, second

    def owners_of(part, i):
        return part, pl.ds(i * per_head, per_head), pl.ds(0, piece)

    def join_forward(part):
        for i in range(pair):
            first, second = pair_of(fl_own, fl_got, part * pair + i)
            decay0, decay1 = decay_pair(part * pair + i)
            joined = decay1 * first + second
            fm_out[owners_of(part, i)] = joined.reshape(per_head, piece, 128)
            fm_out[part, pl.ds(i * per_head, per_head), pl.ds(piece, 8)] = jnp.broadcast_to(
                (decay0 * decay1)[None], (per_head, 8, 128)
            )

    for part in range(parts):
        heads_of(theirs, part, local_state)
        if part == 0:
            pl.semaphore_wait(barrier, (chips - 1) + (ranks - 1) + 1)
        swap_of(fl_own, fl_got, part, part).start()
    for part in range(parts):
        heads_of(mine, part, local_state)
        swap_of(fl_own, fl_got, part, part).wait_recv()
        join_forward(part)
        ring_start(fm_out, fm_in, part, piece + 1, part)

    for load in loads[5:]:
        load.wait()
    skips_ref[...] = jnp.broadcast_to(as_column(skip_ref[...]), (heads, 128))
    ctr_ref[...] = c_ref[...].astype(F32).T.astype(BF16)
    scores_ref[...] = mm(c_ref[...], b_ref[...], NT)

    def near(h):
        cols = columns_of(h)
        gap = jnp.where(down_iota >= along_iota, cols[CUM] - cum_row(h), -1e30)
        weights = scores_ref[...] * jnp.exp(gap) * step_row(h)
        high, low = split2(weights)
        x_h = x_ref[:, channels(h)]
        mixed_ref[:, channels(h)] = mm(high, x_h) + mm(low, x_h)

    loop(0, heads, near)
    sum_ref[...] = jnp.zeros_like(sum_ref)

    for part in range(parts):
        ring_all(fm_out, fm_in, part, piece + 1, part).wait_recv()
        state = jnp.zeros((piece, 128), F32)
        for t in range(chips):
            fp_out[part, t] = state
            state = fm_in[part, t, piece : piece + 1, :] * state + fm_in[part, t, 0:piece, :]
        ring_start(fp_out, fp_in, part, piece, 2 + part)

    def enter(part):
        for i in range(pair):
            at = part * pair + i
            first, _ = pair_of(fl_own, fl_got, at)
            decay0, _ = decay_pair(at)
            for_first = fp_in[owners_of(part, i)].reshape(128, 128)
            for_second = decay0 * for_first + first
            sin_ref[mine + at] = jnp.where(core == 0, for_first, for_second)
            fs_out[at] = jnp.where(core == 0, for_second, for_first)

    def both(own, got, part, sem):
        here = pl.ds(part * pair, pair)
        return to_sibling(own.at[here], got.at[here], sem)

    def far(h):
        cols = columns_of(h)
        high, low = split2(sin_ref[h])
        reached = mm(c_ref[...], high) + mm(c_ref[...], low)
        x_h = x_ref[:, channels(h)].astype(F32)
        mixed = mixed_ref[:, channels(h)] + cols[EXPCUM] * reached + skip_of(h) * x_h
        mixed_ref[:, channels(h)] = mixed
        gained = gain_ref[:, channels(h)] * mixed
        sum_ref[0] += mixed * mixed
        sum_ref[1] += gained * (x_h - target_ref[:, channels(h)].astype(F32))
        sum_ref[2] += gained * gained

    for part in range(parts):
        ring_all(fp_out, fp_in, part, piece, 2 + part).wait_recv()
        enter(part)
        both(fs_out, fs_in, part, 2 + part).start()
        heads_of(mine, part, far)
    for part in range(parts):
        both(fs_out, fs_in, part, 2 + part).wait_recv()
        for i in range(pair):
            sin_ref[theirs + part * pair + i] = fs_in[part * pair + i]
        heads_of(theirs, part, far)

    lane = lax.broadcasted_iota(jnp.int32, (tokens, 128), 1)
    packed = jnp.zeros((tokens, 128), F32)
    for i in range(3):
        packed = jnp.where(lane == i, jnp.sum(sum_ref[i], axis=1, keepdims=True), packed)
    z_out[...] = packed.T[0:8, :]

    def z_copy(to, slot):
        return pltpu.make_async_remote_copy(
            src_ref=z_out,
            dst_ref=z_in.at[slot],
            send_sem=z_send.at[to],
            recv_sem=z_recv.at[slot],
            device_id=(ctx, to),
            device_id_type=MESH,
        )

    other_ranks(lambda other: z_copy(other, rank).start())
    z_in[rank] = z_out[...]
    other_ranks(lambda other: z_copy(other, other).wait_recv())
    total = z_in[0]
    for i in range(1, ranks):
        total = total + z_in[i]
    inv_scale = lax.rsqrt(total[0:1, :] / width + EPSILON)
    inner = total[1:2, :] + inv_scale * total[2:3, :]
    coef = inner * inv_scale * inv_scale * inv_scale / width
    back = jnp.concatenate([inv_scale, coef, jnp.zeros((126, tokens), F32)], axis=0).T
    inv_col, coef_col = back[:, 0:1], back[:, 1:2]

    def norm_back(h):
        gain = gain_ref[:, channels(h)]
        mixed = mixed_ref[:, channels(h)]
        x_h = x_ref[:, channels(h)].astype(F32)
        grad_out = x_h + gain * mixed * inv_col - target_ref[:, channels(h)].astype(F32)
        grad_mixed = gain * grad_out * inv_col - mixed * coef_col
        gm_ref[:, channels(h)] = grad_mixed
        gx_ref[:, channels(h)] = grad_out + skip_of(h) * grad_mixed
        high, low = split2(grad_mixed * columns_of(h)[EXPCUM])
        bl_own[h] = mm(ctr_ref[...], high) + mm(ctr_ref[...], low)

    def join_back(part):
        for i in range(pair):
            first, second = pair_of(bl_own, bl_got, part * pair + i)
            decay0, _ = decay_pair(part * pair + i)
            bm_out[owners_of(part, i)] = (decay0 * second + first).reshape(per_head, piece, 128)

    for part in range(parts):
        heads_of(theirs, part, norm_back)
        swap_of(bl_own, bl_got, part, 4 + part).start()
    for part in range(parts):
        heads_of(mine, part, norm_back)
        swap_of(bl_own, bl_got, part, 4 + part).wait_recv()
        join_back(part)
        ring_start(bm_out, bm_in, part, piece, 4 + part)

    rq_ref[...] = jnp.zeros_like(rq_ref)
    gc_ref[...] = jnp.zeros_like(gc_ref)
    gb_ref[...] = jnp.zeros_like(gb_ref)
    dst_ref[...] = jnp.zeros_like(dst_ref)
    scores_ref[...] = mm(b_ref[...], c_ref[...], NT)

    def near_back(h):
        cols = columns_of(h)
        gap = jnp.where(along_iota >= down_iota, cum_row(h) - cols[CUM], -1e30)
        decay = jnp.exp(gap)
        grad_mixed = gm_ref[:, channels(h)]
        gm_parts = split2(grad_mixed)
        x_h = x_ref[:, channels(h)]
        y_ref[:, channels(h)] = mm3(split2(scores_ref[...] * decay), gm_parts)
        grad_weights = mm(x_h, gm_parts[0], NT) + mm(x_h, gm_parts[1], NT)
        dst_ref[...] += grad_weights * decay * cols[STEP]
        own = grad_mixed * (mixed_ref[:, channels(h)] - skip_of(h) * x_h.astype(F32))
        rq_ref[...] = jnp.where(lane == h, jnp.sum(own, axis=1, keepdims=True), rq_ref[...])
        gc_ref[...] += mm3(split2(grad_mixed * cols[EXPCUM]), split2(sin_ref[h]), NT)

    loop(0, heads, near_back)
    grad_scores = dst_ref[...]
    high, low = split2(grad_scores)
    gb_ref[...] += mm(high, c_ref[...]) + mm(low, c_ref[...])
    high, low = split2(grad_scores.T)
    gc_ref[...] += mm(high, b_ref[...]) + mm(low, b_ref[...])

    for part in range(parts):
        ring_all(bm_out, bm_in, part, piece, 4 + part).wait_recv()
        grad = jnp.zeros((piece, 128), F32)
        for t in reversed(range(chips)):
            bp_out[part, t] = grad
            grad = fm_in[part, t, piece : piece + 1, :] * grad + bm_in[part, t]
        ring_start(bp_out, bp_in, part, piece, 6 + part)

    def leave(part):
        for i in range(pair):
            at = part * pair + i
            _, second = pair_of(bl_own, bl_got, at)
            _, decay1 = decay_pair(at)
            for_second = bp_in[owners_of(part, i)].reshape(128, 128)
            for_first = decay1 * for_second + second
            gout_ref[mine + at] = jnp.where(core == 0, for_first, for_second)
            bs_out[at] = jnp.where(core == 0, for_second, for_first)

    def far_back(h):
        cols = columns_of(h)
        grad_state = gout_ref[h]
        high, low = split2(grad_state)
        x_h = x_ref[:, channels(h)]
        reached = mm(b_ref[...], high) + mm(b_ref[...], low)
        value = y_ref[:, channels(h)] + cols[ENDDEC] * reached
        gx_ref[:, channels(h)] += cols[STEP] * value
        own = jnp.sum(x_h.astype(F32) * value, axis=1, keepdims=True)
        rq_ref[...] = jnp.where(lane == h + 8, own, rq_ref[...])
        gb_ref[...] += cols[ENDW] * (mm(x_h, high, NT) + mm(x_h, low, NT))
        leaving = decay_of(h) * sin_ref[h] + fl_own[h, 0:128, :]
        ext_ref[pl.ds(h, 1), :] = jnp.sum(grad_state * leaving, axis=0, keepdims=True)

    for part in range(parts):
        ring_all(bp_out, bp_in, part, piece, 6 + part).wait_recv()
        leave(part)
        both(bs_out, bs_in, part, 6 + part).start()
        heads_of(mine, part, far_back)
    for part in range(parts):
        both(bs_out, bs_in, part, 6 + part).wait_recv()
        for i in range(pair):
            gout_ref[theirs + part * pair + i] = bs_in[part * pair + i]
        heads_of(theirs, part, far_back)

    ends = rq_ref[...].T
    inner_x = ends[8 : 8 + heads, :]
    extra = jnp.sum(ext_ref[...], axis=1, keepdims=True)
    token_iota = lax.broadcasted_iota(jnp.int32, (heads, tokens), 1)
    grad_cum = ends[0:heads, :] - step * inner_x + jnp.where(token_iota == tokens - 1, extra, 0.0)
    lower = (down_iota >= along_iota).astype(F32).astype(BF16)
    high, mid, low = split3(grad_cum)
    grad_dec = mm(high, lower) + (mm(mid, lower) + mm(low, lower))
    gs_ref[...] = inner_x - rate * grad_dec

    for part in range(parts):
        swap_of(fl_own, fl_got, part, part).wait_send()
        both(fs_out, fs_in, part, 2 + part).wait_send()
        swap_of(bl_own, bl_got, part, 4 + part).wait_send()
        both(bs_out, bs_in, part, 6 + part).wait_send()
        ring_all(fm_out, fm_in, part, piece + 1, part).wait_send()
        ring_all(fp_out, fp_in, part, piece, 2 + part).wait_send()
        ring_all(bm_out, bm_in, part, piece, 4 + part).wait_send()
        ring_all(bp_out, bp_in, part, piece, 6 + part).wait_send()
    other_ranks(lambda other: z_copy(other, other).wait_send())


def copy_out(*refs):
    count = len(refs) // 2
    sources, targets, sems = refs[:count], refs[count:-1], refs[-1]
    copies = [pltpu.make_async_copy(s, t, sems.at[i]) for i, (s, t) in enumerate(zip(sources, targets))]
    for copy in copies:
        copy.start()
    for copy in copies:
        copy.wait()


def body(chips, ranks, inputs, b_proj, c_proj, step_sizes, log_rate, forget, skip_gain, norm_gain, target):
    tokens, wide = inputs.shape
    heads = step_sizes.shape[1]
    half = heads // 2
    piece = half * 64 // chips
    vmem = pl.BlockSpec(memory_space=pltpu.VMEM)
    hbm = pl.BlockSpec(memory_space=pltpu.HBM)

    def buffer(*shape, dtype=F32):
        return pltpu.VMEM(shape, dtype)

    state = (heads, 128, 128)
    half_state = (half, 128, 128)
    operands = (
        inputs,
        target,
        b_proj.reshape(tokens, 128),
        c_proj.reshape(tokens, 128),
        step_sizes[0],
        forget[0],
        log_rate,
        skip_gain,
        norm_gain,
    )
    out_shape = (
        jax.ShapeDtypeStruct((tokens, wide), F32),
        jax.ShapeDtypeStruct((tokens, 128), F32),
        jax.ShapeDtypeStruct((tokens, 128), F32),
        jax.ShapeDtypeStruct((heads, tokens), F32),
    )
    results = pl.pallas_call(
        functools.partial(kernel, chips, ranks, float(wide * ranks)),
        out_shape=out_shape,
        in_specs=[hbm] * len(operands),
        out_specs=[vmem] * 4,
        scratch_shapes=[buffer(*operand.shape, dtype=operand.dtype) for operand in operands]
        + [
            buffer(2, heads, tokens),
            buffer(tokens, 128),
            buffer(heads, 128),
            buffer(heads, 128),
            buffer(tokens, tokens),
            buffer(tokens, wide),
            buffer(tokens, wide),
            buffer(tokens, wide),
            buffer(tokens, 128),
            buffer(heads, 128),
            buffer(*state),
            buffer(*state),
            buffer(128, tokens, dtype=BF16),
            buffer(128, tokens, dtype=BF16),
            buffer(tokens, tokens),
            buffer(3, tokens, 128),
            buffer(heads, 136, 128),
            buffer(half, 136, 128),
            buffer(2, chips, piece + 8, 128),
            buffer(2, chips, piece + 8, 128),
            buffer(2, chips, piece, 128),
            buffer(2, chips, piece, 128),
            buffer(*half_state),
            buffer(*half_state),
            buffer(*state),
            buffer(*half_state),
            buffer(2, chips, piece, 128),
            buffer(2, chips, piece, 128),
            buffer(2, chips, piece, 128),
            buffer(2, chips, piece, 128),
            buffer(*half_state),
            buffer(*half_state),
            buffer(8, tokens),
            buffer(ranks, 8, tokens),
            pltpu.SemaphoreType.DMA((9,)),
            pltpu.SemaphoreType.DMA((8,)),
            pltpu.SemaphoreType.DMA((8,)),
            pltpu.SemaphoreType.DMA((8,)),
            pltpu.SemaphoreType.DMA((8,)),
            pltpu.SemaphoreType.DMA((ranks,)),
            pltpu.SemaphoreType.DMA((ranks,)),
        ],
        compiler_params=pltpu.CompilerParams(
            collective_id=0, has_side_effects=True, vmem_limit_bytes=24 * 1024 * 1024
        ),
        name="layer",
    )(*operands)
    grad_x, grad_b, grad_c, grad_steps = pl.pallas_call(
        copy_out,
        out_shape=out_shape,
        in_specs=[pl.BlockSpec(memory_space=pl.ANY)] * 4,
        out_specs=[hbm] * 4,
        scratch_shapes=[pltpu.SemaphoreType.DMA((4,))],
        name="copy_out",
    )(*results)
    return (
        grad_x,
        grad_b.reshape(1, tokens, 1, 128),
        grad_c.reshape(1, tokens, 1, 128),
        grad_steps[None],
    )


def solution(mesh):
    chips, ranks = mesh.shape["ctx"] // 2, mesh.shape["head"]
    in_specs = (
        P("ctx", "head"),
        P(None, "ctx", "head", None),
        P(None, "ctx", "head", None),
        P(None, "head", "ctx"),
        P(None, "head"),
        P(None, "head", "ctx"),
        P(None, "head"),
        P(None, "head"),
        P("ctx", "head"),
    )
    out_specs = (
        P("ctx", "head"),
        P(None, "ctx", "head", None),
        P(None, "ctx", "head", None),
        P(None, "head", "ctx"),
    )
    return jax.shard_map(
        functools.partial(body, chips, ranks),
        mesh=mesh,
        in_specs=in_specs,
        out_specs=out_specs,
        check_vma=False,
    )
```

```python
import functools

import jax
import jax.numpy as jnp
from jax import lax
from jax.experimental import pallas as pl
from jax.experimental.pallas import tpu as pltpu
from jax.sharding import PartitionSpec as P

EPSILON = 1e-05
MESH = pl.DeviceIdType.MESH
F32 = jnp.float32
BF16 = jnp.bfloat16
NN = (((1,), (0,)), ((), ()))
NT = (((1,), (1,)), ((), ()))

CUM, EXPCUM, ENDW, ENDDEC, STEP = range(5)


def mm(left, right, dims=NN):
    return lax.dot_general(left, right, dims, preferred_element_type=F32)


def split2(value):
    high = value.astype(BF16)
    low = (value - high.astype(F32)).astype(BF16)
    return high, low


def split3(value):
    high = value.astype(BF16)
    rest = value - high.astype(F32)
    mid = rest.astype(BF16)
    low = (rest - mid.astype(F32)).astype(BF16)
    return high, mid, low


def mm3(left, right, dims=NN):
    (lh, ll), (rh, rl) = left, right
    return mm(lh, rh, dims) + (mm(lh, rl, dims) + mm(ll, rh, dims))


def kernel(
    chips,
    ranks,
    width,
    x_hbm,
    target_hbm,
    b_hbm,
    c_hbm,
    step_hbm,
    forget_hbm,
    rate_hbm,
    skip_hbm,
    gain_hbm,
    gx_ref,
    gb_ref,
    gc_ref,
    gs_ref,
    x_ref,
    target_ref,
    b_ref,
    c_ref,
    step_ref,
    forget_ref,
    rate_ref,
    skip_ref,
    gain_ref,
    rows_ref,
    cols_ref,
    ends_ref,
    skips_ref,
    scores_ref,
    mixed_ref,
    gm_ref,
    y_ref,
    rq_ref,
    ext_ref,
    sin_ref,
    gout_ref,
    btr_ref,
    ctr_ref,
    dst_ref,
    sum_ref,
    fl_own,
    fl_got,
    fm_out,
    fm_in,
    fp_out,
    fp_in,
    fs_out,
    fs_in,
    bl_own,
    bl_got,
    bm_out,
    bm_in,
    bp_out,
    bp_in,
    bs_out,
    bs_in,
    z_out,
    z_in,
    load_sem,
    pair_send,
    pair_recv,
    ring_send,
    ring_recv,
    z_send,
    z_recv,
):
    tokens = x_ref.shape[0]
    heads = step_ref.shape[0]
    half = heads // 2
    chan = x_ref.shape[1] // heads
    parts, pair = 2, half // 2
    piece = pair * 128 // chips
    per_head = chips // pair
    ctx = lax.axis_index("ctx")
    rank = lax.axis_index("head")
    chip, core = lax.div(ctx, 2), lax.rem(ctx, 2)
    sibling = (chip * 2 + 1 - core, rank)
    lines = chips // 4
    line, place = lax.div(chip, 4), lax.rem(chip, 4)

    loads = [
        pltpu.make_async_copy(source, target, load_sem.at[i])
        for i, (source, target) in enumerate(
            (
                (step_hbm, step_ref),
                (forget_hbm, forget_ref),
                (rate_hbm, rate_ref),
                (b_hbm, b_ref),
                (x_hbm, x_ref),
                (c_hbm, c_ref),
                (skip_hbm, skip_ref),
                (gain_hbm, gain_ref),
                (target_hbm, target_ref),
            )
        )
    ]
    for load in loads:
        load.start()

    def loop(low, high, step):
        def turn(i, carry):
            step(i)
            return carry

        lax.fori_loop(low, high, turn, 0)

    def other_chips(act):
        columns = [lax.rem(place + along, 4) for along in (2, 1, 3, 0)]

        def on_line(q, count):
            down = lines // 2 + (1 - 2 * lax.rem(q, 2)) * lax.div(q + 1, 2)
            base = lax.rem(line + down, lines) * 4
            for column in columns[:count]:
                act(base + column)

        if lines > 1:
            loop(0, lines - 1, lambda q: on_line(q, 4))
        on_line(jnp.int32(lines - 1), 3)

    def other_ranks(act):
        for away in sorted(range(1, ranks), key=lambda k: -min(k, ranks - k)):
            act(lax.rem(rank + away, ranks))

    barrier = pltpu.get_barrier_semaphore()

    def greet(device):
        pl.semaphore_signal(barrier, inc=1, device_id=device, device_id_type=MESH)

    other_chips(lambda other: greet((other * 2 + core, rank)))
    other_ranks(lambda other: greet((ctx, other)))
    greet(sibling)

    down_iota = lax.broadcasted_iota(jnp.int32, (tokens, tokens), 0)
    along_iota = lax.broadcasted_iota(jnp.int32, (tokens, tokens), 1)
    diagonal = down_iota[0:heads, 0:heads] == along_iota[0:heads, 0:heads]

    def as_column(row):
        return jnp.sum(jnp.where(diagonal, row, 0.0), axis=1, keepdims=True)

    for load in loads[0:3]:
        load.wait()
    rate = jnp.exp(as_column(rate_ref[...]))
    step = step_ref[...]
    logdec = -step * rate - forget_ref[...]
    upper = (down_iota <= along_iota).astype(F32).astype(BF16)
    high, mid, low = split3(logdec)
    cum = mm(high, upper) + (mm(mid, upper) + mm(low, upper))
    last = cum[:, tokens - 1 : tokens]
    expcum = jnp.exp(cum)
    enddec = jnp.exp(last - cum)
    table = [cum, expcum, enddec * step, enddec, step]
    rows_ref[0] = cum
    rows_ref[1] = step
    ends_ref[...] = jnp.broadcast_to(jnp.exp(last), (heads, 128))
    table = jnp.concatenate(table + [jnp.zeros((128 - heads * len(table), tokens), F32)], axis=0)
    cols_ref[...] = table.T
    loads[3].wait()
    btr_ref[...] = b_ref[...].astype(F32).T.astype(BF16)
    loads[4].wait()

    def columns_of(h):
        rolled = pltpu.roll(cols_ref[...], lax.rem(128 - h, 128), 1)
        return [rolled[:, 8 * q : 8 * q + 1] for q in range(5)]

    def channels(h):
        return pl.ds(pl.multiple_of(h * chan, chan), chan)

    def cum_row(h):
        return rows_ref[0, pl.ds(h, 1), :]

    def step_row(h):
        return rows_ref[1, pl.ds(h, 1), :]

    def decay_of(h):
        return ends_ref[pl.ds(h, 1), :]

    def skip_of(h):
        return skips_ref[pl.ds(h, 1), :]

    def local_state(h):
        weighted = x_ref[:, channels(h)].astype(F32) * columns_of(h)[ENDW]
        high, low = split2(weighted)
        fl_own[h, 0:128, :] = mm(btr_ref[...], high) + mm(btr_ref[...], low)
        fl_own[h, 128:136, :] = jnp.broadcast_to(decay_of(h), (8, 128))

    def to_sibling(source, target, sem):
        return pltpu.make_async_remote_copy(
            src_ref=source,
            dst_ref=target,
            send_sem=pair_send.at[sem],
            recv_sem=pair_recv.at[sem],
            device_id=sibling,
            device_id_type=MESH,
        )

    mine, theirs = core * half, (1 - core) * half

    def swap_of(own, got, part, sem):
        return to_sibling(own.at[pl.ds(theirs + part * pair, pair)], got.at[pl.ds(part * pair, pair)], sem)

    def heads_of(base, part, act):
        loop(0, pair, lambda i: act(base + part * pair + i))

    def ring_start(source, target, part, rows_sent, sem):
        def start(other):
            pltpu.make_async_remote_copy(
                src_ref=source.at[part, other, 0:rows_sent],
                dst_ref=target.at[part, chip, 0:rows_sent],
                send_sem=ring_send.at[sem],
                recv_sem=ring_recv.at[sem],
                device_id=(other * 2 + core, rank),
                device_id_type=MESH,
            ).start()

        other_chips(start)
        target[part, chip, 0:rows_sent, :] = source[part, chip, 0:rows_sent, :]

    def ring_all(source, target, part, rows_sent, sem):
        return pltpu.make_async_remote_copy(
            src_ref=source.at[part, 0 : chips - 1, 0:rows_sent],
            dst_ref=target.at[part, 0 : chips - 1, 0:rows_sent],
            send_sem=ring_send.at[sem],
            recv_sem=ring_recv.at[sem],
            device_id=sibling,
            device_id_type=MESH,
        )

    def pair_of(own, got, i):
        own_rows, got_rows = own[mine + i, 0:128, :], got[i, 0:128, :]
        first = jnp.where(core == 0, own_rows, got_rows)
        second = jnp.where(core == 0, got_rows, own_rows)
        return first, second

    def decay_pair(i):
        own_decay, got_decay = fl_own[mine + i, 128:129, :], fl_got[i, 128:129, :]
        first = jnp.where(core == 0, own_decay, got_decay)
        second = jnp.where(core == 0, got_decay, own_decay)
        return first, second

    def owners_of(part, i):
        return part, pl.ds(i * per_head, per_head), pl.ds(0, piece)

    def join_forward(part):
        for i in range(pair):
            first, second = pair_of(fl_own, fl_got, part * pair + i)
            decay0, decay1 = decay_pair(part * pair + i)
            joined = decay1 * first + second
            fm_out[owners_of(part, i)] = joined.reshape(per_head, piece, 128)
            fm_out[part, pl.ds(i * per_head, per_head), pl.ds(piece, 8)] = jnp.broadcast_to(
                (decay0 * decay1)[None], (per_head, 8, 128)
            )

    for part in range(parts):
        heads_of(theirs, part, local_state)
        if part == 0:
            pl.semaphore_wait(barrier, (chips - 1) + (ranks - 1) + 1)
        swap_of(fl_own, fl_got, part, part).start()
    for part in range(parts):
        heads_of(mine, part, local_state)
        swap_of(fl_own, fl_got, part, part).wait_recv()
        join_forward(part)
        ring_start(fm_out, fm_in, part, piece + 1, part)

    for load in loads[5:]:
        load.wait()
    skips_ref[...] = jnp.broadcast_to(as_column(skip_ref[...]), (heads, 128))
    ctr_ref[...] = c_ref[...].astype(F32).T.astype(BF16)
    scores_ref[...] = mm(c_ref[...], b_ref[...], NT)

    def near(h):
        cols = columns_of(h)
        gap = jnp.where(down_iota >= along_iota, cols[CUM] - cum_row(h), -1e30)
        weights = scores_ref[...] * jnp.exp(gap) * step_row(h)
        high, low = split2(weights)
        x_h = x_ref[:, channels(h)]
        mixed_ref[:, channels(h)] = mm(high, x_h) + mm(low, x_h)

    loop(0, heads, near)
    sum_ref[...] = jnp.zeros_like(sum_ref)

    for part in range(parts):
        ring_all(fm_out, fm_in, part, piece + 1, part).wait_recv()
        state = jnp.zeros((piece, 128), F32)
        for t in range(chips):
            fp_out[part, t] = state
            state = fm_in[part, t, piece : piece + 1, :] * state + fm_in[part, t, 0:piece, :]
        ring_start(fp_out, fp_in, part, piece, 2 + part)

    def enter(part):
        for i in range(pair):
            at = part * pair + i
            first, _ = pair_of(fl_own, fl_got, at)
            decay0, _ = decay_pair(at)
            for_first = fp_in[owners_of(part, i)].reshape(128, 128)
            for_second = decay0 * for_first + first
            sin_ref[mine + at] = jnp.where(core == 0, for_first, for_second)
            fs_out[at] = jnp.where(core == 0, for_second, for_first)

    def both(own, got, part, sem):
        here = pl.ds(part * pair, pair)
        return to_sibling(own.at[here], got.at[here], sem)

    def far(h):
        cols = columns_of(h)
        high, low = split2(sin_ref[h])
        reached = mm(c_ref[...], high) + mm(c_ref[...], low)
        x_h = x_ref[:, channels(h)].astype(F32)
        mixed = mixed_ref[:, channels(h)] + cols[EXPCUM] * reached + skip_of(h) * x_h
        mixed_ref[:, channels(h)] = mixed
        gained = gain_ref[:, channels(h)] * mixed
        sum_ref[0] += mixed * mixed
        sum_ref[1] += gained * (x_h - target_ref[:, channels(h)].astype(F32))
        sum_ref[2] += gained * gained

    for part in range(parts):
        ring_all(fp_out, fp_in, part, piece, 2 + part).wait_recv()
        enter(part)
        both(fs_out, fs_in, part, 2 + part).start()
        heads_of(mine, part, far)
    for part in range(parts):
        both(fs_out, fs_in, part, 2 + part).wait_recv()
        for i in range(pair):
            sin_ref[theirs + part * pair + i] = fs_in[part * pair + i]
        heads_of(theirs, part, far)

    lane = lax.broadcasted_iota(jnp.int32, (tokens, 128), 1)
    packed = jnp.zeros((tokens, 128), F32)
    for i in range(3):
        packed = jnp.where(lane == i, jnp.sum(sum_ref[i], axis=1, keepdims=True), packed)
    z_out[...] = packed.T[0:8, :]

    def z_copy(to, slot):
        return pltpu.make_async_remote_copy(
            src_ref=z_out,
            dst_ref=z_in.at[slot],
            send_sem=z_send.at[to],
            recv_sem=z_recv.at[slot],
            device_id=(ctx, to),
            device_id_type=MESH,
        )

    other_ranks(lambda other: z_copy(other, rank).start())
    z_in[rank] = z_out[...]
    other_ranks(lambda other: z_copy(other, other).wait_recv())
    total = z_in[0]
    for i in range(1, ranks):
        total = total + z_in[i]
    inv_scale = lax.rsqrt(total[0:1, :] / width + EPSILON)
    inner = total[1:2, :] + inv_scale * total[2:3, :]
    coef = inner * inv_scale * inv_scale * inv_scale / width
    back = jnp.concatenate([inv_scale, coef, jnp.zeros((126, tokens), F32)], axis=0).T
    inv_col, coef_col = back[:, 0:1], back[:, 1:2]

    def norm_back(h):
        gain = gain_ref[:, channels(h)]
        mixed = mixed_ref[:, channels(h)]
        x_h = x_ref[:, channels(h)].astype(F32)
        grad_out = x_h + gain * mixed * inv_col - target_ref[:, channels(h)].astype(F32)
        grad_mixed = gain * grad_out * inv_col - mixed * coef_col
        gm_ref[:, channels(h)] = grad_mixed
        gx_ref[:, channels(h)] = grad_out + skip_of(h) * grad_mixed
        high, low = split2(grad_mixed * columns_of(h)[EXPCUM])
        bl_own[h] = mm(ctr_ref[...], high) + mm(ctr_ref[...], low)

    def join_back(part):
        for i in range(pair):
            first, second = pair_of(bl_own, bl_got, part * pair + i)
            decay0, _ = decay_pair(part * pair + i)
            bm_out[owners_of(part, i)] = (decay0 * second + first).reshape(per_head, piece, 128)

    for part in range(parts):
        heads_of(theirs, part, norm_back)
        swap_of(bl_own, bl_got, part, 4 + part).start()
    for part in range(parts):
        heads_of(mine, part, norm_back)
        swap_of(bl_own, bl_got, part, 4 + part).wait_recv()
        join_back(part)
        ring_start(bm_out, bm_in, part, piece, 4 + part)

    rq_ref[...] = jnp.zeros_like(rq_ref)
    gc_ref[...] = jnp.zeros_like(gc_ref)
    gb_ref[...] = jnp.zeros_like(gb_ref)
    dst_ref[...] = jnp.zeros_like(dst_ref)
    scores_ref[...] = mm(b_ref[...], c_ref[...], NT)

    def near_back(h):
        cols = columns_of(h)
        gap = jnp.where(along_iota >= down_iota, cum_row(h) - cols[CUM], -1e30)
        decay = jnp.exp(gap)
        grad_mixed = gm_ref[:, channels(h)]
        gm_parts = split2(grad_mixed)
        x_h = x_ref[:, channels(h)]
        y_ref[:, channels(h)] = mm3(split2(scores_ref[...] * decay), gm_parts)
        grad_weights = mm(x_h, gm_parts[0], NT) + mm(x_h, gm_parts[1], NT)
        dst_ref[...] += grad_weights * decay * cols[STEP]
        own = grad_mixed * (mixed_ref[:, channels(h)] - skip_of(h) * x_h.astype(F32))
        rq_ref[...] = jnp.where(lane == h, jnp.sum(own, axis=1, keepdims=True), rq_ref[...])
        gc_ref[...] += mm3(split2(grad_mixed * cols[EXPCUM]), split2(sin_ref[h]), NT)

    loop(0, heads, near_back)
    grad_scores = dst_ref[...]
    high, low = split2(grad_scores)
    gb_ref[...] += mm(high, c_ref[...]) + mm(low, c_ref[...])
    high, low = split2(grad_scores.T)
    gc_ref[...] += mm(high, b_ref[...]) + mm(low, b_ref[...])

    for part in range(parts):
        ring_all(bm_out, bm_in, part, piece, 4 + part).wait_recv()
        grad = jnp.zeros((piece, 128), F32)
        for t in reversed(range(chips)):
            bp_out[part, t] = grad
            grad = fm_in[part, t, piece : piece + 1, :] * grad + bm_in[part, t]
        ring_start(bp_out, bp_in, part, piece, 6 + part)

    def leave(part):
        for i in range(pair):
            at = part * pair + i
            _, second = pair_of(bl_own, bl_got, at)
            _, decay1 = decay_pair(at)
            for_second = bp_in[owners_of(part, i)].reshape(128, 128)
            for_first = decay1 * for_second + second
            gout_ref[mine + at] = jnp.where(core == 0, for_first, for_second)
            bs_out[at] = jnp.where(core == 0, for_second, for_first)

    def far_back(h):
        cols = columns_of(h)
        grad_state = gout_ref[h]
        high, low = split2(grad_state)
        x_h = x_ref[:, channels(h)]
        reached = mm(b_ref[...], high) + mm(b_ref[...], low)
        value = y_ref[:, channels(h)] + cols[ENDDEC] * reached
        gx_ref[:, channels(h)] += cols[STEP] * value
        own = jnp.sum(x_h.astype(F32) * value, axis=1, keepdims=True)
        rq_ref[...] = jnp.where(lane == h + 8, own, rq_ref[...])
        gb_ref[...] += cols[ENDW] * (mm(x_h, high, NT) + mm(x_h, low, NT))
        leaving = decay_of(h) * sin_ref[h] + fl_own[h, 0:128, :]
        ext_ref[pl.ds(h, 1), :] = jnp.sum(grad_state * leaving, axis=0, keepdims=True)

    for part in range(parts):
        ring_all(bp_out, bp_in, part, piece, 6 + part).wait_recv()
        leave(part)
        both(bs_out, bs_in, part, 6 + part).start()
        heads_of(mine, part, far_back)
    for part in range(parts):
        both(bs_out, bs_in, part, 6 + part).wait_recv()
        for i in range(pair):
            gout_ref[theirs + part * pair + i] = bs_in[part * pair + i]
        heads_of(theirs, part, far_back)

    ends = rq_ref[...].T
    inner_x = ends[8 : 8 + heads, :]
    extra = jnp.sum(ext_ref[...], axis=1, keepdims=True)
    token_iota = lax.broadcasted_iota(jnp.int32, (heads, tokens), 1)
    grad_cum = ends[0:heads, :] - step * inner_x + jnp.where(token_iota == tokens - 1, extra, 0.0)
    lower = (down_iota >= along_iota).astype(F32).astype(BF16)
    high, mid, low = split3(grad_cum)
    grad_dec = mm(high, lower) + (mm(mid, lower) + mm(low, lower))
    gs_ref[...] = inner_x - rate * grad_dec

    for part in range(parts):
        swap_of(fl_own, fl_got, part, part).wait_send()
        both(fs_out, fs_in, part, 2 + part).wait_send()
        swap_of(bl_own, bl_got, part, 4 + part).wait_send()
        both(bs_out, bs_in, part, 6 + part).wait_send()
        ring_all(fm_out, fm_in, part, piece + 1, part).wait_send()
        ring_all(fp_out, fp_in, part, piece, 2 + part).wait_send()
        ring_all(bm_out, bm_in, part, piece, 4 + part).wait_send()
        ring_all(bp_out, bp_in, part, piece, 6 + part).wait_send()
    other_ranks(lambda other: z_copy(other, other).wait_send())


def copy_out(*refs):
    count = len(refs) // 2
    sources, targets, sems = refs[:count], refs[count:-1], refs[-1]
    copies = [pltpu.make_async_copy(s, t, sems.at[i]) for i, (s, t) in enumerate(zip(sources, targets))]
    for copy in copies:
        copy.start()
    for copy in copies:
        copy.wait()


def body(chips, ranks, inputs, b_proj, c_proj, step_sizes, log_rate, forget, skip_gain, norm_gain, target):
    tokens, wide = inputs.shape
    heads = step_sizes.shape[1]
    half = heads // 2
    piece = half * 64 // chips
    vmem = pl.BlockSpec(memory_space=pltpu.VMEM)
    hbm = pl.BlockSpec(memory_space=pltpu.HBM)

    def buffer(*shape, dtype=F32):
        return pltpu.VMEM(shape, dtype)

    state = (heads, 128, 128)
    half_state = (half, 128, 128)
    operands = (
        inputs,
        target,
        b_proj.reshape(tokens, 128),
        c_proj.reshape(tokens, 128),
        step_sizes[0],
        forget[0],
        log_rate,
        skip_gain,
        norm_gain,
    )
    operands = tuple(pltpu.with_memory_space_constraint(operand, pltpu.HBM) for operand in operands)
    out_shape = (
        jax.ShapeDtypeStruct((tokens, wide), F32),
        jax.ShapeDtypeStruct((tokens, 128), F32),
        jax.ShapeDtypeStruct((tokens, 128), F32),
        jax.ShapeDtypeStruct((heads, tokens), F32),
    )
    results = pl.pallas_call(
        functools.partial(kernel, chips, ranks, float(wide * ranks)),
        out_shape=out_shape,
        in_specs=[hbm] * len(operands),
        out_specs=[vmem] * 4,
        scratch_shapes=[buffer(*operand.shape, dtype=operand.dtype) for operand in operands]
        + [
            buffer(2, heads, tokens),
            buffer(tokens, 128),
            buffer(heads, 128),
            buffer(heads, 128),
            buffer(tokens, tokens),
            buffer(tokens, wide),
            buffer(tokens, wide),
            buffer(tokens, wide),
            buffer(tokens, 128),
            buffer(heads, 128),
            buffer(*state),
            buffer(*state),
            buffer(128, tokens, dtype=BF16),
            buffer(128, tokens, dtype=BF16),
            buffer(tokens, tokens),
            buffer(3, tokens, 128),
            buffer(heads, 136, 128),
            buffer(half, 136, 128),
            buffer(2, chips, piece + 8, 128),
            buffer(2, chips, piece + 8, 128),
            buffer(2, chips, piece, 128),
            buffer(2, chips, piece, 128),
            buffer(*half_state),
            buffer(*half_state),
            buffer(*state),
            buffer(*half_state),
            buffer(2, chips, piece, 128),
            buffer(2, chips, piece, 128),
            buffer(2, chips, piece, 128),
            buffer(2, chips, piece, 128),
            buffer(*half_state),
            buffer(*half_state),
            buffer(8, tokens),
            buffer(ranks, 8, tokens),
            pltpu.SemaphoreType.DMA((9,)),
            pltpu.SemaphoreType.DMA((8,)),
            pltpu.SemaphoreType.DMA((8,)),
            pltpu.SemaphoreType.DMA((8,)),
            pltpu.SemaphoreType.DMA((8,)),
            pltpu.SemaphoreType.DMA((ranks,)),
            pltpu.SemaphoreType.DMA((ranks,)),
        ],
        compiler_params=pltpu.CompilerParams(
            collective_id=0, has_side_effects=True, vmem_limit_bytes=24 * 1024 * 1024
        ),
        name="layer",
    )(*operands)
    grad_x, grad_b, grad_c, grad_steps = pl.pallas_call(
        copy_out,
        out_shape=out_shape,
        in_specs=[pl.BlockSpec(memory_space=pl.ANY)] * 4,
        out_specs=[hbm] * 4,
        scratch_shapes=[pltpu.SemaphoreType.DMA((4,))],
        compiler_params=pltpu.CompilerParams(vmem_limit_bytes=1024 * 1024),
        name="copy_out",
    )(*results)
    return (
        grad_x,
        grad_b.reshape(1, tokens, 1, 128),
        grad_c.reshape(1, tokens, 1, 128),
        grad_steps[None],
    )


def solution(mesh):
    chips, ranks = mesh.shape["ctx"] // 2, mesh.shape["head"]
    in_specs = (
        P("ctx", "head"),
        P(None, "ctx", "head", None),
        P(None, "ctx", "head", None),
        P(None, "head", "ctx"),
        P(None, "head"),
        P(None, "head", "ctx"),
        P(None, "head"),
        P(None, "head"),
        P("ctx", "head"),
    )
    out_specs = (
        P("ctx", "head"),
        P(None, "ctx", "head", None),
        P(None, "ctx", "head", None),
        P(None, "head", "ctx"),
    )
    return jax.shard_map(
        functools.partial(body, chips, ranks),
        mesh=mesh,
        in_specs=in_specs,
        out_specs=out_specs,
        check_vma=False,
    )
```

```python
import functools

import jax
import jax.numpy as jnp
from jax import lax
from jax.experimental import pallas as pl
from jax.experimental.pallas import tpu as pltpu
from jax.sharding import PartitionSpec as P

EPSILON = 1e-05
MESH = pl.DeviceIdType.MESH
F32 = jnp.float32
BF16 = jnp.bfloat16
NN = (((1,), (0,)), ((), ()))
NT = (((1,), (1,)), ((), ()))

CUM, EXPCUM, ENDW, ENDDEC, STEP = range(5)


def mm(left, right, dims=NN):
    return lax.dot_general(left, right, dims, preferred_element_type=F32)


def split2(value):
    high = value.astype(BF16)
    low = (value - high.astype(F32)).astype(BF16)
    return high, low


def split3(value):
    high = value.astype(BF16)
    rest = value - high.astype(F32)
    mid = rest.astype(BF16)
    low = (rest - mid.astype(F32)).astype(BF16)
    return high, mid, low


def mm3(left, right, dims=NN):
    (lh, ll), (rh, rl) = left, right
    return mm(lh, rh, dims) + (mm(lh, rl, dims) + mm(ll, rh, dims))


def kernel(
    chips,
    ranks,
    width,
    x_hbm,
    target_hbm,
    b_hbm,
    c_hbm,
    step_hbm,
    forget_hbm,
    rate_hbm,
    skip_hbm,
    gain_hbm,
    gx_ref,
    gb_ref,
    gc_ref,
    gs_ref,
    x_ref,
    target_ref,
    b_ref,
    c_ref,
    step_ref,
    forget_ref,
    rate_ref,
    skip_ref,
    gain_ref,
    rows_ref,
    cols_ref,
    ends_ref,
    skips_ref,
    scores_ref,
    mixed_ref,
    gm_ref,
    u_ref,
    expb_ref,
    endwb_ref,
    cc_ref,
    bb_ref,
    scale_ref,
    rq_ref,
    ext_ref,
    sin_ref,
    gout_ref,
    btr_ref,
    ctr_ref,
    dst_ref,
    sum_ref,
    fl_own,
    fl_got,
    fm_out,
    fm_in,
    fp_out,
    fp_in,
    fs_out,
    fs_in,
    bl_own,
    bl_got,
    bm_out,
    bm_in,
    bp_out,
    bp_in,
    bs_out,
    bs_in,
    z_out,
    z_in,
    load_sem,
    pair_send,
    pair_recv,
    ring_send,
    ring_recv,
    z_send,
    z_recv,
):
    tokens = x_ref.shape[0]
    heads = step_ref.shape[0]
    half = heads // 2
    chan = x_ref.shape[1] // heads
    parts, pair = 2, half // 2
    piece = pair * 128 // chips
    per_head = chips // pair
    ctx = lax.axis_index("ctx")
    rank = lax.axis_index("head")
    chip, core = lax.div(ctx, 2), lax.rem(ctx, 2)
    sibling = (chip * 2 + 1 - core, rank)
    lines = chips // 4
    line, place = lax.div(chip, 4), lax.rem(chip, 4)

    def loop(low, high, step):
        def turn(i, carry):
            step(i)
            return carry

        lax.fori_loop(low, high, turn, 0)

    def other_chips(act):
        columns = [lax.rem(place + along, 4) for along in (2, 1, 3, 0)]

        def on_line(q, count):
            down = lines // 2 + (1 - 2 * lax.rem(q, 2)) * lax.div(q + 1, 2)
            base = lax.rem(line + down, lines) * 4
            for column in columns[:count]:
                act(base + column)

        if lines > 1:
            loop(0, lines - 1, lambda q: on_line(q, 4))
        on_line(jnp.int32(lines - 1), 3)

    def other_ranks(act):
        for away in sorted(range(1, ranks), key=lambda k: -min(k, ranks - k)):
            act(lax.rem(rank + away, ranks))

    barrier = pltpu.get_barrier_semaphore()

    def greet(device):
        pl.semaphore_signal(barrier, inc=1, device_id=device, device_id_type=MESH)

    other_chips(lambda other: greet((other * 2 + core, rank)))
    other_ranks(lambda other: greet((ctx, other)))
    greet(sibling)

    loads = [
        pltpu.make_async_copy(source, target, load_sem.at[i])
        for i, (source, target) in enumerate(
            (
                (step_hbm, step_ref),
                (forget_hbm, forget_ref),
                (rate_hbm, rate_ref),
                (b_hbm, b_ref),
                (x_hbm, x_ref),
                (c_hbm, c_ref),
                (skip_hbm, skip_ref),
                (gain_hbm, gain_ref),
                (target_hbm, target_ref),
            )
        )
    ]
    for load in loads:
        load.start()

    down_iota = lax.broadcasted_iota(jnp.int32, (tokens, tokens), 0)
    along_iota = lax.broadcasted_iota(jnp.int32, (tokens, tokens), 1)
    diagonal = down_iota[0:heads, 0:heads] == along_iota[0:heads, 0:heads]

    def as_column(row):
        return jnp.sum(jnp.where(diagonal, row, 0.0), axis=1, keepdims=True)

    for load in loads[0:3]:
        load.wait()
    rate = jnp.exp(as_column(rate_ref[...]))
    step = step_ref[...]
    logdec = -step * rate - forget_ref[...]
    upper = (down_iota <= along_iota).astype(F32).astype(BF16)
    high, mid, low = split3(logdec)
    cum = mm(high, upper) + (mm(mid, upper) + mm(low, upper))
    last = cum[:, tokens - 1 : tokens]
    expcum = jnp.exp(cum)
    enddec = jnp.exp(last - cum)
    table = [cum, expcum, enddec * step, enddec, step]
    rows_ref[0] = cum
    rows_ref[1] = step
    rows_ref[2] = enddec
    ends_ref[...] = jnp.broadcast_to(jnp.exp(last), (heads, 128))
    table = jnp.concatenate(table + [jnp.zeros((128 - heads * len(table), tokens), F32)], axis=0)
    cols_ref[...] = table.T
    loads[3].wait()
    btr_ref[...] = b_ref[...].astype(F32).T.astype(BF16)
    loads[4].wait()

    def columns_of(h, count=1):
        rolled = pltpu.roll(cols_ref[...], lax.rem(128 - h, 128), 1)
        each = [[rolled[:, 8 * q + k : 8 * q + k + 1] for q in range(5)] for k in range(count)]
        return each if count > 1 else each[0]

    def channels(h):
        return pl.ds(pl.multiple_of(h * chan, chan), chan)

    def cum_row(h):
        return rows_ref[0, pl.ds(h, 1), :]

    def step_row(h):
        return rows_ref[1, pl.ds(h, 1), :]

    def decay_of(h):
        return ends_ref[pl.ds(h, 1), :]

    def skip_of(h):
        return skips_ref[pl.ds(h, 1), :]

    def two(make):
        return jnp.concatenate([make(0), make(1)], axis=1)

    def local_state(h):
        columns = columns_of(h, 2)
        weighted = two(lambda k: x_ref[:, channels(h + k)].astype(F32) * columns[k][ENDW])
        high, low = split2(weighted)
        state = mm(btr_ref[...], high) + mm(btr_ref[...], low)
        for k in range(2):
            fl_own[h + k, 0:128, :] = state[:, k * 128 : k * 128 + 128]
            fl_own[h + k, 128:136, :] = jnp.broadcast_to(decay_of(h + k), (8, 128))

    def to_sibling(source, target, sem):
        return pltpu.make_async_remote_copy(
            src_ref=source,
            dst_ref=target,
            send_sem=pair_send.at[sem],
            recv_sem=pair_recv.at[sem],
            device_id=sibling,
            device_id_type=MESH,
        )

    mine, theirs = core * half, (1 - core) * half

    def swap_of(own, got, part, sem):
        return to_sibling(own.at[pl.ds(theirs + part * pair, pair)], got.at[pl.ds(part * pair, pair)], sem)

    def heads_of(base, part, act):
        act(base + part * pair)

    def ring_start(source, target, part, rows_sent, sem):
        def start(other):
            pltpu.make_async_remote_copy(
                src_ref=source.at[part, other, 0:rows_sent],
                dst_ref=target.at[part, chip, 0:rows_sent],
                send_sem=ring_send.at[sem],
                recv_sem=ring_recv.at[sem],
                device_id=(other * 2 + core, rank),
                device_id_type=MESH,
            ).start()

        other_chips(start)
        target[part, chip, 0:rows_sent, :] = source[part, chip, 0:rows_sent, :]

    def ring_all(source, target, part, rows_sent, sem):
        return pltpu.make_async_remote_copy(
            src_ref=source.at[part, 0 : chips - 1, 0:rows_sent],
            dst_ref=target.at[part, 0 : chips - 1, 0:rows_sent],
            send_sem=ring_send.at[sem],
            recv_sem=ring_recv.at[sem],
            device_id=sibling,
            device_id_type=MESH,
        )

    def pair_of(own, got, i):
        own_rows, got_rows = own[mine + i, 0:128, :], got[i, 0:128, :]
        first = jnp.where(core == 0, own_rows, got_rows)
        second = jnp.where(core == 0, got_rows, own_rows)
        return first, second

    def decay_pair(i):
        own_decay, got_decay = fl_own[mine + i, 128:129, :], fl_got[i, 128:129, :]
        first = jnp.where(core == 0, own_decay, got_decay)
        second = jnp.where(core == 0, got_decay, own_decay)
        return first, second

    def owners_of(part, i):
        return part, pl.ds(i * per_head, per_head), pl.ds(0, piece)

    def join_forward(part):
        for i in range(pair):
            first, second = pair_of(fl_own, fl_got, part * pair + i)
            decay0, decay1 = decay_pair(part * pair + i)
            joined = decay1 * first + second
            fm_out[owners_of(part, i)] = joined.reshape(per_head, piece, 128)
            fm_out[part, pl.ds(i * per_head, per_head), pl.ds(piece, 8)] = jnp.broadcast_to(
                (decay0 * decay1)[None], (per_head, 8, 128)
            )

    for part in range(parts):
        heads_of(theirs, part, local_state)
        if part == 0:
            pl.semaphore_wait(barrier, (chips - 1) + (ranks - 1) + 1)
        swap_of(fl_own, fl_got, part, part).start()
    for part in range(parts):
        heads_of(mine, part, local_state)
        swap_of(fl_own, fl_got, part, part).wait_recv()
        join_forward(part)
        ring_start(fm_out, fm_in, part, piece + 1, part)

    for load in loads[5:]:
        load.wait()
    skips_ref[...] = jnp.broadcast_to(as_column(skip_ref[...]), (heads, 128))
    ctr_ref[...] = c_ref[...].astype(F32).T.astype(BF16)
    scores_ref[...] = mm(c_ref[...], b_ref[...], NT)
    cc_ref[...] = jnp.concatenate([c_ref[...], c_ref[...]], axis=1)
    bb_ref[...] = jnp.concatenate([b_ref[...], b_ref[...]], axis=1)

    def near(h):
        cols = columns_of(h)
        gap = jnp.where(down_iota >= along_iota, cols[CUM] - cum_row(h), -1e30)
        weights = scores_ref[...] * jnp.exp(gap) * step_row(h)
        high, low = split2(weights)
        x_h = x_ref[:, channels(h)]
        wide_x = x_h.astype(F32)
        mixed_ref[:, channels(h)] = mm(high, x_h) + mm(low, x_h) + skip_of(h) * wide_x
        u_ref[:, channels(h)] = gain_ref[:, channels(h)] * (wide_x - target_ref[:, channels(h)].astype(F32))
        expb_ref[:, channels(h)] = jnp.broadcast_to(cols[EXPCUM], (tokens, 128))
        endwb_ref[:, channels(h)] = jnp.broadcast_to(cols[ENDW], (tokens, 128))

    loop(0, heads, near)
    sum_ref[...] = jnp.zeros_like(sum_ref)

    for part in range(parts):
        ring_all(fm_out, fm_in, part, piece + 1, part).wait_recv()
        state = jnp.zeros((piece, 128), F32)
        for t in range(chips):
            fp_out[part, t] = state
            state = fm_in[part, t, piece : piece + 1, :] * state + fm_in[part, t, 0:piece, :]
        ring_start(fp_out, fp_in, part, piece, 2 + part)

    def enter(part):
        for i in range(pair):
            at = part * pair + i
            first, _ = pair_of(fl_own, fl_got, at)
            decay0, _ = decay_pair(at)
            for_first = fp_in[owners_of(part, i)].reshape(128, 128)
            for_second = decay0 * for_first + first
            sin_ref[mine + at] = jnp.where(core == 0, for_first, for_second)
            fs_out[at] = jnp.where(core == 0, for_second, for_first)

    def both(own, got, part, sem):
        here = pl.ds(part * pair, pair)
        return to_sibling(own.at[here], got.at[here], sem)

    def stacked(ref, h):
        high, low = split2(two(lambda k: ref[h + k]))
        return jnp.concatenate([high, low], axis=0)

    def far(h):
        reached = mm(cc_ref[...], stacked(sin_ref, h))
        sums = [0.0, 0.0, 0.0]
        for k in range(2):
            here = channels(h + k)
            mixed = mixed_ref[:, here] + expb_ref[:, here] * reached[:, k * 128 : k * 128 + 128]
            mixed_ref[:, here] = mixed
            gained = gain_ref[:, here] * mixed
            sums = [sums[0] + mixed * mixed, sums[1] + u_ref[:, here] * mixed, sums[2] + gained * gained]
        for i in range(3):
            sum_ref[i] += sums[i]

    for part in range(parts):
        ring_all(fp_out, fp_in, part, piece, 2 + part).wait_recv()
        enter(part)
        both(fs_out, fs_in, part, 2 + part).start()
        heads_of(mine, part, far)
    for part in range(parts):
        both(fs_out, fs_in, part, 2 + part).wait_recv()
        for i in range(pair):
            sin_ref[theirs + part * pair + i] = fs_in[part * pair + i]
        heads_of(theirs, part, far)

    lane = lax.broadcasted_iota(jnp.int32, (tokens, 128), 1)
    packed = jnp.zeros((tokens, 128), F32)
    for i in range(3):
        packed = jnp.where(lane == i, jnp.sum(sum_ref[i], axis=1, keepdims=True), packed)
    z_out[...] = packed.T[0:8, :]

    def z_copy(to, slot):
        return pltpu.make_async_remote_copy(
            src_ref=z_out,
            dst_ref=z_in.at[slot],
            send_sem=z_send.at[to],
            recv_sem=z_recv.at[slot],
            device_id=(ctx, to),
            device_id_type=MESH,
        )

    other_ranks(lambda other: z_copy(other, rank).start())
    z_in[rank] = z_out[...]
    other_ranks(lambda other: z_copy(other, other).wait_recv())
    total = z_in[0]
    for i in range(1, ranks):
        total = total + z_in[i]
    inv_scale = lax.rsqrt(total[0:1, :] / width + EPSILON)
    inner = total[1:2, :] + inv_scale * total[2:3, :]
    coef = inner * inv_scale * inv_scale * inv_scale / width
    back = jnp.concatenate([inv_scale, coef, jnp.zeros((126, tokens), F32)], axis=0).T
    inv_col = jnp.broadcast_to(back[:, 0:1], (tokens, 128))
    scale_ref[0] = inv_col
    scale_ref[1] = inv_col * inv_col
    scale_ref[2] = jnp.broadcast_to(back[:, 1:2], (tokens, 128))

    def norm_back(h):
        def weighted(k):
            here = channels(h + k)
            gain = gain_ref[:, here]
            factor = (gain * gain) * scale_ref[1] - scale_ref[2]
            grad_mixed = u_ref[:, here] * scale_ref[0] + mixed_ref[:, here] * factor
            gm_ref[:, here] = grad_mixed
            return grad_mixed * expb_ref[:, here]

        high, low = split2(two(weighted))
        state = mm(ctr_ref[...], high) + mm(ctr_ref[...], low)
        for k in range(2):
            bl_own[h + k] = state[:, k * 128 : k * 128 + 128]

    def join_back(part):
        for i in range(pair):
            first, second = pair_of(bl_own, bl_got, part * pair + i)
            decay0, _ = decay_pair(part * pair + i)
            bm_out[owners_of(part, i)] = (decay0 * second + first).reshape(per_head, piece, 128)

    for part in range(parts):
        heads_of(theirs, part, norm_back)
        swap_of(bl_own, bl_got, part, 4 + part).start()
    for part in range(parts):
        heads_of(mine, part, norm_back)
        swap_of(bl_own, bl_got, part, 4 + part).wait_recv()
        join_back(part)
        ring_start(bm_out, bm_in, part, piece, 4 + part)

    rq_ref[...] = jnp.zeros_like(rq_ref)
    gc_ref[...] = jnp.zeros_like(gc_ref)
    gb_ref[...] = jnp.zeros_like(gb_ref)
    dst_ref[...] = jnp.zeros_like(dst_ref)
    scores_ref[...] = mm(b_ref[...], c_ref[...], NT)

    def near_back(h):
        cols = columns_of(h)
        here = channels(h)
        gap = jnp.where(along_iota >= down_iota, cum_row(h) - cols[CUM], -1e30)
        decay = jnp.exp(gap)
        grad_mixed = gm_ref[:, here]
        gm_parts = split2(grad_mixed)
        x_h = x_ref[:, here]
        wide_x = x_h.astype(F32)
        mixed = mixed_ref[:, here]
        value = mm3(split2(scores_ref[...] * decay), gm_parts)
        grad_out = wide_x + gain_ref[:, here] * mixed * scale_ref[0] - target_ref[:, here].astype(F32)
        gx_ref[:, here] = grad_out + skip_of(h) * grad_mixed + cols[STEP] * value
        grad_weights = mm(x_h, gm_parts[0], NT) + mm(x_h, gm_parts[1], NT)
        dst_ref[...] += grad_weights * decay * cols[STEP]
        row_sum = jnp.sum(grad_mixed * (mixed - skip_of(h) * wide_x), axis=1, keepdims=True)
        column_sum = jnp.sum(wide_x * value, axis=1, keepdims=True)
        rq_ref[...] = jnp.where(lane == h, row_sum, jnp.where(lane == h + 8, column_sum, rq_ref[...]))
        gc_ref[...] += mm3(split2(grad_mixed * expb_ref[:, here]), split2(sin_ref[h]), NT)

    loop(0, heads, near_back)
    grad_scores = dst_ref[...]
    high, low = split2(grad_scores)
    gb_ref[...] += mm(high, c_ref[...]) + mm(low, c_ref[...])
    high, low = split2(grad_scores.T)
    gc_ref[...] += mm(high, b_ref[...]) + mm(low, b_ref[...])

    for part in range(parts):
        ring_all(bm_out, bm_in, part, piece, 4 + part).wait_recv()
        grad = jnp.zeros((piece, 128), F32)
        for t in reversed(range(chips)):
            bp_out[part, t] = grad
            grad = fm_in[part, t, piece : piece + 1, :] * grad + bm_in[part, t]
        ring_start(bp_out, bp_in, part, piece, 6 + part)

    def leave(part):
        for i in range(pair):
            at = part * pair + i
            _, second = pair_of(bl_own, bl_got, at)
            _, decay1 = decay_pair(at)
            for_second = bp_in[owners_of(part, i)].reshape(128, 128)
            for_first = decay1 * for_second + second
            gout_ref[mine + at] = jnp.where(core == 0, for_first, for_second)
            bs_out[at] = jnp.where(core == 0, for_second, for_first)

    def far_back(h):
        both_parts = stacked(gout_ref, h)
        reached = mm(bb_ref[...], both_parts)
        table = rq_ref[...]
        grad_b = gb_ref[...]
        for k in range(2):
            here = channels(h + k)
            at = slice(k * 128, k * 128 + 128)
            x_h = x_ref[:, here]
            weight = endwb_ref[:, here]
            gx_ref[:, here] += weight * reached[:, at]
            row_sum = jnp.sum(x_h.astype(F32) * reached[:, at], axis=1, keepdims=True)
            table = jnp.where(lane == h + k + 16, row_sum, table)
            parts_along = jnp.concatenate([both_parts[0:128, at], both_parts[128:256, at]], axis=1)
            grad_b = grad_b + weight * mm(jnp.concatenate([x_h, x_h], axis=1), parts_along, NT)
            leaving = decay_of(h + k) * sin_ref[h + k] + fl_own[h + k, 0:128, :]
            ext_ref[pl.ds(h + k, 1), :] = jnp.sum(gout_ref[h + k] * leaving, axis=0, keepdims=True)
        rq_ref[...] = table
        gb_ref[...] = grad_b

    for part in range(parts):
        ring_all(bp_out, bp_in, part, piece, 6 + part).wait_recv()
        leave(part)
        both(bs_out, bs_in, part, 6 + part).start()
        heads_of(mine, part, far_back)
    for part in range(parts):
        both(bs_out, bs_in, part, 6 + part).wait_recv()
        for i in range(pair):
            gout_ref[theirs + part * pair + i] = bs_in[part * pair + i]
        heads_of(theirs, part, far_back)

    ends = rq_ref[...].T
    inner_x = ends[8 : 8 + heads, :] + rows_ref[2] * ends[16 : 16 + heads, :]
    extra = jnp.sum(ext_ref[...], axis=1, keepdims=True)
    lower = (down_iota >= along_iota).astype(F32).astype(BF16)
    high, mid, low = split3(ends[0:heads, :] - step * inner_x)
    grad_dec = mm(high, lower) + (mm(mid, lower) + mm(low, lower)) + extra
    gs_ref[...] = inner_x - rate * grad_dec

    for part in range(parts):
        swap_of(fl_own, fl_got, part, part).wait_send()
        both(fs_out, fs_in, part, 2 + part).wait_send()
        swap_of(bl_own, bl_got, part, 4 + part).wait_send()
        both(bs_out, bs_in, part, 6 + part).wait_send()
        ring_all(fm_out, fm_in, part, piece + 1, part).wait_send()
        ring_all(fp_out, fp_in, part, piece, 2 + part).wait_send()
        ring_all(bm_out, bm_in, part, piece, 4 + part).wait_send()
        ring_all(bp_out, bp_in, part, piece, 6 + part).wait_send()
    other_ranks(lambda other: z_copy(other, other).wait_send())


def copy_out(*refs):
    count = len(refs) // 2
    sources, targets, sems = refs[:count], refs[count:-1], refs[-1]
    copies = [pltpu.make_async_copy(s, t, sems.at[i]) for i, (s, t) in enumerate(zip(sources, targets))]
    for copy in copies:
        copy.start()
    for copy in copies:
        copy.wait()


def body(chips, ranks, inputs, b_proj, c_proj, step_sizes, log_rate, forget, skip_gain, norm_gain, target):
    tokens, wide = inputs.shape
    heads = step_sizes.shape[1]
    half = heads // 2
    piece = half * 64 // chips
    vmem = pl.BlockSpec(memory_space=pltpu.VMEM)
    hbm = pl.BlockSpec(memory_space=pltpu.HBM)

    def buffer(*shape, dtype=F32):
        return pltpu.VMEM(shape, dtype)

    state = (heads, 128, 128)
    half_state = (half, 128, 128)
    operands = (
        inputs,
        target,
        b_proj.reshape(tokens, 128),
        c_proj.reshape(tokens, 128),
        step_sizes[0],
        forget[0],
        log_rate,
        skip_gain,
        norm_gain,
    )
    operands = tuple(pltpu.with_memory_space_constraint(operand, pltpu.HBM) for operand in operands)
    out_shape = (
        jax.ShapeDtypeStruct((tokens, wide), F32),
        jax.ShapeDtypeStruct((tokens, 128), F32),
        jax.ShapeDtypeStruct((tokens, 128), F32),
        jax.ShapeDtypeStruct((heads, tokens), F32),
    )
    results = pl.pallas_call(
        functools.partial(kernel, chips, ranks, float(wide * ranks)),
        out_shape=out_shape,
        in_specs=[hbm] * len(operands),
        out_specs=[vmem] * 4,
        scratch_shapes=[buffer(*operand.shape, dtype=operand.dtype) for operand in operands]
        + [
            buffer(3, heads, tokens),
            buffer(tokens, 128),
            buffer(heads, 128),
            buffer(heads, 128),
            buffer(tokens, tokens),
            buffer(tokens, wide),
            buffer(tokens, wide),
            buffer(tokens, wide),
            buffer(tokens, wide),
            buffer(tokens, wide),
            buffer(tokens, 256, dtype=BF16),
            buffer(tokens, 256, dtype=BF16),
            buffer(3, tokens, 128),
            buffer(tokens, 128),
            buffer(heads, 128),
            buffer(*state),
            buffer(*state),
            buffer(128, tokens, dtype=BF16),
            buffer(128, tokens, dtype=BF16),
            buffer(tokens, tokens),
            buffer(3, tokens, 128),
            buffer(heads, 136, 128),
            buffer(half, 136, 128),
            buffer(2, chips, piece + 8, 128),
            buffer(2, chips, piece + 8, 128),
            buffer(2, chips, piece, 128),
            buffer(2, chips, piece, 128),
            buffer(*half_state),
            buffer(*half_state),
            buffer(*state),
            buffer(*half_state),
            buffer(2, chips, piece, 128),
            buffer(2, chips, piece, 128),
            buffer(2, chips, piece, 128),
            buffer(2, chips, piece, 128),
            buffer(*half_state),
            buffer(*half_state),
            buffer(8, tokens),
            buffer(ranks, 8, tokens),
            pltpu.SemaphoreType.DMA((9,)),
            pltpu.SemaphoreType.DMA((8,)),
            pltpu.SemaphoreType.DMA((8,)),
            pltpu.SemaphoreType.DMA((8,)),
            pltpu.SemaphoreType.DMA((8,)),
            pltpu.SemaphoreType.DMA((ranks,)),
            pltpu.SemaphoreType.DMA((ranks,)),
        ],
        compiler_params=pltpu.CompilerParams(
            collective_id=0, has_side_effects=True, vmem_limit_bytes=24 * 1024 * 1024
        ),
        name="layer",
    )(*operands)
    grad_x, grad_b, grad_c, grad_steps = pl.pallas_call(
        copy_out,
        out_shape=out_shape,
        in_specs=[pl.BlockSpec(memory_space=pl.ANY)] * 4,
        out_specs=[hbm] * 4,
        scratch_shapes=[pltpu.SemaphoreType.DMA((4,))],
        compiler_params=pltpu.CompilerParams(vmem_limit_bytes=1024 * 1024),
        name="copy_out",
    )(*results)
    return (
        grad_x,
        grad_b.reshape(1, tokens, 1, 128),
        grad_c.reshape(1, tokens, 1, 128),
        grad_steps[None],
    )


def solution(mesh):
    chips, ranks = mesh.shape["ctx"] // 2, mesh.shape["head"]
    in_specs = (
        P("ctx", "head"),
        P(None, "ctx", "head", None),
        P(None, "ctx", "head", None),
        P(None, "head", "ctx"),
        P(None, "head"),
        P(None, "head", "ctx"),
        P(None, "head"),
        P(None, "head"),
        P("ctx", "head"),
    )
    out_specs = (
        P("ctx", "head"),
        P(None, "ctx", "head", None),
        P(None, "ctx", "head", None),
        P(None, "head", "ctx"),
    )
    return jax.shard_map(
        functools.partial(body, chips, ranks),
        mesh=mesh,
        in_specs=in_specs,
        out_specs=out_specs,
        check_vma=False,
    )
```

```python
import functools

import jax
import jax.numpy as jnp
from jax import lax
from jax.experimental import pallas as pl
from jax.experimental.pallas import tpu as pltpu
from jax.sharding import PartitionSpec as P

EPSILON = 1e-05
MESH = pl.DeviceIdType.MESH
F32 = jnp.float32
BF16 = jnp.bfloat16
NN = (((1,), (0,)), ((), ()))
NT = (((1,), (1,)), ((), ()))

CUM, EXPCUM, ENDW, ENDDEC, STEP = range(5)


def mm(left, right, dims=NN):
    return lax.dot_general(left, right, dims, preferred_element_type=F32)


def split2(value):
    high = value.astype(BF16)
    low = (value - high.astype(F32)).astype(BF16)
    return high, low


def split3(value):
    high = value.astype(BF16)
    rest = value - high.astype(F32)
    mid = rest.astype(BF16)
    low = (rest - mid.astype(F32)).astype(BF16)
    return high, mid, low


def mm3(left, right, dims=NN):
    (lh, ll), (rh, rl) = left, right
    return mm(lh, rh, dims) + (mm(lh, rl, dims) + mm(ll, rh, dims))


def kernel(
    chips,
    ranks,
    width,
    x_hbm,
    target_hbm,
    b_hbm,
    c_hbm,
    step_hbm,
    forget_hbm,
    rate_hbm,
    skip_hbm,
    gain_hbm,
    gx_ref,
    gb_ref,
    gc_ref,
    rows_ref,
    rq_ref,
    ext_ref,
    x_ref,
    target_ref,
    b_ref,
    c_ref,
    step_ref,
    forget_ref,
    rate_ref,
    skip_ref,
    gain_ref,
    cols_ref,
    ends_ref,
    skips_ref,
    scores_ref,
    mixed_ref,
    gm_ref,
    u_ref,
    expb_ref,
    endwb_ref,
    cc_ref,
    bb_ref,
    scale_ref,
    sin_ref,
    gout_ref,
    btr_ref,
    ctr_ref,
    dst_ref,
    sum_ref,
    fl_own,
    fl_got,
    fm_out,
    fm_in,
    fp_out,
    fp_in,
    fs_out,
    bl_own,
    bl_got,
    bm_out,
    bm_in,
    bp_out,
    bp_in,
    bs_out,
    z_out,
    z_in,
    load_sem,
    pair_send,
    pair_recv,
    ring_send,
    ring_recv,
    z_send,
    z_recv,
):
    tokens = x_ref.shape[0]
    heads = step_ref.shape[0]
    half = heads // 2
    chan = x_ref.shape[1] // heads
    parts, pair = 2, half // 2
    piece = pair * 128 // chips
    per_head = chips // pair
    ctx = lax.axis_index("ctx")
    rank = lax.axis_index("head")
    chip, core = lax.div(ctx, 2), lax.rem(ctx, 2)
    sibling = (chip * 2 + 1 - core, rank)
    lines = chips // 4
    line, place = lax.div(chip, 4), lax.rem(chip, 4)

    def loop(low, high, step):
        def turn(i, carry):
            step(i)
            return carry

        lax.fori_loop(low, high, turn, 0)

    def other_chips(act):
        columns = [lax.rem(place + along, 4) for along in (2, 1, 3, 0)]

        def on_line(q, count):
            down = lines // 2 + (1 - 2 * lax.rem(q, 2)) * lax.div(q + 1, 2)
            base = lax.rem(line + down, lines) * 4
            for column in columns[:count]:
                act(base + column)

        if lines > 1:
            loop(0, lines - 1, lambda q: on_line(q, 4))
        on_line(jnp.int32(lines - 1), 3)

    def other_ranks(act):
        for away in sorted(range(1, ranks), key=lambda k: -min(k, ranks - k)):
            act(lax.rem(rank + away, ranks))

    barrier = pltpu.get_barrier_semaphore()

    def greet(device):
        pl.semaphore_signal(barrier, inc=1, device_id=device, device_id_type=MESH)

    other_chips(lambda other: greet((other * 2 + core, rank)))
    other_ranks(lambda other: greet((ctx, other)))
    greet(sibling)

    loads = [
        pltpu.make_async_copy(source, target, load_sem.at[i])
        for i, (source, target) in enumerate(
            (
                (step_hbm, step_ref),
                (forget_hbm, forget_ref),
                (rate_hbm, rate_ref),
                (b_hbm, b_ref),
                (x_hbm, x_ref),
                (c_hbm, c_ref),
                (skip_hbm, skip_ref),
                (gain_hbm, gain_ref),
                (target_hbm, target_ref),
            )
        )
    ]
    for load in loads:
        load.start()

    down_iota = lax.broadcasted_iota(jnp.int32, (tokens, tokens), 0)
    along_iota = lax.broadcasted_iota(jnp.int32, (tokens, tokens), 1)
    diagonal = down_iota[0:heads, 0:heads] == along_iota[0:heads, 0:heads]

    def as_column(row):
        return jnp.sum(jnp.where(diagonal, row, 0.0), axis=1, keepdims=True)

    for load in loads[0:3]:
        load.wait()
    rate = jnp.exp(as_column(rate_ref[...]))
    step = step_ref[...]
    logdec = -step * rate - forget_ref[...]
    upper = (down_iota <= along_iota).astype(F32).astype(BF16)
    high, mid, low = split3(logdec)
    cum = mm(high, upper) + (mm(mid, upper) + mm(low, upper))
    last = cum[:, tokens - 1 : tokens]
    expcum = jnp.exp(cum)
    enddec = jnp.exp(last - cum)
    table = [cum, expcum, enddec * step, enddec, step]
    rows_ref[0] = cum
    rows_ref[1] = step
    rows_ref[2] = enddec
    rows_ref[3] = jnp.broadcast_to(rate, (heads, tokens))
    ends_ref[...] = jnp.broadcast_to(jnp.exp(last), (heads, 128))
    table = jnp.concatenate(table + [jnp.zeros((128 - heads * len(table), tokens), F32)], axis=0)
    cols_ref[...] = table.T
    loads[3].wait()
    btr_ref[...] = b_ref[...].astype(F32).T.astype(BF16)
    loads[4].wait()

    def columns_of(h, count=1):
        rolled = pltpu.roll(cols_ref[...], lax.rem(128 - h, 128), 1)
        each = [[rolled[:, 8 * q + k : 8 * q + k + 1] for q in range(5)] for k in range(count)]
        return each if count > 1 else each[0]

    def channels(h):
        return pl.ds(pl.multiple_of(h * chan, chan), chan)

    def cum_row(h):
        return rows_ref[0, pl.ds(h, 1), :]

    def step_row(h):
        return rows_ref[1, pl.ds(h, 1), :]

    def decay_of(h):
        return ends_ref[pl.ds(h, 1), :]

    def skip_of(h):
        return skips_ref[pl.ds(h, 1), :]

    def two(make):
        return jnp.concatenate([make(0), make(1)], axis=1)

    def local_state(h):
        columns = columns_of(h, 2)
        weighted = two(lambda k: x_ref[:, channels(h + k)].astype(F32) * columns[k][ENDW])
        high, low = split2(weighted)
        state = mm(btr_ref[...], high) + mm(btr_ref[...], low)
        for k in range(2):
            fl_own[h + k, 0:128, :] = state[:, k * 128 : k * 128 + 128]
            fl_own[h + k, 128:136, :] = jnp.broadcast_to(decay_of(h + k), (8, 128))

    def to_sibling(source, target, sem):
        return pltpu.make_async_remote_copy(
            src_ref=source,
            dst_ref=target,
            send_sem=pair_send.at[sem],
            recv_sem=pair_recv.at[sem],
            device_id=sibling,
            device_id_type=MESH,
        )

    mine, theirs = core * half, (1 - core) * half

    def swap_of(own, got, part, sem):
        return to_sibling(own.at[pl.ds(theirs + part * pair, pair)], got.at[pl.ds(part * pair, pair)], sem)

    def heads_of(base, part, act):
        act(base + part * pair)

    def ring_start(source, target, part, rows_sent, sem):
        def start(other):
            pltpu.make_async_remote_copy(
                src_ref=source.at[part, other, 0:rows_sent],
                dst_ref=target.at[part, chip, 0:rows_sent],
                send_sem=ring_send.at[sem],
                recv_sem=ring_recv.at[sem],
                device_id=(other * 2 + core, rank),
                device_id_type=MESH,
            ).start()

        other_chips(start)
        target[part, chip, 0:rows_sent, :] = source[part, chip, 0:rows_sent, :]

    def ring_all(source, target, part, rows_sent, sem):
        return pltpu.make_async_remote_copy(
            src_ref=source.at[part, 0 : chips - 1, 0:rows_sent],
            dst_ref=target.at[part, 0 : chips - 1, 0:rows_sent],
            send_sem=ring_send.at[sem],
            recv_sem=ring_recv.at[sem],
            device_id=sibling,
            device_id_type=MESH,
        )

    def pair_of(own, got, i):
        own_rows, got_rows = own[mine + i, 0:128, :], got[i, 0:128, :]
        first = jnp.where(core == 0, own_rows, got_rows)
        second = jnp.where(core == 0, got_rows, own_rows)
        return first, second

    def decay_pair(i):
        own_decay, got_decay = fl_own[mine + i, 128:129, :], fl_got[i, 128:129, :]
        first = jnp.where(core == 0, own_decay, got_decay)
        second = jnp.where(core == 0, got_decay, own_decay)
        return first, second

    def owners_of(part, i):
        return part, pl.ds(i * per_head, per_head), pl.ds(0, piece)

    def join_forward(part):
        for i in range(pair):
            first, second = pair_of(fl_own, fl_got, part * pair + i)
            decay0, decay1 = decay_pair(part * pair + i)
            joined = decay1 * first + second
            fm_out[owners_of(part, i)] = joined.reshape(per_head, piece, 128)
            fm_out[part, pl.ds(i * per_head, per_head), pl.ds(piece, 8)] = jnp.broadcast_to(
                (decay0 * decay1)[None], (per_head, 8, 128)
            )

    loop(0, half, lambda i: local_state(2 * i))
    pl.semaphore_wait(barrier, (chips - 1) + (ranks - 1) + 1)
    for part in range(parts):
        swap_of(fl_own, fl_got, part, part).start()

    def first_round(part):
        swap_of(fl_own, fl_got, part, part).wait_recv()
        join_forward(part)
        ring_start(fm_out, fm_in, part, piece + 1, part)

    loop(0, parts, first_round)

    for load in loads[5:]:
        load.wait()
    skips_ref[...] = jnp.broadcast_to(as_column(skip_ref[...]), (heads, 128))
    ctr_ref[...] = c_ref[...].astype(F32).T.astype(BF16)
    scores_ref[...] = mm(c_ref[...], b_ref[...], NT)
    cc_ref[...] = jnp.concatenate([c_ref[...], c_ref[...]], axis=1)
    bb_ref[...] = jnp.concatenate([b_ref[...], b_ref[...]], axis=1)

    def near(h):
        cols = columns_of(h)
        gap = jnp.where(down_iota >= along_iota, cols[CUM] - cum_row(h), -1e30)
        weights = scores_ref[...] * jnp.exp(gap) * step_row(h)
        high, low = split2(weights)
        x_h = x_ref[:, channels(h)]
        wide_x = x_h.astype(F32)
        mixed_ref[:, channels(h)] = mm(high, x_h) + mm(low, x_h) + skip_of(h) * wide_x
        u_ref[:, channels(h)] = gain_ref[:, channels(h)] * (wide_x - target_ref[:, channels(h)].astype(F32))
        expb_ref[:, channels(h)] = jnp.broadcast_to(cols[EXPCUM], (tokens, 128))
        endwb_ref[:, channels(h)] = jnp.broadcast_to(cols[ENDW], (tokens, 128))

    loop(0, heads, near)
    sum_ref[...] = jnp.zeros_like(sum_ref)

    def scan_forward(part):
        ring_all(fm_out, fm_in, part, piece + 1, part).wait_recv()
        state = jnp.zeros((piece, 128), F32)
        for t in range(chips):
            fp_out[part, t] = state
            state = fm_in[part, t, piece : piece + 1, :] * state + fm_in[part, t, 0:piece, :]
        ring_start(fp_out, fp_in, part, piece, 2 + part)

    loop(0, parts, scan_forward)

    def enter(part):
        for i in range(pair):
            at = part * pair + i
            first, _ = pair_of(fl_own, fl_got, at)
            decay0, _ = decay_pair(at)
            for_first = fp_in[owners_of(part, i)].reshape(128, 128)
            for_second = decay0 * for_first + first
            sin_ref[mine + at] = jnp.where(core == 0, for_first, for_second)
            fs_out[at] = jnp.where(core == 0, for_second, for_first)

    def both(own, got, part, sem):
        return to_sibling(own.at[pl.ds(part * pair, pair)], got.at[pl.ds(mine + part * pair, pair)], sem)

    def stacked(ref, h):
        high, low = split2(two(lambda k: ref[h + k]))
        return jnp.concatenate([high, low], axis=0)

    def far(h):
        reached = mm(cc_ref[...], stacked(sin_ref, h))
        sums = [0.0, 0.0, 0.0]
        for k in range(2):
            here = channels(h + k)
            mixed = mixed_ref[:, here] + expb_ref[:, here] * reached[:, k * 128 : k * 128 + 128]
            mixed_ref[:, here] = mixed
            gained = gain_ref[:, here] * mixed
            sums = [sums[0] + mixed * mixed, sums[1] + u_ref[:, here] * mixed, sums[2] + gained * gained]
        for i in range(3):
            sum_ref[i] += sums[i]

    def far_mine(part):
        ring_all(fp_out, fp_in, part, piece, 2 + part).wait_recv()
        enter(part)
        both(fs_out, sin_ref, part, 2 + part).start()
        heads_of(mine, part, far)

    def far_theirs(part):
        both(fs_out, sin_ref, part, 2 + part).wait_recv()
        heads_of(theirs, part, far)

    loop(0, parts, far_mine)
    loop(0, parts, far_theirs)

    lane = lax.broadcasted_iota(jnp.int32, (tokens, 128), 1)
    row_iota = lax.broadcasted_iota(jnp.int32, (8, 256), 0)
    sums = jnp.zeros((8, tokens), F32)
    for i in range(3):
        ones = (row_iota == i).astype(F32).astype(BF16)
        sums = sums + mm(ones, jnp.concatenate(split2(sum_ref[i]), axis=1), NT)
    z_out[...] = sums

    def z_copy(to, slot):
        return pltpu.make_async_remote_copy(
            src_ref=z_out,
            dst_ref=z_in.at[slot],
            send_sem=z_send.at[to],
            recv_sem=z_recv.at[slot],
            device_id=(ctx, to),
            device_id_type=MESH,
        )

    other_ranks(lambda other: z_copy(other, rank).start())
    z_in[rank] = z_out[...]
    other_ranks(lambda other: z_copy(other, other).wait_recv())
    total = z_in[0]
    for i in range(1, ranks):
        total = total + z_in[i]
    inv_scale = lax.rsqrt(total[0:1, :] / width + EPSILON)
    inner = total[1:2, :] + inv_scale * total[2:3, :]
    coef = inner * inv_scale * inv_scale * inv_scale / width
    back = jnp.concatenate([inv_scale, coef, jnp.zeros((126, tokens), F32)], axis=0).T
    inv_col = jnp.broadcast_to(back[:, 0:1], (tokens, 128))
    scale_ref[0] = inv_col
    scale_ref[1] = inv_col * inv_col
    scale_ref[2] = jnp.broadcast_to(back[:, 1:2], (tokens, 128))

    def norm_back(h):
        def weighted(k):
            here = channels(h + k)
            gain = gain_ref[:, here]
            factor = (gain * gain) * scale_ref[1] - scale_ref[2]
            grad_mixed = u_ref[:, here] * scale_ref[0] + mixed_ref[:, here] * factor
            gm_ref[:, here] = grad_mixed
            return grad_mixed * expb_ref[:, here]

        high, low = split2(two(weighted))
        state = mm(ctr_ref[...], high) + mm(ctr_ref[...], low)
        for k in range(2):
            bl_own[h + k] = state[:, k * 128 : k * 128 + 128]

    def join_back(part):
        for i in range(pair):
            first, second = pair_of(bl_own, bl_got, part * pair + i)
            decay0, _ = decay_pair(part * pair + i)
            bm_out[owners_of(part, i)] = (decay0 * second + first).reshape(per_head, piece, 128)

    def back_theirs(part):
        heads_of(theirs, part, norm_back)
        swap_of(bl_own, bl_got, part, 4 + part).start()

    def back_mine(part):
        heads_of(mine, part, norm_back)
        swap_of(bl_own, bl_got, part, 4 + part).wait_recv()
        join_back(part)
        ring_start(bm_out, bm_in, part, piece, 4 + part)

    loop(0, parts, back_theirs)
    loop(0, parts, back_mine)

    rq_ref[...] = jnp.zeros_like(rq_ref)
    gc_ref[...] = jnp.zeros_like(gc_ref)
    gb_ref[...] = jnp.zeros_like(gb_ref)
    dst_ref[...] = jnp.zeros_like(dst_ref)
    scores_ref[...] = mm(b_ref[...], c_ref[...], NT)

    def near_back(h):
        cols = columns_of(h)
        here = channels(h)
        gap = jnp.where(along_iota >= down_iota, cum_row(h) - cols[CUM], -1e30)
        decay = jnp.exp(gap)
        grad_mixed = gm_ref[:, here]
        gm_parts = split2(grad_mixed)
        x_h = x_ref[:, here]
        wide_x = x_h.astype(F32)
        mixed = mixed_ref[:, here]
        value = mm3(split2(scores_ref[...] * decay), gm_parts)
        grad_out = wide_x + gain_ref[:, here] * mixed * scale_ref[0] - target_ref[:, here].astype(F32)
        gx_ref[:, here] = grad_out + skip_of(h) * grad_mixed + cols[STEP] * value
        grad_weights = mm(x_h, gm_parts[0], NT) + mm(x_h, gm_parts[1], NT)
        dst_ref[...] += grad_weights * decay * cols[STEP]
        row_sum = jnp.sum(grad_mixed * (mixed - skip_of(h) * wide_x), axis=1, keepdims=True)
        column_sum = jnp.sum(wide_x * value, axis=1, keepdims=True)
        rq_ref[...] = jnp.where(lane == h, row_sum, jnp.where(lane == h + 8, column_sum, rq_ref[...]))
        gc_ref[...] += mm3(split2(grad_mixed * expb_ref[:, here]), split2(sin_ref[h]), NT)

    loop(0, heads, near_back)
    grad_scores = dst_ref[...]
    high, low = split2(grad_scores)
    gb_ref[...] += mm(high, c_ref[...]) + mm(low, c_ref[...])
    high, low = split2(grad_scores.T)
    gc_ref[...] += mm(high, b_ref[...]) + mm(low, b_ref[...])

    def scan_back(part):
        ring_all(bm_out, bm_in, part, piece, 4 + part).wait_recv()
        grad = jnp.zeros((piece, 128), F32)
        for t in reversed(range(chips)):
            bp_out[part, t] = grad
            grad = fm_in[part, t, piece : piece + 1, :] * grad + bm_in[part, t]
        ring_start(bp_out, bp_in, part, piece, 6 + part)

    loop(0, parts, scan_back)

    def leave(part):
        for i in range(pair):
            at = part * pair + i
            _, second = pair_of(bl_own, bl_got, at)
            _, decay1 = decay_pair(at)
            for_second = bp_in[owners_of(part, i)].reshape(128, 128)
            for_first = decay1 * for_second + second
            gout_ref[mine + at] = jnp.where(core == 0, for_first, for_second)
            bs_out[at] = jnp.where(core == 0, for_second, for_first)

    def far_back(h):
        both_parts = stacked(gout_ref, h)
        reached = mm(bb_ref[...], both_parts)
        table = rq_ref[...]
        grad_b = gb_ref[...]
        for k in range(2):
            here = channels(h + k)
            at = slice(k * 128, k * 128 + 128)
            x_h = x_ref[:, here]
            weight = endwb_ref[:, here]
            gx_ref[:, here] += weight * reached[:, at]
            row_sum = jnp.sum(x_h.astype(F32) * reached[:, at], axis=1, keepdims=True)
            table = jnp.where(lane == h + k + 16, row_sum, table)
            parts_along = jnp.concatenate([both_parts[0:128, at], both_parts[128:256, at]], axis=1)
            grad_b = grad_b + weight * mm(jnp.concatenate([x_h, x_h], axis=1), parts_along, NT)
            leaving = decay_of(h + k) * sin_ref[h + k] + fl_own[h + k, 0:128, :]
            ext_ref[pl.ds(h + k, 1), :] = jnp.sum(gout_ref[h + k] * leaving, axis=0, keepdims=True)
        rq_ref[...] = table
        gb_ref[...] = grad_b

    def last_mine(part):
        ring_all(bp_out, bp_in, part, piece, 6 + part).wait_recv()
        leave(part)
        both(bs_out, gout_ref, part, 6 + part).start()
        heads_of(mine, part, far_back)

    def last_theirs(part):
        both(bs_out, gout_ref, part, 6 + part).wait_recv()
        heads_of(theirs, part, far_back)

    loop(0, parts, last_mine)
    loop(0, parts, last_theirs)

    for part in range(parts):
        swap_of(fl_own, fl_got, part, part).wait_send()
        both(fs_out, sin_ref, part, 2 + part).wait_send()
        swap_of(bl_own, bl_got, part, 4 + part).wait_send()
        both(bs_out, gout_ref, part, 6 + part).wait_send()
        ring_all(fm_out, fm_in, part, piece + 1, part).wait_send()
        ring_all(fp_out, fp_in, part, piece, 2 + part).wait_send()
        ring_all(bm_out, bm_in, part, piece, 4 + part).wait_send()
        ring_all(bp_out, bp_in, part, piece, 6 + part).wait_send()
    other_ranks(lambda other: z_copy(other, other).wait_send())


def finish(gx_in, gb_in, gc_in, rows_ref, rq_ref, ext_ref, gx_ref, gb_ref, gc_ref, gs_ref, sums_ref, sems):
    pairs = ((gx_in, gx_ref), (gb_in, gb_ref), (gc_in, gc_ref))
    copies = [pltpu.make_async_copy(source, target, sems.at[i]) for i, (source, target) in enumerate(pairs)]
    for copy in copies:
        copy.start()
    heads, tokens = sums_ref.shape
    step, enddec, rate = rows_ref[1], rows_ref[2], rows_ref[3]
    ends = rq_ref[...].T
    inner_x = ends[8 : 8 + heads, :] + enddec * ends[16 : 16 + heads, :]
    extra = jnp.sum(ext_ref[...], axis=1, keepdims=True)
    down_iota = lax.broadcasted_iota(jnp.int32, (tokens, tokens), 0)
    along_iota = lax.broadcasted_iota(jnp.int32, (tokens, tokens), 1)
    lower = (down_iota >= along_iota).astype(F32).astype(BF16)
    high, mid, low = split3(ends[0:heads, :] - step * inner_x)
    grad_dec = mm(high, lower) + (mm(mid, lower) + mm(low, lower)) + extra
    sums_ref[...] = inner_x - rate * grad_dec
    last = pltpu.make_async_copy(sums_ref, gs_ref, sems.at[3])
    last.start()
    for copy in copies:
        copy.wait()
    last.wait()


def body(chips, ranks, inputs, b_proj, c_proj, step_sizes, log_rate, forget, skip_gain, norm_gain, target):
    tokens, wide = inputs.shape
    heads = step_sizes.shape[1]
    half = heads // 2
    piece = half * 64 // chips
    vmem = pl.BlockSpec(memory_space=pltpu.VMEM)
    hbm = pl.BlockSpec(memory_space=pltpu.HBM)

    def buffer(*shape, dtype=F32):
        return pltpu.VMEM(shape, dtype)

    state = (heads, 128, 128)
    half_state = (half, 128, 128)
    operands = (
        inputs,
        target,
        b_proj.reshape(tokens, 128),
        c_proj.reshape(tokens, 128),
        step_sizes[0],
        forget[0],
        log_rate,
        skip_gain,
        norm_gain,
    )
    operands = tuple(pltpu.with_memory_space_constraint(operand, pltpu.HBM) for operand in operands)
    out_shape = (
        jax.ShapeDtypeStruct((tokens, wide), F32),
        jax.ShapeDtypeStruct((tokens, 128), F32),
        jax.ShapeDtypeStruct((tokens, 128), F32),
        jax.ShapeDtypeStruct((heads, tokens), F32),
    )
    results = pl.pallas_call(
        functools.partial(kernel, chips, ranks, float(wide * ranks)),
        out_shape=out_shape[0:3]
        + (
            jax.ShapeDtypeStruct((4, heads, tokens), F32),
            jax.ShapeDtypeStruct((tokens, 128), F32),
            jax.ShapeDtypeStruct((heads, 128), F32),
        ),
        in_specs=[hbm] * len(operands),
        out_specs=[vmem] * 6,
        scratch_shapes=[buffer(*operand.shape, dtype=operand.dtype) for operand in operands]
        + [
            buffer(tokens, 128),
            buffer(heads, 128),
            buffer(heads, 128),
            buffer(tokens, tokens),
            buffer(tokens, wide),
            buffer(tokens, wide),
            buffer(tokens, wide),
            buffer(tokens, wide),
            buffer(tokens, wide),
            buffer(tokens, 256, dtype=BF16),
            buffer(tokens, 256, dtype=BF16),
            buffer(3, tokens, 128),
            buffer(*state),
            buffer(*state),
            buffer(128, tokens, dtype=BF16),
            buffer(128, tokens, dtype=BF16),
            buffer(tokens, tokens),
            buffer(3, tokens, 128),
            buffer(heads, 136, 128),
            buffer(half, 136, 128),
            buffer(2, chips, piece + 8, 128),
            buffer(2, chips, piece + 8, 128),
            buffer(2, chips, piece, 128),
            buffer(2, chips, piece, 128),
            buffer(*half_state),
            buffer(*state),
            buffer(*half_state),
            buffer(2, chips, piece, 128),
            buffer(2, chips, piece, 128),
            buffer(2, chips, piece, 128),
            buffer(2, chips, piece, 128),
            buffer(*half_state),
            buffer(8, tokens),
            buffer(ranks, 8, tokens),
            pltpu.SemaphoreType.DMA((9,)),
            pltpu.SemaphoreType.DMA((8,)),
            pltpu.SemaphoreType.DMA((8,)),
            pltpu.SemaphoreType.DMA((8,)),
            pltpu.SemaphoreType.DMA((8,)),
            pltpu.SemaphoreType.DMA((ranks,)),
            pltpu.SemaphoreType.DMA((ranks,)),
        ],
        compiler_params=pltpu.CompilerParams(
            collective_id=0, has_side_effects=True, vmem_limit_bytes=24 * 1024 * 1024
        ),
        name="layer",
    )(*operands)
    grad_x, grad_b, grad_c, grad_steps = pl.pallas_call(
        finish,
        out_shape=out_shape,
        in_specs=[pl.BlockSpec(memory_space=pl.ANY)] * 3 + [vmem] * 3,
        out_specs=[hbm] * 4,
        scratch_shapes=[buffer(heads, tokens), pltpu.SemaphoreType.DMA((4,))],
        compiler_params=pltpu.CompilerParams(vmem_limit_bytes=4 * 1024 * 1024),
        name="finish",
    )(*results)
    return (
        grad_x,
        grad_b.reshape(1, tokens, 1, 128),
        grad_c.reshape(1, tokens, 1, 128),
        grad_steps[None],
    )


def solution(mesh):
    chips, ranks = mesh.shape["ctx"] // 2, mesh.shape["head"]
    in_specs = (
        P("ctx", "head"),
        P(None, "ctx", "head", None),
        P(None, "ctx", "head", None),
        P(None, "head", "ctx"),
        P(None, "head"),
        P(None, "head", "ctx"),
        P(None, "head"),
        P(None, "head"),
        P("ctx", "head"),
    )
    out_specs = (
        P("ctx", "head"),
        P(None, "ctx", "head", None),
        P(None, "ctx", "head", None),
        P(None, "head", "ctx"),
    )
    return jax.shard_map(
        functools.partial(body, chips, ranks),
        mesh=mesh,
        in_specs=in_specs,
        out_specs=out_specs,
        check_vma=False,
    )
```

```python
import functools

import jax
import jax.numpy as jnp
from jax import lax
from jax.experimental import pallas as pl
from jax.experimental.pallas import tpu as pltpu
from jax.sharding import PartitionSpec as P

EPSILON = 1e-05
MESH = pl.DeviceIdType.MESH
F32 = jnp.float32
BF16 = jnp.bfloat16
NN = (((1,), (0,)), ((), ()))
NT = (((1,), (1,)), ((), ()))

CUM, EXPCUM, ENDW, ENDDEC, STEP = range(5)


def mm(left, right, dims=NN):
    return lax.dot_general(left, right, dims, preferred_element_type=F32)


def split2(value):
    high = value.astype(BF16)
    low = (value - high.astype(F32)).astype(BF16)
    return high, low


def split3(value):
    high = value.astype(BF16)
    rest = value - high.astype(F32)
    mid = rest.astype(BF16)
    low = (rest - mid.astype(F32)).astype(BF16)
    return high, mid, low


def mm3(left, right, dims=NN):
    (lh, ll), (rh, rl) = left, right
    return mm(lh, rh, dims) + (mm(lh, rl, dims) + mm(ll, rh, dims))


def kernel(
    chips,
    ranks,
    width,
    x_hbm,
    target_hbm,
    b_hbm,
    c_hbm,
    step_hbm,
    forget_hbm,
    rate_hbm,
    skip_hbm,
    gain_hbm,
    gx_ref,
    gb_ref,
    gc_ref,
    rows_ref,
    rq_ref,
    ext_ref,
    x_ref,
    target_ref,
    b_ref,
    c_ref,
    step_ref,
    forget_ref,
    rate_ref,
    skip_ref,
    gain_ref,
    cols_ref,
    ends_ref,
    skips_ref,
    scores_ref,
    mixed_ref,
    u_ref,
    expb_ref,
    endwb_ref,
    cc_ref,
    bb_ref,
    scale_ref,
    sin_ref,
    gout_ref,
    btr_ref,
    ctr_ref,
    dst_ref,
    sum_ref,
    fl_own,
    fl_got,
    fm_out,
    fm_in,
    fp_out,
    fp_in,
    fs_out,
    bl_second,
    su_ref,
    sm_ref,
    se_ref,
    sc_ref,
    cf_ref,
    sct_ref,
    bm_out,
    bm_in,
    bp_out,
    bp_in,
    bs_out,
    z_out,
    z_in,
    load_sem,
    pair_send,
    pair_recv,
    ring_send,
    ring_recv,
    z_send,
    z_recv,
):
    tokens = x_ref.shape[0]
    heads = step_ref.shape[0]
    half = heads // 2
    chan = x_ref.shape[1] // heads
    parts, pair = 2, half // 2
    piece = pair * 128 // chips
    per_head = chips // pair
    ctx = lax.axis_index("ctx")
    rank = lax.axis_index("head")
    chip, core = lax.div(ctx, 2), lax.rem(ctx, 2)
    twin = chip * 2 + 1 - core
    sibling = (twin, rank)
    lines = chips // 4
    line, place = lax.div(chip, 4), lax.rem(chip, 4)

    def loop(low, high, step):
        def turn(i, carry):
            step(i)
            return carry

        lax.fori_loop(low, high, turn, 0)

    lines_from = [lax.rem(line + down, lines) * 4 for down in range(lines)]
    columns_from = [lax.rem(place + along, 4) for along in range(4)]
    offsets = [(down, along) for down in range(lines) for along in range(4)][1:]
    offsets.sort(key=lambda o: -(min(o[0], lines - o[0]) + min(o[1], 4 - o[1])))

    def other_chips(act):
        for down, along in offsets:
            act(lines_from[down] + columns_from[along])

    def other_ranks(act):
        for away in sorted(range(1, ranks), key=lambda k: -min(k, ranks - k)):
            act(lax.rem(rank + away, ranks))

    barrier = pltpu.get_barrier_semaphore()

    def greet(device):
        pl.semaphore_signal(barrier, inc=1, device_id=device, device_id_type=MESH)

    other_chips(lambda other: greet((other * 2 + core, rank)))
    other_ranks(lambda other: greet((ctx, other)))
    other_ranks(lambda other: greet((twin, other)))
    greet(sibling)

    loads = [
        pltpu.make_async_copy(source, target, load_sem.at[i])
        for i, (source, target) in enumerate(
            (
                (step_hbm, step_ref),
                (forget_hbm, forget_ref),
                (rate_hbm, rate_ref),
                (b_hbm, b_ref),
                (x_hbm, x_ref),
                (c_hbm, c_ref),
                (skip_hbm, skip_ref),
                (gain_hbm, gain_ref),
                (target_hbm, target_ref),
            )
        )
    ]
    for load in loads:
        load.start()

    down_iota = lax.broadcasted_iota(jnp.int32, (tokens, tokens), 0)
    along_iota = lax.broadcasted_iota(jnp.int32, (tokens, tokens), 1)
    diagonal = down_iota[0:heads, 0:heads] == along_iota[0:heads, 0:heads]

    def as_column(row):
        return jnp.sum(jnp.where(diagonal, row, 0.0), axis=1, keepdims=True)

    for load in loads[0:3]:
        load.wait()
    rate = jnp.exp(as_column(rate_ref[...]))
    step = step_ref[...]
    logdec = -step * rate - forget_ref[...]
    upper = (down_iota <= along_iota).astype(F32).astype(BF16)
    high, mid, low = split3(logdec)
    cum = mm(high, upper) + (mm(mid, upper) + mm(low, upper))
    last = cum[:, tokens - 1 : tokens]
    expcum = jnp.exp(cum)
    enddec = jnp.exp(last - cum)
    table = [cum, expcum, enddec * step, enddec, step]
    rows_ref[0] = cum
    rows_ref[1] = step
    rows_ref[2] = enddec
    rows_ref[3] = jnp.broadcast_to(rate, (heads, tokens))
    ends_ref[...] = jnp.broadcast_to(jnp.exp(last), (heads, 128))
    table = jnp.concatenate(table + [jnp.zeros((128 - heads * len(table), tokens), F32)], axis=0)
    cols_ref[...] = table.T
    loads[3].wait()
    btr_ref[...] = b_ref[...].astype(F32).T.astype(BF16)
    loads[4].wait()

    def columns_of(h, count=1):
        rolled = pltpu.roll(cols_ref[...], lax.rem(128 - h, 128), 1)
        each = [[rolled[:, 8 * q + k : 8 * q + k + 1] for q in range(5)] for k in range(count)]
        return each if count > 1 else each[0]

    def channels(h):
        return pl.ds(pl.multiple_of(h * chan, chan), chan)

    def cum_row(h):
        return rows_ref[0, pl.ds(h, 1), :]

    def step_row(h):
        return rows_ref[1, pl.ds(h, 1), :]

    def decay_of(h):
        return ends_ref[pl.ds(h, 1), :]

    def skip_of(h):
        return skips_ref[pl.ds(h, 1), :]

    def two(make):
        return jnp.concatenate([make(0), make(1)], axis=1)

    def local_state(h):
        columns = columns_of(h, 2)
        weighted = two(lambda k: x_ref[:, channels(h + k)].astype(F32) * columns[k][ENDW])
        high, low = split2(weighted)
        state = mm(btr_ref[...], high) + mm(btr_ref[...], low)
        for k in range(2):
            fl_own[h + k, 0:128, :] = state[:, k * 128 : k * 128 + 128]
            fl_own[h + k, 128:136, :] = jnp.broadcast_to(decay_of(h + k), (8, 128))

    def to_sibling(source, target, sem):
        return pltpu.make_async_remote_copy(
            src_ref=source,
            dst_ref=target,
            send_sem=pair_send.at[sem],
            recv_sem=pair_recv.at[sem],
            device_id=sibling,
            device_id_type=MESH,
        )

    mine, theirs = core * half, (1 - core) * half

    def swap_of(own, got, part, sem):
        return to_sibling(own.at[pl.ds(theirs + part * pair, pair)], got.at[pl.ds(part * pair, pair)], sem)

    def heads_of(base, part, act):
        act(base + part * pair)

    def ring_start(source, target, part, rows_sent, sem):
        def start(other):
            pltpu.make_async_remote_copy(
                src_ref=source.at[part, other, 0:rows_sent],
                dst_ref=target.at[part, chip, 0:rows_sent],
                send_sem=ring_send.at[sem],
                recv_sem=ring_recv.at[sem],
                device_id=(other * 2 + core, rank),
                device_id_type=MESH,
            ).start()

        other_chips(start)
        target[part, chip, 0:rows_sent, :] = source[part, chip, 0:rows_sent, :]

    def ring_all(source, target, part, rows_sent, sem):
        return pltpu.make_async_remote_copy(
            src_ref=source.at[part, 0 : chips - 1, 0:rows_sent],
            dst_ref=target.at[part, 0 : chips - 1, 0:rows_sent],
            send_sem=ring_send.at[sem],
            recv_sem=ring_recv.at[sem],
            device_id=sibling,
            device_id_type=MESH,
        )

    def pair_of(own, got, i):
        own_rows, got_rows = own[mine + i, 0:128, :], got[i, 0:128, :]
        first = jnp.where(core == 0, own_rows, got_rows)
        second = jnp.where(core == 0, got_rows, own_rows)
        return first, second

    def decay_pair(i):
        own_decay, got_decay = fl_own[mine + i, 128:129, :], fl_got[i, 128:129, :]
        first = jnp.where(core == 0, own_decay, got_decay)
        second = jnp.where(core == 0, got_decay, own_decay)
        return first, second

    def owners_of(part, i):
        return part, pl.ds(i * per_head, per_head), pl.ds(0, piece)

    def join_forward(part):
        for i in range(pair):
            first, second = pair_of(fl_own, fl_got, part * pair + i)
            decay0, decay1 = decay_pair(part * pair + i)
            joined = decay1 * first + second
            fm_out[owners_of(part, i)] = joined.reshape(per_head, piece, 128)
            fm_out[part, pl.ds(i * per_head, per_head), pl.ds(piece, 8)] = jnp.broadcast_to(
                (decay0 * decay1)[None], (per_head, 8, 128)
            )

    loop(0, half, lambda i: local_state(2 * i))
    pl.semaphore_wait(barrier, (chips - 1) + 2 * (ranks - 1) + 1)
    for part in range(parts):
        swap_of(fl_own, fl_got, part, part).start()

    def first_round(part):
        swap_of(fl_own, fl_got, part, part).wait_recv()
        join_forward(part)
        ring_start(fm_out, fm_in, part, piece + 1, part)

    loop(0, parts, first_round)

    for load in loads[5:]:
        load.wait()
    skips_ref[...] = jnp.broadcast_to(as_column(skip_ref[...]), (heads, 128))
    cf_ref[...] = c_ref[...].astype(F32).T
    ctr_ref[...] = cf_ref[...].astype(BF16)
    scores_ref[...] = mm(c_ref[...], b_ref[...], NT)
    cc_ref[...] = jnp.concatenate([c_ref[...], c_ref[...]], axis=1)
    bb_ref[...] = jnp.concatenate([b_ref[...], b_ref[...]], axis=1)

    def near(h):
        cols = columns_of(h)
        gap = jnp.where(down_iota >= along_iota, cols[CUM] - cum_row(h), -1e30)
        weights = scores_ref[...] * jnp.exp(gap) * step_row(h)
        high, low = split2(weights)
        x_h = x_ref[:, channels(h)]
        wide_x = x_h.astype(F32)
        mixed_ref[:, channels(h)] = mm(high, x_h) + mm(low, x_h) + skip_of(h) * wide_x
        u_ref[:, channels(h)] = gain_ref[:, channels(h)] * (wide_x - target_ref[:, channels(h)].astype(F32))
        expb_ref[:, channels(h)] = jnp.broadcast_to(cols[EXPCUM], (tokens, 128))
        endwb_ref[:, channels(h)] = jnp.broadcast_to(cols[ENDW], (tokens, 128))

    loop(0, heads, near)

    def channels_of(base, count):
        return pl.ds(pl.multiple_of(base * chan, chan), count * chan)

    def to_twin():
        return (
            to_sibling(u_ref.at[:, channels_of(theirs, half)], su_ref, 8),
            to_sibling(expb_ref.at[:, channels_of(theirs, half)], se_ref, 9),
            to_sibling(cf_ref, sc_ref, 10),
        )

    def mixed_to_twin(part):
        source = mixed_ref.at[:, channels_of(theirs + part * pair, pair)]
        return to_sibling(source, sm_ref.at[:, channels_of(part * pair, pair)], 4 + part)

    for copy in to_twin():
        copy.start()
    sum_ref[...] = jnp.zeros_like(sum_ref)

    def scan_forward(part):
        ring_all(fm_out, fm_in, part, piece + 1, part).wait_recv()
        state = jnp.zeros((piece, 128), F32)
        for t in range(chips):
            fp_out[part, t] = state
            state = fm_in[part, t, piece : piece + 1, :] * state + fm_in[part, t, 0:piece, :]
        ring_start(fp_out, fp_in, part, piece, 2 + part)

    loop(0, parts, scan_forward)

    def enter(part):
        for i in range(pair):
            at = part * pair + i
            first, _ = pair_of(fl_own, fl_got, at)
            decay0, _ = decay_pair(at)
            for_first = fp_in[owners_of(part, i)].reshape(128, 128)
            for_second = decay0 * for_first + first
            sin_ref[mine + at] = jnp.where(core == 0, for_first, for_second)
            fs_out[at] = jnp.where(core == 0, for_second, for_first)

    def both(own, got, part, sem):
        return to_sibling(own.at[pl.ds(part * pair, pair)], got.at[pl.ds(mine + part * pair, pair)], sem)

    def stacked(ref, h):
        high, low = split2(two(lambda k: ref[h + k]))
        return jnp.concatenate([high, low], axis=0)

    def far(h):
        reached = mm(cc_ref[...], stacked(sin_ref, h))
        sums = [0.0, 0.0, 0.0]
        for k in range(2):
            here = channels(h + k)
            mixed = mixed_ref[:, here] + expb_ref[:, here] * reached[:, k * 128 : k * 128 + 128]
            mixed_ref[:, here] = mixed
            gained = gain_ref[:, here] * mixed
            sums = [sums[0] + mixed * mixed, sums[1] + u_ref[:, here] * mixed, sums[2] + gained * gained]
        for i in range(3):
            sum_ref[i] += sums[i]

    def far_mine(part):
        ring_all(fp_out, fp_in, part, piece, 2 + part).wait_recv()
        enter(part)
        both(fs_out, sin_ref, part, 2 + part).start()
        heads_of(mine, part, far)

    def far_theirs(part):
        both(fs_out, sin_ref, part, 2 + part).wait_recv()
        heads_of(theirs, part, far)
        mixed_to_twin(part).start()

    loop(0, parts, far_mine)
    loop(0, parts, far_theirs)

    lane = lax.broadcasted_iota(jnp.int32, (tokens, 128), 1)
    row_iota = lax.broadcasted_iota(jnp.int32, (8, 256), 0)
    sums = jnp.zeros((8, tokens), F32)
    for i in range(3):
        ones = (row_iota == i).astype(F32).astype(BF16)
        sums = sums + mm(ones, jnp.concatenate(split2(sum_ref[i]), axis=1), NT)
    z_out[...] = sums

    def z_copy(block, to, slot):
        return pltpu.make_async_remote_copy(
            src_ref=z_out,
            dst_ref=z_in.at[block, slot],
            send_sem=z_send.at[block, to],
            recv_sem=z_recv.at[block, slot],
            device_id=(twin if block else ctx, to),
            device_id_type=MESH,
        )

    other_ranks(lambda other: z_copy(0, other, rank).start())
    other_ranks(lambda other: z_copy(1, other, rank).start())
    z_copy(1, rank, rank).start()
    z_in[0, rank] = z_out[...]
    for copy in to_twin():
        copy.wait_recv()
    sct_ref[...] = sc_ref[...].astype(BF16)
    z_copy(1, rank, rank).wait_recv()
    other_ranks(lambda other: z_copy(0, other, other).wait_recv())
    other_ranks(lambda other: z_copy(1, other, other).wait_recv())
    factors = []
    for block in range(2):
        total = z_in[block, 0]
        for i in range(1, ranks):
            total = total + z_in[block, i]
        inv_scale = lax.rsqrt(total[0:1, :] / width + EPSILON)
        inner = total[1:2, :] + inv_scale * total[2:3, :]
        factors += [inv_scale, inner * inv_scale * inv_scale * inv_scale / width]
    back = jnp.concatenate(factors + [jnp.zeros((124, tokens), F32)], axis=0).T
    for block in range(2):
        inv_col = jnp.broadcast_to(back[:, 2 * block : 2 * block + 1], (tokens, 128))
        scale_ref[3 * block] = inv_col
        scale_ref[3 * block + 1] = inv_col * inv_col
        scale_ref[3 * block + 2] = jnp.broadcast_to(back[:, 2 * block + 1 : 2 * block + 2], (tokens, 128))

    def norm_grad(gained, mixed, gain, block):
        factor = (gain * gain) * scale_ref[3 * block + 1] - scale_ref[3 * block + 2]
        return gained * scale_ref[3 * block] + mixed * factor

    def back_round(part):
        mixed_to_twin(part).wait_recv()

        def own(k):
            here = channels(mine + part * pair + k)
            grad_mixed = norm_grad(u_ref[:, here], mixed_ref[:, here], gain_ref[:, here], 0)
            return grad_mixed * expb_ref[:, here]

        def others(k):
            at = channels(part * pair + k)
            gain = gain_ref[:, channels(mine + part * pair + k)]
            return norm_grad(su_ref[:, at], sm_ref[:, at], gain, 1) * se_ref[:, at]

        high, low = split2(two(own))
        own_state = mm(ctr_ref[...], high) + mm(ctr_ref[...], low)
        high, low = split2(two(others))
        got_state = mm(sct_ref[...], high) + mm(sct_ref[...], low)
        first = jnp.where(core == 0, own_state, got_state)
        second = jnp.where(core == 0, got_state, own_state)
        for i in range(pair):
            at = slice(i * 128, i * 128 + 128)
            decay0, _ = decay_pair(part * pair + i)
            bl_second[part * pair + i] = second[:, at]
            bm_out[owners_of(part, i)] = (decay0 * second[:, at] + first[:, at]).reshape(per_head, piece, 128)
        ring_start(bm_out, bm_in, part, piece, 4 + part)

    loop(0, parts, back_round)

    rq_ref[...] = jnp.zeros_like(rq_ref)
    gc_ref[...] = jnp.zeros_like(gc_ref)
    gb_ref[...] = jnp.zeros_like(gb_ref)
    dst_ref[...] = jnp.zeros_like(dst_ref)
    scores_ref[...] = mm(b_ref[...], c_ref[...], NT)

    def near_back(h):
        cols = columns_of(h)
        here = channels(h)
        gap = jnp.where(along_iota >= down_iota, cum_row(h) - cols[CUM], -1e30)
        decay = jnp.exp(gap)
        mixed = mixed_ref[:, here]
        grad_mixed = norm_grad(u_ref[:, here], mixed, gain_ref[:, here], 0)
        gm_parts = split2(grad_mixed)
        x_h = x_ref[:, here]
        wide_x = x_h.astype(F32)
        value = mm3(split2(scores_ref[...] * decay), gm_parts)
        grad_out = wide_x + gain_ref[:, here] * mixed * scale_ref[0] - target_ref[:, here].astype(F32)
        gx_ref[:, here] = grad_out + skip_of(h) * grad_mixed + cols[STEP] * value
        grad_weights = mm(x_h, gm_parts[0], NT) + mm(x_h, gm_parts[1], NT)
        dst_ref[...] += grad_weights * decay * cols[STEP]
        row_sum = jnp.sum(grad_mixed * (mixed - skip_of(h) * wide_x), axis=1, keepdims=True)
        column_sum = jnp.sum(wide_x * value, axis=1, keepdims=True)
        rq_ref[...] = jnp.where(lane == h, row_sum, jnp.where(lane == h + 8, column_sum, rq_ref[...]))
        gc_ref[...] += mm3(split2(grad_mixed * expb_ref[:, here]), split2(sin_ref[h]), NT)

    loop(0, heads, near_back)
    grad_scores = dst_ref[...]
    high, low = split2(grad_scores)
    gb_ref[...] += mm(high, c_ref[...]) + mm(low, c_ref[...])
    high, low = split2(grad_scores.T)
    gc_ref[...] += mm(high, b_ref[...]) + mm(low, b_ref[...])

    def scan_back(part):
        ring_all(bm_out, bm_in, part, piece, 4 + part).wait_recv()
        grad = jnp.zeros((piece, 128), F32)
        for t in reversed(range(chips)):
            bp_out[part, t] = grad
            grad = fm_in[part, t, piece : piece + 1, :] * grad + bm_in[part, t]
        ring_start(bp_out, bp_in, part, piece, 6 + part)

    loop(0, parts, scan_back)

    def leave(part):
        for i in range(pair):
            at = part * pair + i
            second = bl_second[at]
            _, decay1 = decay_pair(at)
            for_second = bp_in[owners_of(part, i)].reshape(128, 128)
            for_first = decay1 * for_second + second
            gout_ref[mine + at] = jnp.where(core == 0, for_first, for_second)
            bs_out[at] = jnp.where(core == 0, for_second, for_first)

    def far_back(h):
        both_parts = stacked(gout_ref, h)
        reached = mm(bb_ref[...], both_parts)
        table = rq_ref[...]
        grad_b = gb_ref[...]
        for k in range(2):
            here = channels(h + k)
            at = slice(k * 128, k * 128 + 128)
            x_h = x_ref[:, here]
            weight = endwb_ref[:, here]
            gx_ref[:, here] += weight * reached[:, at]
            row_sum = jnp.sum(x_h.astype(F32) * reached[:, at], axis=1, keepdims=True)
            table = jnp.where(lane == h + k + 16, row_sum, table)
            parts_along = jnp.concatenate([both_parts[0:128, at], both_parts[128:256, at]], axis=1)
            grad_b = grad_b + weight * mm(jnp.concatenate([x_h, x_h], axis=1), parts_along, NT)
            leaving = decay_of(h + k) * sin_ref[h + k] + fl_own[h + k, 0:128, :]
            ext_ref[pl.ds(h + k, 1), :] = jnp.sum(gout_ref[h + k] * leaving, axis=0, keepdims=True)
        rq_ref[...] = table
        gb_ref[...] = grad_b

    def last_mine(part):
        ring_all(bp_out, bp_in, part, piece, 6 + part).wait_recv()
        leave(part)
        both(bs_out, gout_ref, part, 6 + part).start()
        heads_of(mine, part, far_back)

    def last_theirs(part):
        both(bs_out, gout_ref, part, 6 + part).wait_recv()
        heads_of(theirs, part, far_back)

    loop(0, parts, last_mine)
    loop(0, parts, last_theirs)

    for part in range(parts):
        swap_of(fl_own, fl_got, part, part).wait_send()
        both(fs_out, sin_ref, part, 2 + part).wait_send()
        mixed_to_twin(part).wait_send()
        both(bs_out, gout_ref, part, 6 + part).wait_send()
        ring_all(fm_out, fm_in, part, piece + 1, part).wait_send()
        ring_all(fp_out, fp_in, part, piece, 2 + part).wait_send()
        ring_all(bm_out, bm_in, part, piece, 4 + part).wait_send()
        ring_all(bp_out, bp_in, part, piece, 6 + part).wait_send()
    for copy in to_twin():
        copy.wait_send()
    other_ranks(lambda other: z_copy(0, other, other).wait_send())
    other_ranks(lambda other: z_copy(1, other, other).wait_send())
    z_copy(1, rank, rank).wait_send()


def finish(gx_in, gb_in, gc_in, rows_ref, rq_ref, ext_ref, gx_ref, gb_ref, gc_ref, gs_ref, sums_ref, sems):
    pairs = ((gx_in, gx_ref), (gb_in, gb_ref), (gc_in, gc_ref))
    copies = [pltpu.make_async_copy(source, target, sems.at[i]) for i, (source, target) in enumerate(pairs)]
    for copy in copies:
        copy.start()
    heads, tokens = sums_ref.shape
    step, enddec, rate = rows_ref[1], rows_ref[2], rows_ref[3]
    ends = rq_ref[...].T
    inner_x = ends[8 : 8 + heads, :] + enddec * ends[16 : 16 + heads, :]
    extra = jnp.sum(ext_ref[...], axis=1, keepdims=True)
    down_iota = lax.broadcasted_iota(jnp.int32, (tokens, tokens), 0)
    along_iota = lax.broadcasted_iota(jnp.int32, (tokens, tokens), 1)
    lower = (down_iota >= along_iota).astype(F32).astype(BF16)
    high, mid, low = split3(ends[0:heads, :] - step * inner_x)
    grad_dec = mm(high, lower) + (mm(mid, lower) + mm(low, lower)) + extra
    sums_ref[...] = inner_x - rate * grad_dec
    last = pltpu.make_async_copy(sums_ref, gs_ref, sems.at[3])
    last.start()
    for copy in copies:
        copy.wait()
    last.wait()


def body(chips, ranks, inputs, b_proj, c_proj, step_sizes, log_rate, forget, skip_gain, norm_gain, target):
    tokens, wide = inputs.shape
    heads = step_sizes.shape[1]
    half = heads // 2
    piece = half * 64 // chips
    vmem = pl.BlockSpec(memory_space=pltpu.VMEM)
    hbm = pl.BlockSpec(memory_space=pltpu.HBM)

    def buffer(*shape, dtype=F32):
        return pltpu.VMEM(shape, dtype)

    state = (heads, 128, 128)
    half_state = (half, 128, 128)
    operands = (
        inputs,
        target,
        b_proj.reshape(tokens, 128),
        c_proj.reshape(tokens, 128),
        step_sizes[0],
        forget[0],
        log_rate,
        skip_gain,
        norm_gain,
    )
    operands = tuple(pltpu.with_memory_space_constraint(operand, pltpu.HBM) for operand in operands)
    out_shape = (
        jax.ShapeDtypeStruct((tokens, wide), F32),
        jax.ShapeDtypeStruct((tokens, 128), F32),
        jax.ShapeDtypeStruct((tokens, 128), F32),
        jax.ShapeDtypeStruct((heads, tokens), F32),
    )
    results = pl.pallas_call(
        functools.partial(kernel, chips, ranks, float(wide * ranks)),
        out_shape=out_shape[0:3]
        + (
            jax.ShapeDtypeStruct((4, heads, tokens), F32),
            jax.ShapeDtypeStruct((tokens, 128), F32),
            jax.ShapeDtypeStruct((heads, 128), F32),
        ),
        in_specs=[hbm] * len(operands),
        out_specs=[vmem] * 6,
        scratch_shapes=[buffer(*operand.shape, dtype=operand.dtype) for operand in operands]
        + [
            buffer(tokens, 128),
            buffer(heads, 128),
            buffer(heads, 128),
            buffer(tokens, tokens),
            buffer(tokens, wide),
            buffer(tokens, wide),
            buffer(tokens, wide),
            buffer(tokens, wide),
            buffer(tokens, 256, dtype=BF16),
            buffer(tokens, 256, dtype=BF16),
            buffer(6, tokens, 128),
            buffer(*state),
            buffer(*state),
            buffer(128, tokens, dtype=BF16),
            buffer(128, tokens, dtype=BF16),
            buffer(tokens, tokens),
            buffer(3, tokens, 128),
            buffer(heads, 136, 128),
            buffer(half, 136, 128),
            buffer(2, chips, piece + 8, 128),
            buffer(2, chips, piece + 8, 128),
            buffer(2, chips, piece, 128),
            buffer(2, chips, piece, 128),
            buffer(*half_state),
            buffer(*half_state),
            buffer(tokens, wide // 2),
            buffer(tokens, wide // 2),
            buffer(tokens, wide // 2),
            buffer(128, tokens),
            buffer(128, tokens),
            buffer(128, tokens, dtype=BF16),
            buffer(2, chips, piece, 128),
            buffer(2, chips, piece, 128),
            buffer(2, chips, piece, 128),
            buffer(2, chips, piece, 128),
            buffer(*half_state),
            buffer(8, tokens),
            buffer(2, ranks, 8, tokens),
            pltpu.SemaphoreType.DMA((9,)),
            pltpu.SemaphoreType.DMA((11,)),
            pltpu.SemaphoreType.DMA((11,)),
            pltpu.SemaphoreType.DMA((8,)),
            pltpu.SemaphoreType.DMA((8,)),
            pltpu.SemaphoreType.DMA((2, ranks)),
            pltpu.SemaphoreType.DMA((2, ranks)),
        ],
        compiler_params=pltpu.CompilerParams(
            collective_id=0, has_side_effects=True, vmem_limit_bytes=24 * 1024 * 1024
        ),
        name="layer",
    )(*operands)
    grad_x, grad_b, grad_c, grad_steps = pl.pallas_call(
        finish,
        out_shape=out_shape,
        in_specs=[pl.BlockSpec(memory_space=pl.ANY)] * 3 + [vmem] * 3,
        out_specs=[hbm] * 4,
        scratch_shapes=[buffer(heads, tokens), pltpu.SemaphoreType.DMA((4,))],
        compiler_params=pltpu.CompilerParams(vmem_limit_bytes=4 * 1024 * 1024),
        name="finish",
    )(*results)
    return (
        grad_x,
        grad_b.reshape(1, tokens, 1, 128),
        grad_c.reshape(1, tokens, 1, 128),
        grad_steps[None],
    )


def solution(mesh):
    chips, ranks = mesh.shape["ctx"] // 2, mesh.shape["head"]
    in_specs = (
        P("ctx", "head"),
        P(None, "ctx", "head", None),
        P(None, "ctx", "head", None),
        P(None, "head", "ctx"),
        P(None, "head"),
        P(None, "head", "ctx"),
        P(None, "head"),
        P(None, "head"),
        P("ctx", "head"),
    )
    out_specs = (
        P("ctx", "head"),
        P(None, "ctx", "head", None),
        P(None, "ctx", "head", None),
        P(None, "head", "ctx"),
    )
    return jax.shard_map(
        functools.partial(body, chips, ranks),
        mesh=mesh,
        in_specs=in_specs,
        out_specs=out_specs,
        check_vma=False,
    )
```

```python
import functools

import jax
import jax.numpy as jnp
from jax import lax
from jax.experimental import pallas as pl
from jax.experimental.pallas import tpu as pltpu
from jax.sharding import PartitionSpec as P

EPSILON = 1e-05
MESH = pl.DeviceIdType.MESH
F32 = jnp.float32
BF16 = jnp.bfloat16
NN = (((1,), (0,)), ((), ()))
NT = (((1,), (1,)), ((), ()))

CUM, EXPCUM, ENDW, ENDDEC, STEP = range(5)


def mm(left, right, dims=NN):
    return lax.dot_general(left, right, dims, preferred_element_type=F32)


def split2(value):
    high = value.astype(BF16)
    low = (value - high.astype(F32)).astype(BF16)
    return high, low


def split3(value):
    high = value.astype(BF16)
    rest = value - high.astype(F32)
    mid = rest.astype(BF16)
    low = (rest - mid.astype(F32)).astype(BF16)
    return high, mid, low


def mm3(left, right, dims=NN):
    (lh, ll), (rh, rl) = left, right
    return mm(lh, rh, dims) + (mm(lh, rl, dims) + mm(ll, rh, dims))


def kernel(
    chips,
    ranks,
    width,
    x_hbm,
    target_hbm,
    b_hbm,
    c_hbm,
    step_hbm,
    forget_hbm,
    rate_hbm,
    skip_hbm,
    gain_hbm,
    gx_ref,
    gb_ref,
    gc_ref,
    rows_ref,
    rq_ref,
    ext_ref,
    x_ref,
    target_ref,
    b_ref,
    c_ref,
    step_ref,
    forget_ref,
    rate_ref,
    skip_ref,
    gain_ref,
    cols_ref,
    ends_ref,
    skips_ref,
    scores_ref,
    mixed_ref,
    u_ref,
    expb_ref,
    endwb_ref,
    cc_ref,
    bb_ref,
    scale_ref,
    sin_ref,
    gout_ref,
    btr_ref,
    ctr_ref,
    dst_ref,
    sum_ref,
    fl_own,
    fl_got,
    fm_out,
    fm_in,
    fp_out,
    fp_in,
    fs_out,
    bl_second,
    su_ref,
    sm_ref,
    se_ref,
    sc_ref,
    cf_ref,
    sct_ref,
    bm_out,
    bm_in,
    bp_out,
    bp_in,
    bs_out,
    z_out,
    z_in,
    load_sem,
    pair_send,
    pair_recv,
    ring_send,
    ring_recv,
    z_send,
    z_recv,
):
    tokens = x_ref.shape[0]
    heads = step_ref.shape[0]
    half = heads // 2
    chan = x_ref.shape[1] // heads
    parts, pair = 2, half // 2
    piece = pair * 128 // chips
    per_head = chips // pair
    ctx = lax.axis_index("ctx")
    rank = lax.axis_index("head")
    chip, core = lax.div(ctx, 2), lax.rem(ctx, 2)
    twin = chip * 2 + 1 - core
    sibling = (twin, rank)
    lines = chips // 4
    line, place = lax.div(chip, 4), lax.rem(chip, 4)

    def loop(low, high, step):
        def turn(i, carry):
            step(i)
            return carry

        lax.fori_loop(low, high, turn, 0)

    lines_from = [lax.rem(line + down, lines) * 4 for down in range(lines)]
    columns_from = [lax.rem(place + along, 4) for along in range(4)]
    offsets = [(down, along) for down in range(lines) for along in range(4)][1:]
    offsets.sort(key=lambda o: -(min(o[0], lines - o[0]) + min(o[1], 4 - o[1])))

    def other_chips(act):
        for down, along in offsets:
            act(lines_from[down] + columns_from[along])

    def other_ranks(act):
        for away in sorted(range(1, ranks), key=lambda k: -min(k, ranks - k)):
            act(lax.rem(rank + away, ranks))

    barrier = pltpu.get_barrier_semaphore()

    def greet(device):
        pl.semaphore_signal(barrier, inc=1, device_id=device, device_id_type=MESH)

    other_chips(lambda other: greet((other * 2 + core, rank)))
    other_ranks(lambda other: greet((ctx, other)))
    other_ranks(lambda other: greet((twin, other)))
    greet(sibling)

    loads = [
        pltpu.make_async_copy(source, target, load_sem.at[i])
        for i, (source, target) in enumerate(
            (
                (step_hbm, step_ref),
                (forget_hbm, forget_ref),
                (rate_hbm, rate_ref),
                (b_hbm, b_ref),
                (x_hbm, x_ref),
                (c_hbm, c_ref),
                (skip_hbm, skip_ref),
                (gain_hbm, gain_ref),
                (target_hbm, target_ref),
            )
        )
    ]
    for load in loads:
        load.start()

    down_iota = lax.broadcasted_iota(jnp.int32, (tokens, tokens), 0)
    along_iota = lax.broadcasted_iota(jnp.int32, (tokens, tokens), 1)
    diagonal = down_iota[0:heads, 0:heads] == along_iota[0:heads, 0:heads]

    def as_column(row):
        return jnp.sum(jnp.where(diagonal, row, 0.0), axis=1, keepdims=True)

    for load in loads[0:3]:
        load.wait()
    rate = jnp.exp(as_column(rate_ref[...]))
    step = step_ref[...]
    logdec = -step * rate - forget_ref[...]
    upper = (down_iota <= along_iota).astype(F32).astype(BF16)
    high, mid, low = split3(logdec)
    cum = mm(high, upper) + (mm(mid, upper) + mm(low, upper))
    last = cum[:, tokens - 1 : tokens]
    expcum = jnp.exp(cum)
    enddec = jnp.exp(last - cum)
    table = [cum, expcum, enddec * step, enddec, step]
    rows_ref[0] = cum
    rows_ref[1] = step
    rows_ref[2] = enddec
    rows_ref[3] = jnp.broadcast_to(rate, (heads, tokens))
    ends_ref[...] = jnp.broadcast_to(jnp.exp(last), (heads, 128))
    table = jnp.concatenate(table + [jnp.zeros((128 - heads * len(table), tokens), F32)], axis=0)
    cols_ref[...] = table.T
    loads[3].wait()
    btr_ref[...] = b_ref[...].astype(F32).T.astype(BF16)
    loads[4].wait()

    def columns_of(h, count=1):
        rolled = pltpu.roll(cols_ref[...], lax.rem(128 - h, 128), 1)
        each = [[rolled[:, 8 * q + k : 8 * q + k + 1] for q in range(5)] for k in range(count)]
        return each if count > 1 else each[0]

    def channels(h):
        return pl.ds(pl.multiple_of(h * chan, chan), chan)

    def cum_row(h):
        return rows_ref[0, pl.ds(h, 1), :]

    def step_row(h):
        return rows_ref[1, pl.ds(h, 1), :]

    def decay_of(h):
        return ends_ref[pl.ds(h, 1), :]

    def skip_of(h):
        return skips_ref[pl.ds(h, 1), :]

    def two(make):
        return jnp.concatenate([make(0), make(1)], axis=1)

    def local_state(h):
        columns = columns_of(h, 2)
        weighted = two(lambda k: x_ref[:, channels(h + k)].astype(F32) * columns[k][ENDW])
        high, low = split2(weighted)
        state = mm(btr_ref[...], high) + mm(btr_ref[...], low)
        for k in range(2):
            fl_own[h + k, 0:128, :] = state[:, k * 128 : k * 128 + 128]
            fl_own[h + k, 128:136, :] = jnp.broadcast_to(decay_of(h + k), (8, 128))

    def to_sibling(source, target, sem):
        return pltpu.make_async_remote_copy(
            src_ref=source,
            dst_ref=target,
            send_sem=pair_send.at[sem],
            recv_sem=pair_recv.at[sem],
            device_id=sibling,
            device_id_type=MESH,
        )

    mine, theirs = core * half, (1 - core) * half

    def swap_of(own, got, part, sem):
        return to_sibling(own.at[pl.ds(theirs + part * pair, pair)], got.at[pl.ds(part * pair, pair)], sem)

    def heads_of(base, part, act):
        act(base + part * pair)

    def ring_start(source, target, part, rows_sent, sem):
        def start(other):
            pltpu.make_async_remote_copy(
                src_ref=source.at[part, other, 0:rows_sent],
                dst_ref=target.at[part, chip, 0:rows_sent],
                send_sem=ring_send.at[sem],
                recv_sem=ring_recv.at[sem],
                device_id=(other * 2 + core, rank),
                device_id_type=MESH,
            ).start()

        other_chips(start)
        target[part, chip, 0:rows_sent, :] = source[part, chip, 0:rows_sent, :]

    def ring_all(source, target, part, rows_sent, sem):
        return pltpu.make_async_remote_copy(
            src_ref=source.at[part, 0 : chips - 1, 0:rows_sent],
            dst_ref=target.at[part, 0 : chips - 1, 0:rows_sent],
            send_sem=ring_send.at[sem],
            recv_sem=ring_recv.at[sem],
            device_id=sibling,
            device_id_type=MESH,
        )

    def pair_of(own, got, i):
        own_rows, got_rows = own[mine + i, 0:128, :], got[i, 0:128, :]
        first = jnp.where(core == 0, own_rows, got_rows)
        second = jnp.where(core == 0, got_rows, own_rows)
        return first, second

    def decay_pair(i):
        own_decay, got_decay = fl_own[mine + i, 128:129, :], fl_got[i, 128:129, :]
        first = jnp.where(core == 0, own_decay, got_decay)
        second = jnp.where(core == 0, got_decay, own_decay)
        return first, second

    def owners_of(part, i):
        return part, pl.ds(i * per_head, per_head), pl.ds(0, piece)

    def join_forward(part):
        for i in range(pair):
            first, second = pair_of(fl_own, fl_got, part * pair + i)
            decay0, decay1 = decay_pair(part * pair + i)
            joined = decay1 * first + second
            fm_out[owners_of(part, i)] = joined.reshape(per_head, piece, 128)
            fm_out[part, pl.ds(i * per_head, per_head), pl.ds(piece, 8)] = jnp.broadcast_to(
                (decay0 * decay1)[None], (per_head, 8, 128)
            )

    loop(0, half, lambda i: local_state(2 * i))
    pl.semaphore_wait(barrier, (chips - 1) + 2 * (ranks - 1) + 1)
    for part in range(parts):
        swap_of(fl_own, fl_got, part, part).start()

    def first_round(part):
        swap_of(fl_own, fl_got, part, part).wait_recv()
        join_forward(part)
        ring_start(fm_out, fm_in, part, piece + 1, part)

    loop(0, parts, first_round)

    for load in loads[5:]:
        load.wait()
    skips_ref[...] = jnp.broadcast_to(as_column(skip_ref[...]), (heads, 128))
    cf_ref[...] = c_ref[...].astype(F32).T
    ctr_ref[...] = cf_ref[...].astype(BF16)
    scores_ref[...] = mm(c_ref[...], b_ref[...], NT)
    cc_ref[...] = jnp.concatenate([c_ref[...], c_ref[...]], axis=1)
    bb_ref[...] = jnp.concatenate([b_ref[...], b_ref[...]], axis=1)

    def near(h):
        cols = columns_of(h)
        gap = jnp.where(down_iota >= along_iota, cols[CUM] - cum_row(h), -1e30)
        weights = scores_ref[...] * jnp.exp(gap) * step_row(h)
        high, low = split2(weights)
        x_h = x_ref[:, channels(h)]
        wide_x = x_h.astype(F32)
        mixed_ref[:, channels(h)] = mm(high, x_h) + mm(low, x_h) + skip_of(h) * wide_x
        u_ref[:, channels(h)] = gain_ref[:, channels(h)] * (wide_x - target_ref[:, channels(h)].astype(F32))
        expb_ref[:, channels(h)] = jnp.broadcast_to(cols[EXPCUM], (tokens, 128))
        endwb_ref[:, channels(h)] = jnp.broadcast_to(cols[ENDW], (tokens, 128))

    loop(0, heads, near)

    def channels_of(base, count):
        return pl.ds(pl.multiple_of(base * chan, chan), count * chan)

    def to_twin():
        return (
            to_sibling(u_ref.at[:, channels_of(theirs, half)], su_ref, 8),
            to_sibling(expb_ref.at[:, channels_of(theirs, half)], se_ref, 9),
            to_sibling(cf_ref, sc_ref, 10),
        )

    def mixed_to_twin(part):
        source = mixed_ref.at[:, channels_of(theirs + part * pair, pair)]
        return to_sibling(source, sm_ref.at[:, channels_of(part * pair, pair)], 4 + part)

    for copy in to_twin():
        copy.start()
    sum_ref[...] = jnp.zeros_like(sum_ref)

    def scan_forward(part):
        ring_all(fm_out, fm_in, part, piece + 1, part).wait_recv()
        state = jnp.zeros((piece, 128), F32)
        for t in range(chips):
            fp_out[part, t] = state
            state = fm_in[part, t, piece : piece + 1, :] * state + fm_in[part, t, 0:piece, :]
        ring_start(fp_out, fp_in, part, piece, 2 + part)

    loop(0, parts, scan_forward)

    def enter(part):
        for i in range(pair):
            at = part * pair + i
            first, _ = pair_of(fl_own, fl_got, at)
            decay0, _ = decay_pair(at)
            for_first = fp_in[owners_of(part, i)].reshape(128, 128)
            for_second = decay0 * for_first + first
            sin_ref[mine + at] = jnp.where(core == 0, for_first, for_second)
            fs_out[at] = jnp.where(core == 0, for_second, for_first)

    def both(own, got, part, sem):
        return to_sibling(own.at[pl.ds(part * pair, pair)], got.at[pl.ds(mine + part * pair, pair)], sem)

    def stacked(ref, h):
        high, low = split2(two(lambda k: ref[h + k]))
        return jnp.concatenate([high, low], axis=0)

    def far(h):
        reached = mm(cc_ref[...], stacked(sin_ref, h))
        sums = [0.0, 0.0, 0.0]
        for k in range(2):
            here = channels(h + k)
            mixed = mixed_ref[:, here] + expb_ref[:, here] * reached[:, k * 128 : k * 128 + 128]
            mixed_ref[:, here] = mixed
            gained = gain_ref[:, here] * mixed
            sums = [sums[0] + mixed * mixed, sums[1] + u_ref[:, here] * mixed, sums[2] + gained * gained]
        for i in range(3):
            sum_ref[i] += sums[i]

    def far_mine(part):
        ring_all(fp_out, fp_in, part, piece, 2 + part).wait_recv()
        enter(part)
        both(fs_out, sin_ref, part, 2 + part).start()
        heads_of(mine, part, far)

    def far_theirs(part):
        both(fs_out, sin_ref, part, 2 + part).wait_recv()
        heads_of(theirs, part, far)

    loop(0, parts, far_mine)
    loop(0, parts, far_theirs)

    lane = lax.broadcasted_iota(jnp.int32, (tokens, 128), 1)
    row_iota = lax.broadcasted_iota(jnp.int32, (8, 256), 0)
    sums = jnp.zeros((8, tokens), F32)
    for i in range(3):
        ones = (row_iota == i).astype(F32).astype(BF16)
        sums = sums + mm(ones, jnp.concatenate(split2(sum_ref[i]), axis=1), NT)
    z_out[...] = sums

    def z_copy(block, to, slot):
        return pltpu.make_async_remote_copy(
            src_ref=z_out,
            dst_ref=z_in.at[block, slot],
            send_sem=z_send.at[block, to],
            recv_sem=z_recv.at[block, slot],
            device_id=(twin if block else ctx, to),
            device_id_type=MESH,
        )

    other_ranks(lambda other: z_copy(0, other, rank).start())
    other_ranks(lambda other: z_copy(1, other, rank).start())
    z_copy(1, rank, rank).start()
    for part in range(parts):
        mixed_to_twin(part).start()
    z_in[0, rank] = z_out[...]
    for copy in to_twin():
        copy.wait_recv()
    sct_ref[...] = sc_ref[...].astype(BF16)
    z_copy(1, rank, rank).wait_recv()
    other_ranks(lambda other: z_copy(0, other, other).wait_recv())
    other_ranks(lambda other: z_copy(1, other, other).wait_recv())
    factors = []
    for block in range(2):
        total = z_in[block, 0]
        for i in range(1, ranks):
            total = total + z_in[block, i]
        inv_scale = lax.rsqrt(total[0:1, :] / width + EPSILON)
        inner = total[1:2, :] + inv_scale * total[2:3, :]
        factors += [inv_scale, inner * inv_scale * inv_scale * inv_scale / width]
    back = jnp.concatenate(factors + [jnp.zeros((124, tokens), F32)], axis=0).T
    for block in range(2):
        inv_col = jnp.broadcast_to(back[:, 2 * block : 2 * block + 1], (tokens, 128))
        scale_ref[3 * block] = inv_col
        scale_ref[3 * block + 1] = inv_col * inv_col
        scale_ref[3 * block + 2] = jnp.broadcast_to(back[:, 2 * block + 1 : 2 * block + 2], (tokens, 128))

    def norm_grad(gained, mixed, gain, block):
        factor = (gain * gain) * scale_ref[3 * block + 1] - scale_ref[3 * block + 2]
        return gained * scale_ref[3 * block] + mixed * factor

    def back_round(part):
        mixed_to_twin(part).wait_recv()

        def own(k):
            here = channels(mine + part * pair + k)
            grad_mixed = norm_grad(u_ref[:, here], mixed_ref[:, here], gain_ref[:, here], 0)
            return grad_mixed * expb_ref[:, here]

        def others(k):
            at = channels(part * pair + k)
            gain = gain_ref[:, channels(mine + part * pair + k)]
            return norm_grad(su_ref[:, at], sm_ref[:, at], gain, 1) * se_ref[:, at]

        high, low = split2(two(own))
        own_state = mm(ctr_ref[...], high) + mm(ctr_ref[...], low)
        high, low = split2(two(others))
        got_state = mm(sct_ref[...], high) + mm(sct_ref[...], low)
        first = jnp.where(core == 0, own_state, got_state)
        second = jnp.where(core == 0, got_state, own_state)
        for i in range(pair):
            at = slice(i * 128, i * 128 + 128)
            decay0, _ = decay_pair(part * pair + i)
            bl_second[part * pair + i] = second[:, at]
            bm_out[owners_of(part, i)] = (decay0 * second[:, at] + first[:, at]).reshape(per_head, piece, 128)
        ring_start(bm_out, bm_in, part, piece, 4 + part)

    loop(0, parts, back_round)

    rq_ref[...] = jnp.zeros_like(rq_ref)
    gc_ref[...] = jnp.zeros_like(gc_ref)
    gb_ref[...] = jnp.zeros_like(gb_ref)
    dst_ref[...] = jnp.zeros_like(dst_ref)
    scores_ref[...] = mm(b_ref[...], c_ref[...], NT)

    def near_back(h):
        cols = columns_of(h)
        here = channels(h)
        gap = jnp.where(along_iota >= down_iota, cum_row(h) - cols[CUM], -1e30)
        decay = jnp.exp(gap)
        mixed = mixed_ref[:, here]
        grad_mixed = norm_grad(u_ref[:, here], mixed, gain_ref[:, here], 0)
        gm_parts = split2(grad_mixed)
        x_h = x_ref[:, here]
        wide_x = x_h.astype(F32)
        value = mm3(split2(scores_ref[...] * decay), gm_parts)
        grad_out = wide_x + gain_ref[:, here] * mixed * scale_ref[0] - target_ref[:, here].astype(F32)
        gx_ref[:, here] = grad_out + skip_of(h) * grad_mixed + cols[STEP] * value
        grad_weights = mm(x_h, gm_parts[0], NT) + mm(x_h, gm_parts[1], NT)
        dst_ref[...] += grad_weights * decay * cols[STEP]
        row_sum = jnp.sum(grad_mixed * (mixed - skip_of(h) * wide_x), axis=1, keepdims=True)
        column_sum = jnp.sum(wide_x * value, axis=1, keepdims=True)
        rq_ref[...] = jnp.where(lane == h, row_sum, jnp.where(lane == h + 8, column_sum, rq_ref[...]))
        gc_ref[...] += mm3(split2(grad_mixed * expb_ref[:, here]), split2(sin_ref[h]), NT)

    loop(0, heads, near_back)
    grad_scores = dst_ref[...]
    high, low = split2(grad_scores)
    gb_ref[...] += mm(high, c_ref[...]) + mm(low, c_ref[...])
    high, low = split2(grad_scores.T)
    gc_ref[...] += mm(high, b_ref[...]) + mm(low, b_ref[...])

    def scan_back(part):
        ring_all(bm_out, bm_in, part, piece, 4 + part).wait_recv()
        grad = jnp.zeros((piece, 128), F32)
        for t in reversed(range(chips)):
            bp_out[part, t] = grad
            grad = fm_in[part, t, piece : piece + 1, :] * grad + bm_in[part, t]
        ring_start(bp_out, bp_in, part, piece, 6 + part)

    loop(0, parts, scan_back)

    def leave(part):
        for i in range(pair):
            at = part * pair + i
            second = bl_second[at]
            _, decay1 = decay_pair(at)
            for_second = bp_in[owners_of(part, i)].reshape(128, 128)
            for_first = decay1 * for_second + second
            gout_ref[mine + at] = jnp.where(core == 0, for_first, for_second)
            bs_out[at] = jnp.where(core == 0, for_second, for_first)

    def far_back(h):
        both_parts = stacked(gout_ref, h)
        reached = mm(bb_ref[...], both_parts)
        table = rq_ref[...]
        grad_b = gb_ref[...]
        for k in range(2):
            here = channels(h + k)
            at = slice(k * 128, k * 128 + 128)
            x_h = x_ref[:, here]
            weight = endwb_ref[:, here]
            gx_ref[:, here] += weight * reached[:, at]
            row_sum = jnp.sum(x_h.astype(F32) * reached[:, at], axis=1, keepdims=True)
            table = jnp.where(lane == h + k + 16, row_sum, table)
            parts_along = jnp.concatenate([both_parts[0:128, at], both_parts[128:256, at]], axis=1)
            grad_b = grad_b + weight * mm(jnp.concatenate([x_h, x_h], axis=1), parts_along, NT)
            leaving = decay_of(h + k) * sin_ref[h + k] + fl_own[h + k, 0:128, :]
            ext_ref[pl.ds(h + k, 1), :] = jnp.sum(gout_ref[h + k] * leaving, axis=0, keepdims=True)
        rq_ref[...] = table
        gb_ref[...] = grad_b

    def last_mine(part):
        ring_all(bp_out, bp_in, part, piece, 6 + part).wait_recv()
        leave(part)
        both(bs_out, gout_ref, part, 6 + part).start()
        heads_of(mine, part, far_back)

    def last_theirs(part):
        both(bs_out, gout_ref, part, 6 + part).wait_recv()
        heads_of(theirs, part, far_back)

    loop(0, parts, last_mine)
    loop(0, parts, last_theirs)

    for part in range(parts):
        swap_of(fl_own, fl_got, part, part).wait_send()
        both(fs_out, sin_ref, part, 2 + part).wait_send()
        mixed_to_twin(part).wait_send()
        both(bs_out, gout_ref, part, 6 + part).wait_send()
        ring_all(fm_out, fm_in, part, piece + 1, part).wait_send()
        ring_all(fp_out, fp_in, part, piece, 2 + part).wait_send()
        ring_all(bm_out, bm_in, part, piece, 4 + part).wait_send()
        ring_all(bp_out, bp_in, part, piece, 6 + part).wait_send()
    for copy in to_twin():
        copy.wait_send()
    other_ranks(lambda other: z_copy(0, other, other).wait_send())
    other_ranks(lambda other: z_copy(1, other, other).wait_send())
    z_copy(1, rank, rank).wait_send()


def finish(gx_in, gb_in, gc_in, rows_ref, rq_ref, ext_ref, gx_ref, gb_ref, gc_ref, gs_ref, sums_ref, sems):
    pairs = ((gx_in, gx_ref), (gb_in, gb_ref), (gc_in, gc_ref))
    copies = [pltpu.make_async_copy(source, target, sems.at[i]) for i, (source, target) in enumerate(pairs)]
    for copy in copies:
        copy.start()
    heads, tokens = sums_ref.shape
    step, enddec, rate = rows_ref[1], rows_ref[2], rows_ref[3]
    ends = rq_ref[...].T
    inner_x = ends[8 : 8 + heads, :] + enddec * ends[16 : 16 + heads, :]
    extra = jnp.sum(ext_ref[...], axis=1, keepdims=True)
    down_iota = lax.broadcasted_iota(jnp.int32, (tokens, tokens), 0)
    along_iota = lax.broadcasted_iota(jnp.int32, (tokens, tokens), 1)
    lower = (down_iota >= along_iota).astype(F32).astype(BF16)
    high, mid, low = split3(ends[0:heads, :] - step * inner_x)
    grad_dec = mm(high, lower) + (mm(mid, lower) + mm(low, lower)) + extra
    sums_ref[...] = inner_x - rate * grad_dec
    last = pltpu.make_async_copy(sums_ref, gs_ref, sems.at[3])
    last.start()
    for copy in copies:
        copy.wait()
    last.wait()


def body(chips, ranks, inputs, b_proj, c_proj, step_sizes, log_rate, forget, skip_gain, norm_gain, target):
    tokens, wide = inputs.shape
    heads = step_sizes.shape[1]
    half = heads // 2
    piece = half * 64 // chips
    vmem = pl.BlockSpec(memory_space=pltpu.VMEM)
    hbm = pl.BlockSpec(memory_space=pltpu.HBM)

    def buffer(*shape, dtype=F32):
        return pltpu.VMEM(shape, dtype)

    state = (heads, 128, 128)
    half_state = (half, 128, 128)
    operands = (
        inputs,
        target,
        b_proj.reshape(tokens, 128),
        c_proj.reshape(tokens, 128),
        step_sizes[0],
        forget[0],
        log_rate,
        skip_gain,
        norm_gain,
    )
    operands = tuple(pltpu.with_memory_space_constraint(operand, pltpu.HBM) for operand in operands)
    out_shape = (
        jax.ShapeDtypeStruct((tokens, wide), F32),
        jax.ShapeDtypeStruct((tokens, 128), F32),
        jax.ShapeDtypeStruct((tokens, 128), F32),
        jax.ShapeDtypeStruct((heads, tokens), F32),
    )
    results = pl.pallas_call(
        functools.partial(kernel, chips, ranks, float(wide * ranks)),
        out_shape=out_shape[0:3]
        + (
            jax.ShapeDtypeStruct((4, heads, tokens), F32),
            jax.ShapeDtypeStruct((tokens, 128), F32),
            jax.ShapeDtypeStruct((heads, 128), F32),
        ),
        in_specs=[hbm] * len(operands),
        out_specs=[vmem] * 6,
        scratch_shapes=[buffer(*operand.shape, dtype=operand.dtype) for operand in operands]
        + [
            buffer(tokens, 128),
            buffer(heads, 128),
            buffer(heads, 128),
            buffer(tokens, tokens),
            buffer(tokens, wide),
            buffer(tokens, wide),
            buffer(tokens, wide),
            buffer(tokens, wide),
            buffer(tokens, 256, dtype=BF16),
            buffer(tokens, 256, dtype=BF16),
            buffer(6, tokens, 128),
            buffer(*state),
            buffer(*state),
            buffer(128, tokens, dtype=BF16),
            buffer(128, tokens, dtype=BF16),
            buffer(tokens, tokens),
            buffer(3, tokens, 128),
            buffer(heads, 136, 128),
            buffer(half, 136, 128),
            buffer(2, chips, piece + 8, 128),
            buffer(2, chips, piece + 8, 128),
            buffer(2, chips, piece, 128),
            buffer(2, chips, piece, 128),
            buffer(*half_state),
            buffer(*half_state),
            buffer(tokens, wide // 2),
            buffer(tokens, wide // 2),
            buffer(tokens, wide // 2),
            buffer(128, tokens),
            buffer(128, tokens),
            buffer(128, tokens, dtype=BF16),
            buffer(2, chips, piece, 128),
            buffer(2, chips, piece, 128),
            buffer(2, chips, piece, 128),
            buffer(2, chips, piece, 128),
            buffer(*half_state),
            buffer(8, tokens),
            buffer(2, ranks, 8, tokens),
            pltpu.SemaphoreType.DMA((9,)),
            pltpu.SemaphoreType.DMA((11,)),
            pltpu.SemaphoreType.DMA((11,)),
            pltpu.SemaphoreType.DMA((8,)),
            pltpu.SemaphoreType.DMA((8,)),
            pltpu.SemaphoreType.DMA((2, ranks)),
            pltpu.SemaphoreType.DMA((2, ranks)),
        ],
        compiler_params=pltpu.CompilerParams(
            collective_id=0, has_side_effects=True, vmem_limit_bytes=24 * 1024 * 1024
        ),
        name="layer",
    )(*operands)
    grad_x, grad_b, grad_c, grad_steps = pl.pallas_call(
        finish,
        out_shape=out_shape,
        in_specs=[pl.BlockSpec(memory_space=pl.ANY)] * 3 + [vmem] * 3,
        out_specs=[hbm] * 4,
        scratch_shapes=[buffer(heads, tokens), pltpu.SemaphoreType.DMA((4,))],
        compiler_params=pltpu.CompilerParams(vmem_limit_bytes=4 * 1024 * 1024),
        name="finish",
    )(*results)
    return (
        grad_x,
        grad_b.reshape(1, tokens, 1, 128),
        grad_c.reshape(1, tokens, 1, 128),
        grad_steps[None],
    )


def solution(mesh):
    chips, ranks = mesh.shape["ctx"] // 2, mesh.shape["head"]
    in_specs = (
        P("ctx", "head"),
        P(None, "ctx", "head", None),
        P(None, "ctx", "head", None),
        P(None, "head", "ctx"),
        P(None, "head"),
        P(None, "head", "ctx"),
        P(None, "head"),
        P(None, "head"),
        P("ctx", "head"),
    )
    out_specs = (
        P("ctx", "head"),
        P(None, "ctx", "head", None),
        P(None, "ctx", "head", None),
        P(None, "head", "ctx"),
    )
    return jax.shard_map(
        functools.partial(body, chips, ranks),
        mesh=mesh,
        in_specs=in_specs,
        out_specs=out_specs,
        check_vma=False,
    )
```

```python
import functools

import jax
import jax.numpy as jnp
from jax import lax
from jax.experimental import pallas as pl
from jax.experimental.pallas import tpu as pltpu
from jax.sharding import PartitionSpec as P

EPSILON = 1e-05
MESH = pl.DeviceIdType.MESH
F32 = jnp.float32
BF16 = jnp.bfloat16
NN = (((1,), (0,)), ((), ()))
NT = (((1,), (1,)), ((), ()))

CUM, EXPCUM, ENDW, ENDDEC, STEP = range(5)


def mm(left, right, dims=NN):
    return lax.dot_general(left, right, dims, preferred_element_type=F32)


def split2(value):
    high = value.astype(BF16)
    low = (value - high.astype(F32)).astype(BF16)
    return high, low


def split3(value):
    high = value.astype(BF16)
    rest = value - high.astype(F32)
    mid = rest.astype(BF16)
    low = (rest - mid.astype(F32)).astype(BF16)
    return high, mid, low


def mm3(left, right, dims=NN):
    (lh, ll), (rh, rl) = left, right
    return mm(lh, rh, dims) + (mm(lh, rl, dims) + mm(ll, rh, dims))


def kernel(
    chips,
    ranks,
    width,
    x_hbm,
    target_hbm,
    b_hbm,
    c_hbm,
    step_hbm,
    forget_hbm,
    rate_hbm,
    skip_hbm,
    gain_hbm,
    gx_ref,
    gb_ref,
    gc_ref,
    rows_ref,
    rq_ref,
    ext_ref,
    x_ref,
    target_ref,
    b_ref,
    c_ref,
    step_ref,
    forget_ref,
    rate_ref,
    skip_ref,
    gain_ref,
    cols_ref,
    ends_ref,
    skips_ref,
    scores_ref,
    mixed_ref,
    gm_ref,
    u_ref,
    expb_ref,
    endwb_ref,
    cc_ref,
    bb_ref,
    scale_ref,
    sin_ref,
    gout_ref,
    btr_ref,
    ctr_ref,
    dst_ref,
    sum_ref,
    fl_own,
    fl_got,
    fm_out,
    fm_in,
    fp_out,
    fp_in,
    fs_out,
    bl_own,
    bl_got,
    bm_out,
    bm_in,
    bp_out,
    bp_in,
    bs_out,
    z_out,
    z_in,
    load_sem,
    pair_send,
    pair_recv,
    ring_send,
    ring_recv,
    z_send,
    z_recv,
):
    tokens = x_ref.shape[0]
    heads = step_ref.shape[0]
    half = heads // 2
    chan = x_ref.shape[1] // heads
    parts, pair = 2, half // 2
    piece = pair * 128 // chips
    per_head = chips // pair
    ctx = lax.axis_index("ctx")
    rank = lax.axis_index("head")
    chip, core = lax.div(ctx, 2), lax.rem(ctx, 2)
    sibling = (chip * 2 + 1 - core, rank)
    lines = chips // 4
    line, place = lax.div(chip, 4), lax.rem(chip, 4)

    def loop(low, high, step):
        def turn(i, carry):
            step(i)
            return carry

        lax.fori_loop(low, high, turn, 0)

    lines_from = [lax.rem(line + down, lines) * 4 for down in range(lines)]
    columns_from = [lax.rem(place + along, 4) for along in range(4)]
    offsets = [(down, along) for down in range(lines) for along in range(4)][1:]
    offsets.sort(key=lambda o: -(min(o[0], lines - o[0]) + min(o[1], 4 - o[1])))

    def unrolled(count, act):
        for i in range(count):
            act(i)

    def other_chips(act):
        for down, along in offsets:
            act(lines_from[down] + columns_from[along])

    def other_ranks(act):
        for away in sorted(range(1, ranks), key=lambda k: -min(k, ranks - k)):
            act(lax.rem(rank + away, ranks))

    barrier = pltpu.get_barrier_semaphore()

    def greet(device):
        pl.semaphore_signal(barrier, inc=1, device_id=device, device_id_type=MESH)

    other_chips(lambda other: greet((other * 2 + core, rank)))
    other_ranks(lambda other: greet((ctx, other)))
    greet(sibling)

    loads = [
        pltpu.make_async_copy(source, target, load_sem.at[i])
        for i, (source, target) in enumerate(
            (
                (step_hbm, step_ref),
                (forget_hbm, forget_ref),
                (rate_hbm, rate_ref),
                (b_hbm, b_ref),
                (x_hbm, x_ref),
                (c_hbm, c_ref),
                (skip_hbm, skip_ref),
                (gain_hbm, gain_ref),
                (target_hbm, target_ref),
            )
        )
    ]
    for load in loads:
        load.start()

    down_iota = lax.broadcasted_iota(jnp.int32, (tokens, tokens), 0)
    along_iota = lax.broadcasted_iota(jnp.int32, (tokens, tokens), 1)
    diagonal = down_iota[0:heads, 0:heads] == along_iota[0:heads, 0:heads]

    def as_column(row):
        return jnp.sum(jnp.where(diagonal, row, 0.0), axis=1, keepdims=True)

    for load in loads[0:3]:
        load.wait()
    rate = jnp.exp(as_column(rate_ref[...]))
    step = step_ref[...]
    logdec = -step * rate - forget_ref[...]
    upper = (down_iota <= along_iota).astype(F32).astype(BF16)
    high, mid, low = split3(logdec)
    cum = mm(high, upper) + (mm(mid, upper) + mm(low, upper))
    last = cum[:, tokens - 1 : tokens]
    expcum = jnp.exp(cum)
    enddec = jnp.exp(last - cum)
    table = [cum, expcum, enddec * step, enddec, step]
    rows_ref[0] = cum
    rows_ref[1] = step
    rows_ref[2] = enddec
    rows_ref[3] = jnp.broadcast_to(rate, (heads, tokens))
    ends_ref[...] = jnp.broadcast_to(jnp.exp(last), (heads, 128))
    table = jnp.concatenate(table + [jnp.zeros((128 - heads * len(table), tokens), F32)], axis=0)
    cols_ref[...] = table.T
    loads[3].wait()
    btr_ref[...] = b_ref[...].astype(F32).T.astype(BF16)
    loads[4].wait()

    def columns_of(h, count=1):
        rolled = pltpu.roll(cols_ref[...], lax.rem(128 - h, 128), 1)
        each = [[rolled[:, 8 * q + k : 8 * q + k + 1] for q in range(5)] for k in range(count)]
        return each if count > 1 else each[0]

    def channels(h):
        return pl.ds(pl.multiple_of(h * chan, chan), chan)

    def cum_row(h):
        return rows_ref[0, pl.ds(h, 1), :]

    def step_row(h):
        return rows_ref[1, pl.ds(h, 1), :]

    def decay_of(h):
        return ends_ref[pl.ds(h, 1), :]

    def skip_of(h):
        return skips_ref[pl.ds(h, 1), :]

    def two(make):
        return jnp.concatenate([make(0), make(1)], axis=1)

    def local_state(h):
        columns = columns_of(h, 2)
        weighted = two(lambda k: x_ref[:, channels(h + k)].astype(F32) * columns[k][ENDW])
        high, low = split2(weighted)
        state = mm(btr_ref[...], high) + mm(btr_ref[...], low)
        for k in range(2):
            fl_own[h + k, 0:128, :] = state[:, k * 128 : k * 128 + 128]
            fl_own[h + k, 128:136, :] = jnp.broadcast_to(decay_of(h + k), (8, 128))

    def to_sibling(source, target, sem):
        return pltpu.make_async_remote_copy(
            src_ref=source,
            dst_ref=target,
            send_sem=pair_send.at[sem],
            recv_sem=pair_recv.at[sem],
            device_id=sibling,
            device_id_type=MESH,
        )

    mine, theirs = core * half, (1 - core) * half

    def swap_of(own, got, part, sem):
        return to_sibling(own.at[pl.ds(theirs + part * pair, pair)], got.at[pl.ds(part * pair, pair)], sem)

    def heads_of(base, part, act):
        act(base + part * pair)

    def ring_start(source, target, part, rows_sent, sem):
        def start(other):
            pltpu.make_async_remote_copy(
                src_ref=source.at[part, other, 0:rows_sent],
                dst_ref=target.at[part, chip, 0:rows_sent],
                send_sem=ring_send.at[sem],
                recv_sem=ring_recv.at[sem],
                device_id=(other * 2 + core, rank),
                device_id_type=MESH,
            ).start()

        other_chips(start)
        target[part, chip, 0:rows_sent, :] = source[part, chip, 0:rows_sent, :]

    def ring_all(source, target, part, rows_sent, sem):
        return pltpu.make_async_remote_copy(
            src_ref=source.at[part, 0 : chips - 1, 0:rows_sent],
            dst_ref=target.at[part, 0 : chips - 1, 0:rows_sent],
            send_sem=ring_send.at[sem],
            recv_sem=ring_recv.at[sem],
            device_id=sibling,
            device_id_type=MESH,
        )

    def pair_of(own, got, i):
        own_rows, got_rows = own[mine + i, 0:128, :], got[i, 0:128, :]
        first = jnp.where(core == 0, own_rows, got_rows)
        second = jnp.where(core == 0, got_rows, own_rows)
        return first, second

    def decay_pair(i):
        own_decay, got_decay = fl_own[mine + i, 128:129, :], fl_got[i, 128:129, :]
        first = jnp.where(core == 0, own_decay, got_decay)
        second = jnp.where(core == 0, got_decay, own_decay)
        return first, second

    def owners_of(part, i):
        return part, pl.ds(i * per_head, per_head), pl.ds(0, piece)

    def join_forward(part):
        for i in range(pair):
            first, second = pair_of(fl_own, fl_got, part * pair + i)
            decay0, decay1 = decay_pair(part * pair + i)
            joined = decay1 * first + second
            fm_out[owners_of(part, i)] = joined.reshape(per_head, piece, 128)
            fm_out[part, pl.ds(i * per_head, per_head), pl.ds(piece, 8)] = jnp.broadcast_to(
                (decay0 * decay1)[None], (per_head, 8, 128)
            )

    loop(0, half, lambda i: local_state(2 * i))
    pl.semaphore_wait(barrier, (chips - 1) + (ranks - 1) + 1)
    for part in range(parts):
        swap_of(fl_own, fl_got, part, part).start()

    def first_round(part):
        swap_of(fl_own, fl_got, part, part).wait_recv()
        join_forward(part)
        ring_start(fm_out, fm_in, part, piece + 1, part)

    unrolled(parts, first_round)

    for load in loads[5:]:
        load.wait()
    skips_ref[...] = jnp.broadcast_to(as_column(skip_ref[...]), (heads, 128))
    ctr_ref[...] = c_ref[...].astype(F32).T.astype(BF16)
    scores_ref[...] = mm(c_ref[...], b_ref[...], NT)
    cc_ref[...] = jnp.concatenate([c_ref[...], c_ref[...]], axis=1)
    bb_ref[...] = jnp.concatenate([b_ref[...], b_ref[...]], axis=1)

    def near(h):
        cols = columns_of(h)
        gap = jnp.where(down_iota >= along_iota, cols[CUM] - cum_row(h), -1e30)
        weights = scores_ref[...] * jnp.exp(gap) * step_row(h)
        high, low = split2(weights)
        x_h = x_ref[:, channels(h)]
        wide_x = x_h.astype(F32)
        mixed_ref[:, channels(h)] = mm(high, x_h) + mm(low, x_h) + skip_of(h) * wide_x
        u_ref[:, channels(h)] = gain_ref[:, channels(h)] * (wide_x - target_ref[:, channels(h)].astype(F32))
        expb_ref[:, channels(h)] = jnp.broadcast_to(cols[EXPCUM], (tokens, 128))
        endwb_ref[:, channels(h)] = jnp.broadcast_to(cols[ENDW], (tokens, 128))

    loop(0, heads, near)
    sum_ref[...] = jnp.zeros_like(sum_ref)

    def scan_forward(part):
        ring_all(fm_out, fm_in, part, piece + 1, part).wait_recv()
        state = jnp.zeros((piece, 128), F32)
        for t in range(chips):
            fp_out[part, t] = state
            state = fm_in[part, t, piece : piece + 1, :] * state + fm_in[part, t, 0:piece, :]
        ring_start(fp_out, fp_in, part, piece, 2 + part)

    unrolled(parts, scan_forward)

    def enter(part):
        for i in range(pair):
            at = part * pair + i
            first, _ = pair_of(fl_own, fl_got, at)
            decay0, _ = decay_pair(at)
            for_first = fp_in[owners_of(part, i)].reshape(128, 128)
            for_second = decay0 * for_first + first
            sin_ref[mine + at] = jnp.where(core == 0, for_first, for_second)
            fs_out[at] = jnp.where(core == 0, for_second, for_first)

    def both(own, got, part, sem):
        return to_sibling(own.at[pl.ds(part * pair, pair)], got.at[pl.ds(mine + part * pair, pair)], sem)

    def stacked(ref, h):
        high, low = split2(two(lambda k: ref[h + k]))
        return jnp.concatenate([high, low], axis=0)

    def far(h):
        reached = mm(cc_ref[...], stacked(sin_ref, h))
        sums = [0.0, 0.0, 0.0]
        for k in range(2):
            here = channels(h + k)
            mixed = mixed_ref[:, here] + expb_ref[:, here] * reached[:, k * 128 : k * 128 + 128]
            mixed_ref[:, here] = mixed
            gained = gain_ref[:, here] * mixed
            sums = [sums[0] + mixed * mixed, sums[1] + u_ref[:, here] * mixed, sums[2] + gained * gained]
        for i in range(3):
            sum_ref[i] += sums[i]

    def far_mine(part):
        ring_all(fp_out, fp_in, part, piece, 2 + part).wait_recv()
        enter(part)
        both(fs_out, sin_ref, part, 2 + part).start()
        heads_of(mine, part, far)

    def far_theirs(part):
        both(fs_out, sin_ref, part, 2 + part).wait_recv()
        heads_of(theirs, part, far)

    unrolled(parts, far_mine)
    unrolled(parts, far_theirs)

    lane = lax.broadcasted_iota(jnp.int32, (tokens, 128), 1)
    row_iota = lax.broadcasted_iota(jnp.int32, (8, 256), 0)
    sums = jnp.zeros((8, tokens), F32)
    for i in range(3):
        ones = (row_iota == i).astype(F32).astype(BF16)
        sums = sums + mm(ones, jnp.concatenate(split2(sum_ref[i]), axis=1), NT)
    z_out[...] = sums

    def z_copy(to, slot):
        return pltpu.make_async_remote_copy(
            src_ref=z_out,
            dst_ref=z_in.at[slot],
            send_sem=z_send.at[to],
            recv_sem=z_recv.at[slot],
            device_id=(ctx, to),
            device_id_type=MESH,
        )

    other_ranks(lambda other: z_copy(other, rank).start())
    z_in[rank] = z_out[...]
    other_ranks(lambda other: z_copy(other, other).wait_recv())
    total = z_in[0]
    for i in range(1, ranks):
        total = total + z_in[i]
    inv_scale = lax.rsqrt(total[0:1, :] / width + EPSILON)
    inner = total[1:2, :] + inv_scale * total[2:3, :]
    coef = inner * inv_scale * inv_scale * inv_scale / width
    back = jnp.concatenate([inv_scale, coef, jnp.zeros((126, tokens), F32)], axis=0).T
    inv_col = jnp.broadcast_to(back[:, 0:1], (tokens, 128))
    scale_ref[0] = inv_col
    scale_ref[1] = inv_col * inv_col
    scale_ref[2] = jnp.broadcast_to(back[:, 1:2], (tokens, 128))

    def norm_back(h):
        def weighted(k):
            here = channels(h + k)
            gain = gain_ref[:, here]
            factor = (gain * gain) * scale_ref[1] - scale_ref[2]
            grad_mixed = u_ref[:, here] * scale_ref[0] + mixed_ref[:, here] * factor
            gm_ref[:, here] = grad_mixed
            return grad_mixed * expb_ref[:, here]

        high, low = split2(two(weighted))
        state = mm(ctr_ref[...], high) + mm(ctr_ref[...], low)
        for k in range(2):
            bl_own[h + k] = state[:, k * 128 : k * 128 + 128]

    def join_back(part):
        for i in range(pair):
            first, second = pair_of(bl_own, bl_got, part * pair + i)
            decay0, _ = decay_pair(part * pair + i)
            bm_out[owners_of(part, i)] = (decay0 * second + first).reshape(per_head, piece, 128)

    def back_theirs(part):
        heads_of(theirs, part, norm_back)
        swap_of(bl_own, bl_got, part, 4 + part).start()

    def back_mine(part):
        heads_of(mine, part, norm_back)
        swap_of(bl_own, bl_got, part, 4 + part).wait_recv()
        join_back(part)
        ring_start(bm_out, bm_in, part, piece, 4 + part)

    unrolled(parts, back_theirs)
    unrolled(parts, back_mine)

    rq_ref[...] = jnp.zeros_like(rq_ref)
    gc_ref[...] = jnp.zeros_like(gc_ref)
    gb_ref[...] = jnp.zeros_like(gb_ref)
    dst_ref[...] = jnp.zeros_like(dst_ref)
    scores_ref[...] = mm(b_ref[...], c_ref[...], NT)

    def near_back(h):
        cols = columns_of(h)
        here = channels(h)
        gap = jnp.where(along_iota >= down_iota, cum_row(h) - cols[CUM], -1e30)
        decay = jnp.exp(gap)
        grad_mixed = gm_ref[:, here]
        gm_parts = split2(grad_mixed)
        x_h = x_ref[:, here]
        wide_x = x_h.astype(F32)
        mixed = mixed_ref[:, here]
        value = mm3(split2(scores_ref[...] * decay), gm_parts)
        grad_out = wide_x + gain_ref[:, here] * mixed * scale_ref[0] - target_ref[:, here].astype(F32)
        gx_ref[:, here] = grad_out + skip_of(h) * grad_mixed + cols[STEP] * value
        grad_weights = mm(x_h, gm_parts[0], NT) + mm(x_h, gm_parts[1], NT)
        dst_ref[...] += grad_weights * decay * cols[STEP]
        row_sum = jnp.sum(grad_mixed * (mixed - skip_of(h) * wide_x), axis=1, keepdims=True)
        column_sum = jnp.sum(wide_x * value, axis=1, keepdims=True)
        rq_ref[...] = jnp.where(lane == h, row_sum, jnp.where(lane == h + 8, column_sum, rq_ref[...]))
        gc_ref[...] += mm3(split2(grad_mixed * expb_ref[:, here]), split2(sin_ref[h]), NT)

    loop(0, heads, near_back)
    grad_scores = dst_ref[...]
    high, low = split2(grad_scores)
    gb_ref[...] += mm(high, c_ref[...]) + mm(low, c_ref[...])
    high, low = split2(grad_scores.T)
    gc_ref[...] += mm(high, b_ref[...]) + mm(low, b_ref[...])

    def scan_back(part):
        ring_all(bm_out, bm_in, part, piece, 4 + part).wait_recv()
        grad = jnp.zeros((piece, 128), F32)
        for t in reversed(range(chips)):
            bp_out[part, t] = grad
            grad = fm_in[part, t, piece : piece + 1, :] * grad + bm_in[part, t]
        ring_start(bp_out, bp_in, part, piece, 6 + part)

    unrolled(parts, scan_back)

    def leave(part):
        for i in range(pair):
            at = part * pair + i
            _, second = pair_of(bl_own, bl_got, at)
            _, decay1 = decay_pair(at)
            for_second = bp_in[owners_of(part, i)].reshape(128, 128)
            for_first = decay1 * for_second + second
            gout_ref[mine + at] = jnp.where(core == 0, for_first, for_second)
            bs_out[at] = jnp.where(core == 0, for_second, for_first)

    def far_back(h):
        both_parts = stacked(gout_ref, h)
        reached = mm(bb_ref[...], both_parts)
        table = rq_ref[...]
        grad_b = gb_ref[...]
        for k in range(2):
            here = channels(h + k)
            at = slice(k * 128, k * 128 + 128)
            x_h = x_ref[:, here]
            weight = endwb_ref[:, here]
            gx_ref[:, here] += weight * reached[:, at]
            row_sum = jnp.sum(x_h.astype(F32) * reached[:, at], axis=1, keepdims=True)
            table = jnp.where(lane == h + k + 16, row_sum, table)
            parts_along = jnp.concatenate([both_parts[0:128, at], both_parts[128:256, at]], axis=1)
            grad_b = grad_b + weight * mm(jnp.concatenate([x_h, x_h], axis=1), parts_along, NT)
            leaving = decay_of(h + k) * sin_ref[h + k] + fl_own[h + k, 0:128, :]
            ext_ref[pl.ds(h + k, 1), :] = jnp.sum(gout_ref[h + k] * leaving, axis=0, keepdims=True)
        rq_ref[...] = table
        gb_ref[...] = grad_b

    def last_mine(part):
        ring_all(bp_out, bp_in, part, piece, 6 + part).wait_recv()
        leave(part)
        both(bs_out, gout_ref, part, 6 + part).start()
        heads_of(mine, part, far_back)

    def last_theirs(part):
        both(bs_out, gout_ref, part, 6 + part).wait_recv()
        heads_of(theirs, part, far_back)

    unrolled(parts, last_mine)
    unrolled(parts, last_theirs)

    for part in range(parts):
        swap_of(fl_own, fl_got, part, part).wait_send()
        both(fs_out, sin_ref, part, 2 + part).wait_send()
        swap_of(bl_own, bl_got, part, 4 + part).wait_send()
        both(bs_out, gout_ref, part, 6 + part).wait_send()
        ring_all(fm_out, fm_in, part, piece + 1, part).wait_send()
        ring_all(fp_out, fp_in, part, piece, 2 + part).wait_send()
        ring_all(bm_out, bm_in, part, piece, 4 + part).wait_send()
        ring_all(bp_out, bp_in, part, piece, 6 + part).wait_send()
    other_ranks(lambda other: z_copy(other, other).wait_send())


def finish(gx_in, gb_in, gc_in, rows_ref, rq_ref, ext_ref, gx_ref, gb_ref, gc_ref, gs_ref, sums_ref, sems):
    pairs = ((gx_in, gx_ref), (gb_in, gb_ref), (gc_in, gc_ref))
    copies = [pltpu.make_async_copy(source, target, sems.at[i]) for i, (source, target) in enumerate(pairs)]
    for copy in copies:
        copy.start()
    heads, tokens = sums_ref.shape
    step, enddec, rate = rows_ref[1], rows_ref[2], rows_ref[3]
    ends = rq_ref[...].T
    inner_x = ends[8 : 8 + heads, :] + enddec * ends[16 : 16 + heads, :]
    extra = jnp.sum(ext_ref[...], axis=1, keepdims=True)
    down_iota = lax.broadcasted_iota(jnp.int32, (tokens, tokens), 0)
    along_iota = lax.broadcasted_iota(jnp.int32, (tokens, tokens), 1)
    lower = (down_iota >= along_iota).astype(F32).astype(BF16)
    high, mid, low = split3(ends[0:heads, :] - step * inner_x)
    grad_dec = mm(high, lower) + (mm(mid, lower) + mm(low, lower)) + extra
    sums_ref[...] = inner_x - rate * grad_dec
    last = pltpu.make_async_copy(sums_ref, gs_ref, sems.at[3])
    last.start()
    for copy in copies:
        copy.wait()
    last.wait()


def body(chips, ranks, inputs, b_proj, c_proj, step_sizes, log_rate, forget, skip_gain, norm_gain, target):
    tokens, wide = inputs.shape
    heads = step_sizes.shape[1]
    half = heads // 2
    piece = half * 64 // chips
    vmem = pl.BlockSpec(memory_space=pltpu.VMEM)
    hbm = pl.BlockSpec(memory_space=pltpu.HBM)

    def buffer(*shape, dtype=F32):
        return pltpu.VMEM(shape, dtype)

    state = (heads, 128, 128)
    half_state = (half, 128, 128)
    operands = (
        inputs,
        target,
        b_proj.reshape(tokens, 128),
        c_proj.reshape(tokens, 128),
        step_sizes[0],
        forget[0],
        log_rate,
        skip_gain,
        norm_gain,
    )
    operands = tuple(pltpu.with_memory_space_constraint(operand, pltpu.HBM) for operand in operands)
    out_shape = (
        jax.ShapeDtypeStruct((tokens, wide), F32),
        jax.ShapeDtypeStruct((tokens, 128), F32),
        jax.ShapeDtypeStruct((tokens, 128), F32),
        jax.ShapeDtypeStruct((heads, tokens), F32),
    )
    results = pl.pallas_call(
        functools.partial(kernel, chips, ranks, float(wide * ranks)),
        out_shape=out_shape[0:3]
        + (
            jax.ShapeDtypeStruct((4, heads, tokens), F32),
            jax.ShapeDtypeStruct((tokens, 128), F32),
            jax.ShapeDtypeStruct((heads, 128), F32),
        ),
        in_specs=[hbm] * len(operands),
        out_specs=[vmem] * 6,
        scratch_shapes=[buffer(*operand.shape, dtype=operand.dtype) for operand in operands]
        + [
            buffer(tokens, 128),
            buffer(heads, 128),
            buffer(heads, 128),
            buffer(tokens, tokens),
            buffer(tokens, wide),
            buffer(tokens, wide),
            buffer(tokens, wide),
            buffer(tokens, wide),
            buffer(tokens, wide),
            buffer(tokens, 256, dtype=BF16),
            buffer(tokens, 256, dtype=BF16),
            buffer(3, tokens, 128),
            buffer(*state),
            buffer(*state),
            buffer(128, tokens, dtype=BF16),
            buffer(128, tokens, dtype=BF16),
            buffer(tokens, tokens),
            buffer(3, tokens, 128),
            buffer(heads, 136, 128),
            buffer(half, 136, 128),
            buffer(2, chips, piece + 8, 128),
            buffer(2, chips, piece + 8, 128),
            buffer(2, chips, piece, 128),
            buffer(2, chips, piece, 128),
            buffer(*half_state),
            buffer(*state),
            buffer(*half_state),
            buffer(2, chips, piece, 128),
            buffer(2, chips, piece, 128),
            buffer(2, chips, piece, 128),
            buffer(2, chips, piece, 128),
            buffer(*half_state),
            buffer(8, tokens),
            buffer(ranks, 8, tokens),
            pltpu.SemaphoreType.DMA((9,)),
            pltpu.SemaphoreType.DMA((8,)),
            pltpu.SemaphoreType.DMA((8,)),
            pltpu.SemaphoreType.DMA((8,)),
            pltpu.SemaphoreType.DMA((8,)),
            pltpu.SemaphoreType.DMA((ranks,)),
            pltpu.SemaphoreType.DMA((ranks,)),
        ],
        compiler_params=pltpu.CompilerParams(
            collective_id=0, has_side_effects=True, vmem_limit_bytes=24 * 1024 * 1024
        ),
        name="layer",
    )(*operands)
    grad_x, grad_b, grad_c, grad_steps = pl.pallas_call(
        finish,
        out_shape=out_shape,
        in_specs=[pl.BlockSpec(memory_space=pl.ANY)] * 3 + [vmem] * 3,
        out_specs=[hbm] * 4,
        scratch_shapes=[buffer(heads, tokens), pltpu.SemaphoreType.DMA((4,))],
        compiler_params=pltpu.CompilerParams(vmem_limit_bytes=4 * 1024 * 1024),
        name="finish",
    )(*results)
    return (
        grad_x,
        grad_b.reshape(1, tokens, 1, 128),
        grad_c.reshape(1, tokens, 1, 128),
        grad_steps[None],
    )


def solution(mesh):
    chips, ranks = mesh.shape["ctx"] // 2, mesh.shape["head"]
    in_specs = (
        P("ctx", "head"),
        P(None, "ctx", "head", None),
        P(None, "ctx", "head", None),
        P(None, "head", "ctx"),
        P(None, "head"),
        P(None, "head", "ctx"),
        P(None, "head"),
        P(None, "head"),
        P("ctx", "head"),
    )
    out_specs = (
        P("ctx", "head"),
        P(None, "ctx", "head", None),
        P(None, "ctx", "head", None),
        P(None, "head", "ctx"),
    )
    return jax.shard_map(
        functools.partial(body, chips, ranks),
        mesh=mesh,
        in_specs=in_specs,
        out_specs=out_specs,
        check_vma=False,
    )
```

```python
import functools

import jax
import jax.numpy as jnp
from jax import lax
from jax.experimental import pallas as pl
from jax.experimental.pallas import tpu as pltpu
from jax.sharding import PartitionSpec as P

EPSILON = 1e-05
MESH = pl.DeviceIdType.MESH
F32 = jnp.float32
BF16 = jnp.bfloat16
NN = (((1,), (0,)), ((), ()))
NT = (((1,), (1,)), ((), ()))

CUM, EXPCUM, ENDW, ENDDEC, STEP = range(5)


def mm(left, right, dims=NN):
    return lax.dot_general(left, right, dims, preferred_element_type=F32)


def split2(value):
    high = value.astype(BF16)
    low = (value - high.astype(F32)).astype(BF16)
    return high, low


def split3(value):
    high = value.astype(BF16)
    rest = value - high.astype(F32)
    mid = rest.astype(BF16)
    low = (rest - mid.astype(F32)).astype(BF16)
    return high, mid, low


def mm3(left, right, dims=NN):
    (lh, ll), (rh, rl) = left, right
    return mm(lh, rh, dims) + (mm(lh, rl, dims) + mm(ll, rh, dims))


def kernel(
    chips,
    ranks,
    width,
    x_hbm,
    target_hbm,
    b_hbm,
    c_hbm,
    step_hbm,
    forget_hbm,
    rate_hbm,
    skip_hbm,
    gain_hbm,
    gx_ref,
    gb_ref,
    gc_ref,
    rows_ref,
    rq_ref,
    ext_ref,
    x_ref,
    target_ref,
    b_ref,
    c_ref,
    step_ref,
    forget_ref,
    rate_ref,
    skip_ref,
    gain_ref,
    cols_ref,
    ends_ref,
    skips_ref,
    scores_ref,
    mixed_ref,
    gm_ref,
    u_ref,
    expb_ref,
    endwb_ref,
    cc_ref,
    bb_ref,
    scale_ref,
    sin_ref,
    gout_ref,
    btr_ref,
    ctr_ref,
    dst_ref,
    sum_ref,
    fl_own,
    fl_got,
    fm_out,
    fm_in,
    fp_out,
    fp_in,
    fs_out,
    bl_own,
    bl_got,
    bm_out,
    bm_in,
    bp_out,
    bp_in,
    bs_out,
    z_out,
    z_in,
    load_sem,
    pair_send,
    pair_recv,
    ring_send,
    ring_recv,
    z_send,
    z_recv,
):
    tokens = x_ref.shape[0]
    heads = step_ref.shape[0]
    half = heads // 2
    chan = x_ref.shape[1] // heads
    parts, pair = 2, half // 2
    piece = pair * 128 // chips
    per_head = chips // pair
    ctx = lax.axis_index("ctx")
    rank = lax.axis_index("head")
    chip, core = lax.div(ctx, 2), lax.rem(ctx, 2)
    sibling = (chip * 2 + 1 - core, rank)
    lines = chips // 4
    line, place = lax.div(chip, 4), lax.rem(chip, 4)

    def loop(low, high, step):
        def turn(i, carry):
            step(i)
            return carry

        lax.fori_loop(low, high, turn, 0)

    lines_from = [lax.rem(line + down, lines) * 4 for down in range(lines)]
    columns_from = [lax.rem(place + along, 4) for along in range(4)]
    offsets = [(down, along) for down in range(lines) for along in range(4)][1:]
    offsets.sort(key=lambda o: -(min(o[0], lines - o[0]) + min(o[1], 4 - o[1])))

    def unrolled(count, act):
        for i in range(count):
            act(i)

    def other_chips(act):
        for down, along in offsets:
            act(lines_from[down] + columns_from[along])

    def other_ranks(act):
        for away in sorted(range(1, ranks), key=lambda k: -min(k, ranks - k)):
            act(lax.rem(rank + away, ranks))

    barrier = pltpu.get_barrier_semaphore()

    def greet(device):
        pl.semaphore_signal(barrier, inc=1, device_id=device, device_id_type=MESH)

    other_chips(lambda other: greet((other * 2 + core, rank)))
    other_ranks(lambda other: greet((ctx, other)))
    greet(sibling)

    loads = [
        pltpu.make_async_copy(source, target, load_sem.at[i])
        for i, (source, target) in enumerate(
            (
                (step_hbm, step_ref),
                (forget_hbm, forget_ref),
                (rate_hbm, rate_ref),
                (b_hbm, b_ref),
                (x_hbm, x_ref),
                (c_hbm, c_ref),
                (skip_hbm, skip_ref),
                (gain_hbm, gain_ref),
                (target_hbm, target_ref),
            )
        )
    ]
    for load in loads:
        load.start()

    down_iota = lax.broadcasted_iota(jnp.int32, (tokens, tokens), 0)
    along_iota = lax.broadcasted_iota(jnp.int32, (tokens, tokens), 1)
    diagonal = down_iota[0:heads, 0:heads] == along_iota[0:heads, 0:heads]

    def as_column(row):
        return jnp.sum(jnp.where(diagonal, row, 0.0), axis=1, keepdims=True)

    for load in loads[0:3]:
        load.wait()
    rate = jnp.exp(as_column(rate_ref[...]))
    step = step_ref[...]
    logdec = -step * rate - forget_ref[...]
    upper = (down_iota <= along_iota).astype(F32).astype(BF16)
    high, mid, low = split3(logdec)
    cum = mm(high, upper) + (mm(mid, upper) + mm(low, upper))
    last = cum[:, tokens - 1 : tokens]
    expcum = jnp.exp(cum)
    enddec = jnp.exp(last - cum)
    table = [cum, expcum, enddec * step, enddec, step]
    rows_ref[0] = cum
    rows_ref[1] = step
    rows_ref[2] = enddec
    rows_ref[3] = jnp.broadcast_to(rate, (heads, tokens))
    ends_ref[...] = jnp.broadcast_to(jnp.exp(last), (heads, 128))
    table = jnp.concatenate(table + [jnp.zeros((128 - heads * len(table), tokens), F32)], axis=0)
    cols_ref[...] = table.T
    loads[3].wait()
    btr_ref[...] = b_ref[...].astype(F32).T.astype(BF16)
    loads[4].wait()

    def columns_of(h, count=1):
        rolled = pltpu.roll(cols_ref[...], lax.rem(128 - h, 128), 1)
        each = [[rolled[:, 8 * q + k : 8 * q + k + 1] for q in range(5)] for k in range(count)]
        return each if count > 1 else each[0]

    def channels(h):
        return pl.ds(pl.multiple_of(h * chan, chan), chan)

    def cum_row(h):
        return rows_ref[0, pl.ds(h, 1), :]

    def step_row(h):
        return rows_ref[1, pl.ds(h, 1), :]

    def decay_of(h):
        return ends_ref[pl.ds(h, 1), :]

    def skip_of(h):
        return skips_ref[pl.ds(h, 1), :]

    def two(make):
        return jnp.concatenate([make(0), make(1)], axis=1)

    def local_state(h):
        columns = columns_of(h, 2)
        weighted = two(lambda k: x_ref[:, channels(h + k)].astype(F32) * columns[k][ENDW])
        high, low = split2(weighted)
        state = mm(btr_ref[...], high) + mm(btr_ref[...], low)
        for k in range(2):
            fl_own[h + k, 0:128, :] = state[:, k * 128 : k * 128 + 128]
            fl_own[h + k, 128:136, :] = jnp.broadcast_to(decay_of(h + k), (8, 128))

    def to_sibling(source, target, sem):
        return pltpu.make_async_remote_copy(
            src_ref=source,
            dst_ref=target,
            send_sem=pair_send.at[sem],
            recv_sem=pair_recv.at[sem],
            device_id=sibling,
            device_id_type=MESH,
        )

    mine, theirs = core * half, (1 - core) * half

    def swap_of(own, got, part, sem):
        return to_sibling(own.at[pl.ds(theirs + part * pair, pair)], got.at[pl.ds(part * pair, pair)], sem)

    def heads_of(base, part, act):
        act(base + part * pair)

    def ring_start(source, target, part, rows_sent, sem):
        def start(other):
            pltpu.make_async_remote_copy(
                src_ref=source.at[part, other, 0:rows_sent],
                dst_ref=target.at[part, chip, 0:rows_sent],
                send_sem=ring_send.at[sem],
                recv_sem=ring_recv.at[sem],
                device_id=(other * 2 + core, rank),
                device_id_type=MESH,
            ).start()

        other_chips(start)
        target[part, chip, 0:rows_sent, :] = source[part, chip, 0:rows_sent, :]

    def ring_all(source, target, part, rows_sent, sem):
        return pltpu.make_async_remote_copy(
            src_ref=source.at[part, 0 : chips - 1, 0:rows_sent],
            dst_ref=target.at[part, 0 : chips - 1, 0:rows_sent],
            send_sem=ring_send.at[sem],
            recv_sem=ring_recv.at[sem],
            device_id=sibling,
            device_id_type=MESH,
        )

    def pair_of(own, got, i):
        own_rows, got_rows = own[mine + i, 0:128, :], got[i, 0:128, :]
        first = jnp.where(core == 0, own_rows, got_rows)
        second = jnp.where(core == 0, got_rows, own_rows)
        return first, second

    def decay_pair(i):
        own_decay, got_decay = fl_own[mine + i, 128:129, :], fl_got[i, 128:129, :]
        first = jnp.where(core == 0, own_decay, got_decay)
        second = jnp.where(core == 0, got_decay, own_decay)
        return first, second

    def owners_of(part, i):
        return part, pl.ds(i * per_head, per_head), pl.ds(0, piece)

    def join_forward(part):
        for i in range(pair):
            first, second = pair_of(fl_own, fl_got, part * pair + i)
            decay0, decay1 = decay_pair(part * pair + i)
            joined = decay1 * first + second
            fm_out[owners_of(part, i)] = joined.reshape(per_head, piece, 128)
            fm_out[part, pl.ds(i * per_head, per_head), pl.ds(piece, 8)] = jnp.broadcast_to(
                (decay0 * decay1)[None], (per_head, 8, 128)
            )

    loop(0, half, lambda i: local_state(2 * i))
    pl.semaphore_wait(barrier, (chips - 1) + (ranks - 1) + 1)
    for part in range(parts):
        swap_of(fl_own, fl_got, part, part).start()

    def first_round(part):
        swap_of(fl_own, fl_got, part, part).wait_recv()
        join_forward(part)
        ring_start(fm_out, fm_in, part, piece + 1, part)

    unrolled(parts, first_round)

    for load in loads[5:]:
        load.wait()
    skips_ref[...] = jnp.broadcast_to(as_column(skip_ref[...]), (heads, 128))
    ctr_ref[...] = c_ref[...].astype(F32).T.astype(BF16)
    scores_ref[...] = mm(c_ref[...], b_ref[...], NT)
    cc_ref[...] = jnp.concatenate([c_ref[...], c_ref[...]], axis=1)
    bb_ref[...] = jnp.concatenate([b_ref[...], b_ref[...]], axis=1)

    def near(h):
        cols = columns_of(h)
        gap = jnp.where(down_iota >= along_iota, cols[CUM] - cum_row(h), -1e30)
        weights = scores_ref[...] * jnp.exp(gap) * step_row(h)
        high, low = split2(weights)
        x_h = x_ref[:, channels(h)]
        wide_x = x_h.astype(F32)
        mixed_ref[:, channels(h)] = mm(high, x_h) + mm(low, x_h) + skip_of(h) * wide_x
        u_ref[:, channels(h)] = gain_ref[:, channels(h)] * (wide_x - target_ref[:, channels(h)].astype(F32))
        expb_ref[:, channels(h)] = jnp.broadcast_to(cols[EXPCUM], (tokens, 128))
        endwb_ref[:, channels(h)] = jnp.broadcast_to(cols[ENDW], (tokens, 128))

    loop(0, heads, near)
    sum_ref[...] = jnp.zeros_like(sum_ref)

    def scan_forward(part):
        ring_all(fm_out, fm_in, part, piece + 1, part).wait_recv()
        state = jnp.zeros((piece, 128), F32)
        for t in range(chips):
            fp_out[part, t] = state
            state = fm_in[part, t, piece : piece + 1, :] * state + fm_in[part, t, 0:piece, :]
        ring_start(fp_out, fp_in, part, piece, 2 + part)

    unrolled(parts, scan_forward)

    def enter(part):
        for i in range(pair):
            at = part * pair + i
            first, _ = pair_of(fl_own, fl_got, at)
            decay0, _ = decay_pair(at)
            for_first = fp_in[owners_of(part, i)].reshape(128, 128)
            for_second = decay0 * for_first + first
            sin_ref[mine + at] = jnp.where(core == 0, for_first, for_second)
            fs_out[at] = jnp.where(core == 0, for_second, for_first)

    def both(own, got, part, sem):
        return to_sibling(own.at[pl.ds(part * pair, pair)], got.at[pl.ds(mine + part * pair, pair)], sem)

    def stacked(ref, h):
        high, low = split2(two(lambda k: ref[h + k]))
        return jnp.concatenate([high, low], axis=0)

    def far(h):
        reached = mm(cc_ref[...], stacked(sin_ref, h))
        sums = [0.0, 0.0, 0.0]
        for k in range(2):
            here = channels(h + k)
            mixed = mixed_ref[:, here] + expb_ref[:, here] * reached[:, k * 128 : k * 128 + 128]
            mixed_ref[:, here] = mixed
            gained = gain_ref[:, here] * mixed
            sums = [sums[0] + mixed * mixed, sums[1] + u_ref[:, here] * mixed, sums[2] + gained * gained]
        for i in range(3):
            sum_ref[i] += sums[i]

    def far_mine(part):
        ring_all(fp_out, fp_in, part, piece, 2 + part).wait_recv()
        enter(part)
        both(fs_out, sin_ref, part, 2 + part).start()
        heads_of(mine, part, far)

    def far_theirs(part):
        both(fs_out, sin_ref, part, 2 + part).wait_recv()
        heads_of(theirs, part, far)

    unrolled(parts, far_mine)
    unrolled(parts, far_theirs)

    lane = lax.broadcasted_iota(jnp.int32, (tokens, 128), 1)
    row_iota = lax.broadcasted_iota(jnp.int32, (8, 256), 0)
    sums = jnp.zeros((8, tokens), F32)
    for i in range(3):
        ones = (row_iota == i).astype(F32).astype(BF16)
        sums = sums + mm(ones, jnp.concatenate(split2(sum_ref[i]), axis=1), NT)
    z_out[...] = sums

    def z_copy(to, slot):
        return pltpu.make_async_remote_copy(
            src_ref=z_out,
            dst_ref=z_in.at[slot],
            send_sem=z_send.at[to],
            recv_sem=z_recv.at[slot],
            device_id=(ctx, to),
            device_id_type=MESH,
        )

    other_ranks(lambda other: z_copy(other, rank).start())
    z_in[rank] = z_out[...]
    other_ranks(lambda other: z_copy(other, other).wait_recv())
    total = z_in[0]
    for i in range(1, ranks):
        total = total + z_in[i]
    inv_scale = lax.rsqrt(total[0:1, :] / width + EPSILON)
    inner = total[1:2, :] + inv_scale * total[2:3, :]
    coef = inner * inv_scale * inv_scale * inv_scale / width
    back = jnp.concatenate([inv_scale, coef, jnp.zeros((126, tokens), F32)], axis=0).T
    inv_col = jnp.broadcast_to(back[:, 0:1], (tokens, 128))
    scale_ref[0] = inv_col
    scale_ref[1] = inv_col * inv_col
    scale_ref[2] = jnp.broadcast_to(back[:, 1:2], (tokens, 128))

    def norm_back(h):
        def weighted(k):
            here = channels(h + k)
            gain = gain_ref[:, here]
            factor = (gain * gain) * scale_ref[1] - scale_ref[2]
            grad_mixed = u_ref[:, here] * scale_ref[0] + mixed_ref[:, here] * factor
            gm_ref[:, here] = grad_mixed
            return grad_mixed * expb_ref[:, here]

        high, low = split2(two(weighted))
        state = mm(ctr_ref[...], high) + mm(ctr_ref[...], low)
        for k in range(2):
            bl_own[h + k] = state[:, k * 128 : k * 128 + 128]

    def join_back(part):
        for i in range(pair):
            first, second = pair_of(bl_own, bl_got, part * pair + i)
            decay0, _ = decay_pair(part * pair + i)
            bm_out[owners_of(part, i)] = (decay0 * second + first).reshape(per_head, piece, 128)

    def back_theirs(part):
        heads_of(theirs, part, norm_back)
        swap_of(bl_own, bl_got, part, 4 + part).start()

    def back_mine(part):
        heads_of(mine, part, norm_back)
        swap_of(bl_own, bl_got, part, 4 + part).wait_recv()
        join_back(part)
        ring_start(bm_out, bm_in, part, piece, 4 + part)

    unrolled(parts, back_theirs)
    unrolled(parts, back_mine)

    rq_ref[...] = jnp.zeros_like(rq_ref)
    gc_ref[...] = jnp.zeros_like(gc_ref)
    gb_ref[...] = jnp.zeros_like(gb_ref)
    dst_ref[...] = jnp.zeros_like(dst_ref)
    scores_ref[...] = mm(b_ref[...], c_ref[...], NT)

    def near_back(h):
        cols = columns_of(h)
        here = channels(h)
        gap = jnp.where(along_iota >= down_iota, cum_row(h) - cols[CUM], -1e30)
        decay = jnp.exp(gap)
        grad_mixed = gm_ref[:, here]
        gm_parts = split2(grad_mixed)
        x_h = x_ref[:, here]
        wide_x = x_h.astype(F32)
        mixed = mixed_ref[:, here]
        value = mm3(split2(scores_ref[...] * decay), gm_parts)
        grad_out = wide_x + gain_ref[:, here] * mixed * scale_ref[0] - target_ref[:, here].astype(F32)
        gx_ref[:, here] = grad_out + skip_of(h) * grad_mixed + cols[STEP] * value
        grad_weights = mm(x_h, gm_parts[0], NT) + mm(x_h, gm_parts[1], NT)
        dst_ref[...] += grad_weights * decay * cols[STEP]
        row_sum = jnp.sum(grad_mixed * (mixed - skip_of(h) * wide_x), axis=1, keepdims=True)
        column_sum = jnp.sum(wide_x * value, axis=1, keepdims=True)
        rq_ref[...] = jnp.where(lane == h, row_sum, jnp.where(lane == h + 8, column_sum, rq_ref[...]))
        gc_ref[...] += mm3(split2(grad_mixed * expb_ref[:, here]), split2(sin_ref[h]), NT)

    loop(0, heads, near_back)
    grad_scores = dst_ref[...]
    high, low = split2(grad_scores)
    gb_ref[...] += mm(high, c_ref[...]) + mm(low, c_ref[...])
    high, low = split2(grad_scores.T)
    gc_ref[...] += mm(high, b_ref[...]) + mm(low, b_ref[...])

    def scan_back(part):
        ring_all(bm_out, bm_in, part, piece, 4 + part).wait_recv()
        grad = jnp.zeros((piece, 128), F32)
        for t in reversed(range(chips)):
            bp_out[part, t] = grad
            grad = fm_in[part, t, piece : piece + 1, :] * grad + bm_in[part, t]
        ring_start(bp_out, bp_in, part, piece, 6 + part)

    unrolled(parts, scan_back)

    def leave(part):
        for i in range(pair):
            at = part * pair + i
            _, second = pair_of(bl_own, bl_got, at)
            _, decay1 = decay_pair(at)
            for_second = bp_in[owners_of(part, i)].reshape(128, 128)
            for_first = decay1 * for_second + second
            gout_ref[mine + at] = jnp.where(core == 0, for_first, for_second)
            bs_out[at] = jnp.where(core == 0, for_second, for_first)

    def far_back(h):
        both_parts = stacked(gout_ref, h)
        reached = mm(bb_ref[...], both_parts)
        table = rq_ref[...]
        grad_b = gb_ref[...]
        for k in range(2):
            here = channels(h + k)
            at = slice(k * 128, k * 128 + 128)
            x_h = x_ref[:, here]
            weight = endwb_ref[:, here]
            gx_ref[:, here] += weight * reached[:, at]
            row_sum = jnp.sum(x_h.astype(F32) * reached[:, at], axis=1, keepdims=True)
            table = jnp.where(lane == h + k + 16, row_sum, table)
            parts_along = jnp.concatenate([both_parts[0:128, at], both_parts[128:256, at]], axis=1)
            grad_b = grad_b + weight * mm(jnp.concatenate([x_h, x_h], axis=1), parts_along, NT)
            leaving = decay_of(h + k) * sin_ref[h + k] + fl_own[h + k, 0:128, :]
            ext_ref[pl.ds(h + k, 1), :] = jnp.sum(gout_ref[h + k] * leaving, axis=0, keepdims=True)
        rq_ref[...] = table
        gb_ref[...] = grad_b

    def last_mine(part):
        ring_all(bp_out, bp_in, part, piece, 6 + part).wait_recv()
        leave(part)
        both(bs_out, gout_ref, part, 6 + part).start()
        heads_of(mine, part, far_back)

    def last_theirs(part):
        both(bs_out, gout_ref, part, 6 + part).wait_recv()
        heads_of(theirs, part, far_back)

    unrolled(parts, last_mine)
    unrolled(parts, last_theirs)

    for part in range(parts):
        swap_of(fl_own, fl_got, part, part).wait_send()
        both(fs_out, sin_ref, part, 2 + part).wait_send()
        swap_of(bl_own, bl_got, part, 4 + part).wait_send()
        both(bs_out, gout_ref, part, 6 + part).wait_send()
        ring_all(fm_out, fm_in, part, piece + 1, part).wait_send()
        ring_all(fp_out, fp_in, part, piece, 2 + part).wait_send()
        ring_all(bm_out, bm_in, part, piece, 4 + part).wait_send()
        ring_all(bp_out, bp_in, part, piece, 6 + part).wait_send()
    other_ranks(lambda other: z_copy(other, other).wait_send())


def finish(gx_in, gb_in, gc_in, rows_ref, rq_ref, ext_ref, gx_ref, gb_ref, gc_ref, gs_ref, sums_ref, sems):
    rows = gx_in.shape[0] // 8
    blocks = [pl.ds(i * rows, rows) for i in range(8)]
    pairs = [(gx_in.at[block], gx_ref.at[block]) for block in blocks] + [(gb_in, gb_ref), (gc_in, gc_ref)]
    copies = [pltpu.make_async_copy(source, target, sems.at[i]) for i, (source, target) in enumerate(pairs)]
    for copy in copies:
        copy.start()
    heads, tokens = sums_ref.shape
    step, enddec, rate = rows_ref[1], rows_ref[2], rows_ref[3]
    ends = rq_ref[...].T
    inner_x = ends[8 : 8 + heads, :] + enddec * ends[16 : 16 + heads, :]
    extra = jnp.sum(ext_ref[...], axis=1, keepdims=True)
    down_iota = lax.broadcasted_iota(jnp.int32, (tokens, tokens), 0)
    along_iota = lax.broadcasted_iota(jnp.int32, (tokens, tokens), 1)
    lower = (down_iota >= along_iota).astype(F32).astype(BF16)
    high, mid, low = split3(ends[0:heads, :] - step * inner_x)
    grad_dec = mm(high, lower) + (mm(mid, lower) + mm(low, lower)) + extra
    sums_ref[...] = inner_x - rate * grad_dec
    last = pltpu.make_async_copy(sums_ref, gs_ref, sems.at[10])
    last.start()
    for copy in copies:
        copy.wait()
    last.wait()


def body(chips, ranks, inputs, b_proj, c_proj, step_sizes, log_rate, forget, skip_gain, norm_gain, target):
    tokens, wide = inputs.shape
    heads = step_sizes.shape[1]
    half = heads // 2
    piece = half * 64 // chips
    vmem = pl.BlockSpec(memory_space=pltpu.VMEM)
    hbm = pl.BlockSpec(memory_space=pltpu.HBM)

    def buffer(*shape, dtype=F32):
        return pltpu.VMEM(shape, dtype)

    state = (heads, 128, 128)
    half_state = (half, 128, 128)
    operands = (
        inputs,
        target,
        b_proj.reshape(tokens, 128),
        c_proj.reshape(tokens, 128),
        step_sizes[0],
        forget[0],
        log_rate,
        skip_gain,
        norm_gain,
    )
    operands = tuple(pltpu.with_memory_space_constraint(operand, pltpu.HBM) for operand in operands)
    out_shape = (
        jax.ShapeDtypeStruct((tokens, wide), F32),
        jax.ShapeDtypeStruct((tokens, 128), F32),
        jax.ShapeDtypeStruct((tokens, 128), F32),
        jax.ShapeDtypeStruct((heads, tokens), F32),
    )
    results = pl.pallas_call(
        functools.partial(kernel, chips, ranks, float(wide * ranks)),
        out_shape=out_shape[0:3]
        + (
            jax.ShapeDtypeStruct((4, heads, tokens), F32),
            jax.ShapeDtypeStruct((tokens, 128), F32),
            jax.ShapeDtypeStruct((heads, 128), F32),
        ),
        in_specs=[hbm] * len(operands),
        out_specs=[vmem] * 6,
        scratch_shapes=[buffer(*operand.shape, dtype=operand.dtype) for operand in operands]
        + [
            buffer(tokens, 128),
            buffer(heads, 128),
            buffer(heads, 128),
            buffer(tokens, tokens),
            buffer(tokens, wide),
            buffer(tokens, wide),
            buffer(tokens, wide),
            buffer(tokens, wide),
            buffer(tokens, wide),
            buffer(tokens, 256, dtype=BF16),
            buffer(tokens, 256, dtype=BF16),
            buffer(3, tokens, 128),
            buffer(*state),
            buffer(*state),
            buffer(128, tokens, dtype=BF16),
            buffer(128, tokens, dtype=BF16),
            buffer(tokens, tokens),
            buffer(3, tokens, 128),
            buffer(heads, 136, 128),
            buffer(half, 136, 128),
            buffer(2, chips, piece + 8, 128),
            buffer(2, chips, piece + 8, 128),
            buffer(2, chips, piece, 128),
            buffer(2, chips, piece, 128),
            buffer(*half_state),
            buffer(*state),
            buffer(*half_state),
            buffer(2, chips, piece, 128),
            buffer(2, chips, piece, 128),
            buffer(2, chips, piece, 128),
            buffer(2, chips, piece, 128),
            buffer(*half_state),
            buffer(8, tokens),
            buffer(ranks, 8, tokens),
            pltpu.SemaphoreType.DMA((9,)),
            pltpu.SemaphoreType.DMA((8,)),
            pltpu.SemaphoreType.DMA((8,)),
            pltpu.SemaphoreType.DMA((8,)),
            pltpu.SemaphoreType.DMA((8,)),
            pltpu.SemaphoreType.DMA((ranks,)),
            pltpu.SemaphoreType.DMA((ranks,)),
        ],
        compiler_params=pltpu.CompilerParams(
            collective_id=0, has_side_effects=True, vmem_limit_bytes=24 * 1024 * 1024
        ),
        name="layer",
    )(*operands)
    grad_x, grad_b, grad_c, grad_steps = pl.pallas_call(
        finish,
        out_shape=out_shape,
        in_specs=[pl.BlockSpec(memory_space=pl.ANY)] * 3 + [vmem] * 3,
        out_specs=[hbm] * 4,
        scratch_shapes=[buffer(heads, tokens), pltpu.SemaphoreType.DMA((11,))],
        compiler_params=pltpu.CompilerParams(vmem_limit_bytes=4 * 1024 * 1024),
        name="finish",
    )(*results)
    return (
        grad_x,
        grad_b.reshape(1, tokens, 1, 128),
        grad_c.reshape(1, tokens, 1, 128),
        grad_steps[None],
    )


def solution(mesh):
    chips, ranks = mesh.shape["ctx"] // 2, mesh.shape["head"]
    in_specs = (
        P("ctx", "head"),
        P(None, "ctx", "head", None),
        P(None, "ctx", "head", None),
        P(None, "head", "ctx"),
        P(None, "head"),
        P(None, "head", "ctx"),
        P(None, "head"),
        P(None, "head"),
        P("ctx", "head"),
    )
    out_specs = (
        P("ctx", "head"),
        P(None, "ctx", "head", None),
        P(None, "ctx", "head", None),
        P(None, "head", "ctx"),
    )
    return jax.shard_map(
        functools.partial(body, chips, ranks),
        mesh=mesh,
        in_specs=in_specs,
        out_specs=out_specs,
        check_vma=False,
    )
```
